512 devices in a mesh: row: 8 (over x, core), col: 64 (over y, z).
Axes of the slice: x: 4, y: 4, z: 16, core: 2. Of those that a mesh axis runs over, the one named last changes fastest.
Arguments:
- blocks: bfloat16 [8, 64, 8, 512, 512], P('row', 'col'), may hold values from -0.0234375 to 0.0234375
- block_rows: int32 [8, 64, 8], P('row', 'col'), may hold values from 0 to 3, as said below
- block_cols: int32 [8, 64, 8], P('row', 'col'), may hold values from 0 to 3
- sketch: bfloat16 [16384, 32], P('row'), may hold values from -6 to 6
- theta: float32 [131072], P('col'), may hold values from 0.1 to 10
- rhs: float32 [16384], P('row'), may hold values from -6 to 6
Outputs:
- solution: float32 [16384], P(('row', 'col'))
- residual: float32 [16384], P(('row', 'col'))
- precond_residual: float32 [16384], P(('row', 'col'))
The draws below stay inside these ranges and needn't reach their ends.
Inputs may be any that keep to these rules, and one draw needn't show every extreme that they name: Within one tile the pairs (block_rows, block_cols) are all different.
All inputs are finite; a program needn't handle non-finite values.
Results may differ from the reference program's by a relative error of at most 0.005.
Values may be sent and summed in bfloat16 or wider, within the bound.
No kernel may reach another device: no remote copies, remote signals or barrier semaphores. Data moves between devices by JAX's collectives and lax.ppermute only.
A program may use at most 64 MiB of HBM per device.

```python
import math
import jax
import jax.numpy as jnp
from jax import lax

BLOCK = 512
SKETCH = 32
ROW_BLOCKS = 4
COL_BLOCKS = 4
TILE_BLOCKS = 8
GRID_ROWS = 8
GRID_COLS = 64
ROWS = 16384
COLUMNS = 131072


def tile_positions(key):
    keys = jax.random.split(key, GRID_ROWS * GRID_COLS)
    chosen = jax.vmap(lambda k: jax.random.permutation(k, ROW_BLOCKS * COL_BLOCKS)[:TILE_BLOCKS])(keys)
    return chosen.reshape(GRID_ROWS, GRID_COLS, TILE_BLOCKS).astype(jnp.int32)


def shared_factors(key):
    pattern_key = jax.random.fold_in(key, 101)
    strength_key = jax.random.fold_in(key, 103)
    alignment_key = jax.random.fold_in(key, 107)
    pattern = jnp.clip(jax.random.normal(pattern_key, (GRID_ROWS, BLOCK), jnp.float32), -2.5, 2.5)
    highest = min(16.0, 0.7 * math.sqrt(BLOCK))
    strength = jnp.exp(jax.random.uniform(strength_key, (GRID_ROWS,), jnp.float32, math.log(highest / 8.0), math.log(highest)))
    alignment = jax.random.uniform(alignment_key, (GRID_ROWS, ROW_BLOCKS), jnp.float32, -1.0, 1.0)
    return (pattern, strength, alignment)


def draw_block_rows(key, part):
    places = tile_positions(key)
    return (places // COL_BLOCKS).astype(jnp.int32)


def draw_block_cols(key, part):
    places = tile_positions(key)
    return (places % COL_BLOCKS).astype(jnp.int32)


def draw_blocks(key, part):
    pattern, strength, alignment = shared_factors(key)
    key = jax.random.fold_in(key, 7)
    noise_key = jax.random.fold_in(key, 1)
    factor_key = jax.random.fold_in(key, 2)
    fan_in = BLOCK * TILE_BLOCKS * GRID_COLS / ROW_BLOCKS
    sigma = 1.0 / math.sqrt(fan_in)
    full_shape = (GRID_ROWS, GRID_COLS, TILE_BLOCKS, BLOCK, BLOCK)
    noise_part = jnp.clip(jax.random.normal(noise_key, full_shape, jnp.float32), -4.0, 4.0)
    factor = jnp.clip(jax.random.normal(factor_key, (GRID_ROWS, GRID_COLS, TILE_BLOCKS, BLOCK), jnp.float32), -2.5, 2.5)
    weight_row = strength / math.sqrt(fan_in * BLOCK)
    coupling = weight_row[:, None, None, None, None] * pattern[:, None, None, :, None] * factor[:, :, :, None, :]
    limit = 5.95 * sigma
    return jnp.clip(sigma * noise_part + coupling, -limit, limit).astype(jnp.bfloat16)


def draw_rhs(key, part):
    pattern, strength, alignment = shared_factors(key)
    key = jax.random.fold_in(key, 9)
    noise_part = jnp.clip(jax.random.normal(key, (GRID_ROWS, ROW_BLOCKS, BLOCK), jnp.float32), -3.4, 3.4)
    aligned = alignment[:, :, None] * pattern[:, None, :]
    return (noise_part + aligned).reshape(ROWS).astype(jnp.float32)


def levels(stream_key, shape, cuts, least, high):
    loudness, own = 1.0, jax.random.fold_in(stream_key, 6)
    for axis_at, parts in cuts:
        heights = jnp.exp(jax.random.uniform(jax.random.fold_in(own, axis_at), (parts,), jnp.float32, least / len(cuts), high / len(cuts)))
        loudness = loudness * jnp.repeat(heights, shape[axis_at] // parts).reshape([-1 if axis == axis_at else 1 for axis in range(len(shape))])
    return loudness


def bell_draw(own_key, shape, scale, bound, shards=(), kind=jnp.bfloat16):
    values = scale * jax.random.normal(own_key, shape, jnp.float32)
    if shards:
        values = values * levels(own_key, shape, shards, -0.22, 0.18)
    return jnp.clip(values, -bound, bound).astype(kind)


def setup_inputs(seed: int = 0) -> dict:
    splits = jax.random.split(jax.random.key(seed), 7)
    return {
        "blocks": draw_blocks(jax.random.fold_in(splits[6], 71), 0),
        "block_rows": draw_block_rows(jax.random.fold_in(splits[6], 71), 0),
        "block_cols": draw_block_cols(jax.random.fold_in(splits[6], 71), 0),
        "sketch": bell_draw(splits[3], (ROWS, SKETCH), 1.0, 6.0, ((0, 8),)),
        "theta": jnp.clip(jnp.exp(math.log(10.0) - 4.6051702 * jax.random.uniform(splits[4], (COLUMNS,), jnp.float32) ** levels(splits[4], (COLUMNS,), ((0, 64),), -0.2, 0.2)), 0.1, 10.0),
        "rhs": draw_rhs(jax.random.fold_in(splits[6], 71), 0),
    }


precond_shift = 1.0
regularize = 0.5

def tile_transpose(values, rows_idx, cols_idx, inputs):
    stacked = inputs.reshape(ROW_BLOCKS, BLOCK, -1)
    picked = stacked[rows_idx]
    product = jnp.einsum('cnab,cnak->cnbk', values.astype(jnp.float32), picked, precision=lax.Precision.HIGHEST)
    onehot = (cols_idx[..., None] == jnp.arange(COL_BLOCKS, dtype=jnp.int32)).astype(jnp.float32)
    return jnp.einsum('cnj,cnbk->cjbk', onehot, product, precision=lax.Precision.HIGHEST).reshape(COLUMNS, -1)

def apply_transpose(blocks, block_rows, block_cols, inputs):
    width = inputs.shape[1]
    split_rows = inputs.reshape(GRID_ROWS, ROW_BLOCKS * BLOCK, width)

    def step(total, items):
        values, rows_idx, cols_idx, part_in = items
        return (total + tile_transpose(values, rows_idx, cols_idx, part_in), None)
    total, unused = lax.scan(step, jnp.zeros((COLUMNS, width), jnp.float32), (blocks, block_rows, block_cols, split_rows))
    return total

def apply_forward(blocks, block_rows, block_cols, inputs):
    width = inputs.shape[1]
    split_cols = inputs.reshape(GRID_COLS, COL_BLOCKS, BLOCK, width)

    def one(items):
        values, rows_idx, cols_idx = items
        picked = jax.vmap(lambda whole, index: whole[index])(split_cols, cols_idx)
        product = jnp.einsum('cnab,cnbk->cnak', values.astype(jnp.float32), picked, precision=lax.Precision.HIGHEST)
        onehot = (rows_idx[..., None] == jnp.arange(ROW_BLOCKS, dtype=jnp.int32)).astype(jnp.float32)
        return jnp.einsum('cni,cnak->iak', onehot, product, precision=lax.Precision.HIGHEST).reshape(ROW_BLOCKS * BLOCK, width)
    return lax.map(one, (blocks, block_rows, block_cols)).reshape(ROWS, width)

def solve_gram(factor, vector):
    middle = lax.linalg.triangular_solve(factor, vector[:, None], left_side=True, lower=True)
    result = lax.linalg.triangular_solve(factor, middle, left_side=True, lower=True, transpose_a=True)
    return result[:, 0]

def precondition(ysketch, factor, vector):
    coeffs = solve_gram(factor, jnp.dot(vector, ysketch, precision=lax.Precision.HIGHEST))
    return (vector - jnp.dot(ysketch, coeffs, precision=lax.Precision.HIGHEST)) / precond_shift

def reference(blocks, block_rows, block_cols, sketch, theta, rhs):
    sketch_f = sketch.astype(jnp.float32)
    sketch_cols = apply_transpose(blocks, block_rows, block_cols, sketch_f)
    scaled = (theta[:, None] * sketch_cols).astype(jnp.bfloat16)
    ysketch = apply_forward(blocks, block_rows, block_cols, scaled.astype(jnp.float32)) + regularize * sketch_f
    cross = jnp.dot(sketch_f.T, ysketch, precision=lax.Precision.HIGHEST)
    gram = precond_shift * 0.5 * (cross + cross.T) + jnp.dot(ysketch.T, ysketch, precision=lax.Precision.HIGHEST)
    factor = jnp.linalg.cholesky(gram)
    direction = precondition(ysketch, factor, rhs)
    dir_low = direction.astype(jnp.bfloat16)
    image_cols = apply_transpose(blocks, block_rows, block_cols, dir_low.astype(jnp.float32)[:, None])[:, 0]
    image_scaled = (theta * image_cols).astype(jnp.bfloat16)
    image = apply_forward(blocks, block_rows, block_cols, image_scaled.astype(jnp.float32)[:, None])[:, 0] + regularize * direction
    alpha = jnp.sum(rhs * direction) / jnp.sum(direction * image)
    solution = alpha * direction
    residual = rhs - alpha * image
    precond_residual = precondition(ysketch, factor, residual)
    return (solution, residual, precond_residual)
```

```python
import jax
import jax.numpy as jnp
from jax import lax
from jax.experimental import pallas as pl
from jax.experimental.pallas import tpu as pltpu
from jax.sharding import PartitionSpec as P

precond_shift = 1.0
regularize = 0.5

F32 = jnp.float32
BF16 = jnp.bfloat16
HIGHEST = lax.Precision.HIGHEST
LANES = 128
ROW_PARTS = 8
COL_PARTS = 64
BLOCKS = 8
ORDER = 512
LOCAL = 2048
WIDTH = 32
PIECE = LOCAL // ROW_PARTS
TILES = LOCAL // LANES
GROUPS = WIDTH // 8
VMEM_LIMIT = 24 * 1024 * 1024

NT = (((1,), (1,)), ((), ()))


def vmem():
    return pl.BlockSpec(memory_space=pltpu.VMEM)


def smem():
    return pl.BlockSpec(memory_space=pltpu.SMEM)


def iota(shape, axis):
    return lax.broadcasted_iota(jnp.int32, shape, axis)


def call(body, in_specs, out_shape, scratch=(), flops=0, name=None):
    out_specs = jax.tree.map(lambda _: vmem(), out_shape)
    return pl.pallas_call(
        body,
        in_specs=in_specs,
        out_specs=out_specs,
        out_shape=out_shape,
        scratch_shapes=list(scratch),
        compiler_params=pltpu.CompilerParams(vmem_limit_bytes=VMEM_LIMIT),
        cost_estimate=pl.CostEstimate(flops=flops, bytes_accessed=1 << 20, transcendentals=0),
        name=name,
    )


def sketch_body(rows_ref, cols_ref, omega_ref, blocks_ref, out_ref):
    out_ref[...] = jnp.zeros(out_ref.shape, F32)
    for n in range(BLOCKS):
        start = pl.multiple_of(rows_ref[n] * ORDER, ORDER)
        product = jnp.dot(
            omega_ref[:, pl.ds(start, ORDER)], blocks_ref[n], preferred_element_type=F32
        )
        place = cols_ref[n] * 2
        out_ref[place] += product[:, :PIECE]
        out_ref[place + 1] += product[:, PIECE:]


def scale_body(me_ref, parts_ref, theta_ref, out_ref):
    total = parts_ref[0]
    for i in range(1, ROW_PARTS):
        total += parts_ref[i]
    scaled = (theta_ref[pl.ds(me_ref[0], 1), :] * total).astype(BF16)
    for i in range(ROW_PARTS):
        out_ref[i] = scaled


def forward_body(rows_ref, cols_ref, scaled_ref, blocks_ref, out_ref):
    out_ref[...] = jnp.zeros(out_ref.shape, F32)
    for n in range(BLOCKS):
        place = cols_ref[n] * 2
        left = jnp.concatenate([scaled_ref[place], scaled_ref[place + 1]], axis=1)
        product = lax.dot_general(left, blocks_ref[n], NT, preferred_element_type=F32)
        first = rows_ref[n] * (ORDER // LANES)
        for g in range(GROUPS):
            for q in range(ORDER // LANES):
                out_ref[g * TILES + first + q] += product[
                    8 * g : 8 * g + 8, LANES * q : LANES * (q + 1)
                ]


def spread_body(parts_ref, out_ref):
    sums = [parts_ref[i] for i in range(8)]
    for i in range(8, COL_PARTS):
        sums[i % 8] += parts_ref[i]
    while len(sums) > 1:
        sums = [a + b for a, b in zip(sums[::2], sums[1::2])]
    for i in range(COL_PARTS):
        out_ref[i] = sums[0]


def gram_body(
    rows_ref, cols_ref, tiles_ref, omega_ref, rhs_ref, blocks_ref, y_ref, out_ref, all_ref, cut_ref, acc_ref
):
    for g in range(GROUPS):
        for t in range(TILES):
            y_ref[8 * g : 8 * g + 8, LANES * t : LANES * (t + 1)] = tiles_ref[g * TILES + t]
    omega = omega_ref[...].astype(F32)
    ysketch = y_ref[...] + regularize * omega
    y_ref[...] = ysketch
    top = ysketch.astype(BF16)
    rest = ysketch - top.astype(F32)
    middle = rest.astype(BF16)
    low = (rest - middle.astype(F32)).astype(BF16)
    cut_ref[0:WIDTH, :] = top
    cut_ref[WIDTH : 2 * WIDTH, :] = middle
    cut_ref[2 * WIDTH : 3 * WIDTH, :] = low
    rhs = rhs_ref[...]
    rhs_top = rhs.astype(BF16).astype(F32)
    rhs_rest = rhs - rhs_top
    rhs_middle = rhs_rest.astype(BF16).astype(F32)
    rhs_low = rhs_rest - rhs_middle
    spot = iota((16, LOCAL), 0)
    rhs_cut = jnp.where(
        spot == 0, rhs_top, jnp.where(spot == 1, rhs_middle, jnp.where(spot == 2, rhs_low, 0.0))
    )
    cut_ref[3 * WIDTH :, :] = rhs_cut.astype(BF16)
    all_ref[0:WIDTH, :] = ysketch
    all_ref[WIDTH : 2 * WIDTH, :] = omega
    all_ref[2 * WIDTH :, :] = jnp.where(iota((LANES - 2 * WIDTH, LOCAL), 0) == 0, rhs, 0.0)

    products = lax.dot_general(
        all_ref[0 : 2 * WIDTH + 8, :], all_ref[...], NT, precision=HIGHEST, preferred_element_type=F32
    )
    lane = iota((WIDTH, LANES), 1)
    upper = products[0:WIDTH]
    cross = 0.5 * (upper + pltpu.roll(products[WIDTH : 2 * WIDTH], WIDTH, 1))
    gram = jnp.where(lane < WIDTH, upper, jnp.where(lane < 2 * WIDTH, cross, 0.0))
    for i in range(ROW_PARTS):
        out_ref[i, 0:WIDTH, PIECE:] = gram
        out_ref[i, WIDTH:, PIECE:] = products[2 * WIDTH :]

    acc_ref[...] = jnp.zeros(acc_ref.shape, F32)
    for n in range(BLOCKS):
        start = pl.multiple_of(rows_ref[n] * ORDER, ORDER)
        acc_ref[cols_ref[n]] += jnp.dot(
            cut_ref[:, pl.ds(start, ORDER)], blocks_ref[n], preferred_element_type=F32
        )
    for j in range(LOCAL // ORDER):
        image = acc_ref[j, 0:WIDTH] + (acc_ref[j, WIDTH : 2 * WIDTH] + acc_ref[j, 2 * WIDTH : 3 * WIDTH])
        rhs_image = jnp.sum(acc_ref[j, 3 * WIDTH :], axis=0, keepdims=True)
        for h in range(2):
            out_ref[2 * j + h, 0:WIDTH, 0:PIECE] = image[:, PIECE * h : PIECE * (h + 1)]
            out_ref[2 * j + h, WIDTH:, 0:PIECE] = jnp.broadcast_to(
                rhs_image[:, PIECE * h : PIECE * (h + 1)], (8, PIECE)
            )


def to_column(row, shift):
    lane = iota((WIDTH, LANES), 1)
    return jnp.sum(
        jnp.where(lane == iota((WIDTH, LANES), 0) + shift, row, 0.0), axis=1, keepdims=True
    )


def to_row(column, shift):
    lane = iota((WIDTH, LANES), 1)
    return jnp.sum(
        jnp.where(lane == iota((WIDTH, LANES), 0) + shift, column, 0.0), axis=0, keepdims=True
    )


def solve_gram(inverse, diagonal, row):
    half = jnp.sum(inverse * pltpu.roll(row, WIDTH, 1), axis=1, keepdims=True) / diagonal
    return jnp.sum(inverse * half, axis=0, keepdims=True)


def factor_body(me_ref, parts_ref, theta_ref, out_ref, keep_ref):
    total = parts_ref[0]
    for i in range(1, ROW_PARTS):
        total += parts_ref[i]
    gram = total[0:WIDTH, PIECE:]
    lane = iota((WIDTH, LANES), 1)
    spot = iota((WIDTH, LANES), 0)
    work = jnp.where(
        lane < WIDTH,
        gram + pltpu.roll(gram, LANES - WIDTH, 1),
        jnp.where(lane == spot + WIDTH, 1.0, 0.0),
    )
    for k in range(WIDTH - 1):
        pivot = work[k : k + 1, :]
        factor = work[:, k : k + 1] / pivot[:, k : k + 1]
        work = work - jnp.where(spot > k, factor, 0.0) * pivot
    diagonal = jnp.sum(jnp.where(lane == spot, work, 0.0), axis=1, keepdims=True)
    inverse = jnp.where((lane >= WIDTH) & (lane < 2 * WIDTH), work, 0.0)

    tail = total[WIDTH:, PIECE:]
    sketched_rhs = jnp.where(iota((1, LANES), 1) < WIDTH, tail[0:1], 0.0)
    coeffs = solve_gram(inverse, diagonal, sketched_rhs)
    column = to_column(coeffs, WIDTH)
    crossed = jnp.sum(jnp.where((lane >= WIDTH) & (lane < 2 * WIDTH), gram * column, 0.0), axis=0, keepdims=True)

    image_sketch = total[0:WIDTH, 0:PIECE]
    image_cols = total[WIDTH : WIDTH + 1, 0:PIECE] - jnp.sum(image_sketch * column, axis=0, keepdims=True)
    scaled = (theta_ref[pl.ds(me_ref[0], 1), :] * image_cols).astype(BF16).astype(F32)
    sketched = to_row(jnp.sum(image_sketch * scaled, axis=1, keepdims=True), 0)
    curvature = jnp.sum(image_cols * scaled, axis=1, keepdims=True)
    sums = jnp.where(iota((1, LANES), 1) == WIDTH, curvature, sketched)
    where = iota((8, LANES), 0) % 4
    pack = jnp.where(
        where == 0,
        scaled[:, :LANES],
        jnp.where(where == 1, scaled[:, LANES:], jnp.where(where == 2, sums, 0.0)),
    )
    for i in range(ROW_PARTS // 2):
        out_ref[8 * i : 8 * i + 8, :] = pack
    keep_ref[0:WIDTH, :] = inverse
    keep_ref[WIDTH : 2 * WIDTH, :] = jnp.broadcast_to(diagonal, (WIDTH, LANES))
    keep_ref[2 * WIDTH : 2 * WIDTH + 8, :] = tail
    keep_ref[2 * WIDTH + 8 : 2 * WIDTH + 16, :] = jnp.broadcast_to(coeffs, (8, LANES))
    keep_ref[2 * WIDTH + 16 :, :] = jnp.broadcast_to(crossed, (8, LANES))


def image_body(rows_ref, cols_ref, parts_ref, blocks_ref, out_ref, scaled_ref, acc_ref):
    sums = parts_ref[2:3, :]
    for i in range(1, ROW_PARTS):
        sums += parts_ref[4 * i + 2 : 4 * i + 3, :]
    for j in range(LOCAL // ORDER):
        line = jnp.concatenate(
            [parts_ref[4 * (2 * j + h) + s : 4 * (2 * j + h) + s + 1, :] for h in range(2) for s in range(2)],
            axis=1,
        )
        scaled_ref[j] = jnp.broadcast_to(line, (16, ORDER)).astype(BF16)
    acc_ref[...] = jnp.zeros(acc_ref.shape, F32)
    for n in range(BLOCKS):
        product = lax.dot_general(
            scaled_ref[cols_ref[n]], blocks_ref[n], NT, preferred_element_type=F32
        )
        acc_ref[rows_ref[n]] += product[0:8]
    even = iota((8, LANES), 0) % 2 == 0
    for t in range(TILES):
        at = LANES * (t % 4)
        out_ref[8 * t : 8 * t + 8, :] = jnp.where(even, acc_ref[t // 4, :, at : at + LANES], sums)


def step_body(me_ref, parts_ref, keep_ref, y_ref, rhs_ref, out_ref):
    total = parts_ref[0:8, :]
    for i in range(1, COL_PARTS // 4):
        total += parts_ref[8 * i : 8 * i + 8, :]
    even = iota((8, LANES), 0) % 2 == 0
    image_rows = jnp.sum(jnp.where(even, total, 0.0), axis=0, keepdims=True)
    sums = jnp.sum(jnp.where(even, 0.0, total), axis=0, keepdims=True)

    lane = iota((1, LANES), 1)
    first = lane < WIDTH
    inverse = keep_ref[0:WIDTH, :]
    diagonal = keep_ref[WIDTH : 2 * WIDTH, 0:1]
    tail = keep_ref[2 * WIDTH : 2 * WIDTH + 1, :]
    coeffs = keep_ref[2 * WIDTH + 8 : 2 * WIDTH + 9, :]
    crossed = keep_ref[2 * WIDTH + 16 : 2 * WIDTH + 17, :]
    sketched_rhs = jnp.where(first, tail, 0.0)
    square = jnp.sum(jnp.where(lane == 2 * WIDTH, tail, 0.0), axis=1, keepdims=True)
    along = square - jnp.sum(pltpu.roll(sketched_rhs, WIDTH, 1) * coeffs, axis=1, keepdims=True)
    length = along - jnp.sum(crossed * coeffs, axis=1, keepdims=True)
    curvature = jnp.sum(jnp.where(lane == WIDTH, sums, 0.0), axis=1, keepdims=True) + regularize * length
    alpha = along / curvature

    start = pl.multiple_of((me_ref[0] // 4) * LANES, LANES)
    ysketch = y_ref[:, pl.ds(start, LANES)]
    rhs = rhs_ref[:, pl.ds(start, LANES)]
    direction = (rhs - jnp.sum(ysketch * to_column(coeffs, WIDTH), axis=0, keepdims=True)) / precond_shift
    image = image_rows + regularize * direction
    residual = rhs - alpha * image
    sketched_image = jnp.where(first, sums, 0.0) + regularize * pltpu.roll(crossed, LANES - WIDTH, 1)
    sketched_res = sketched_rhs - alpha * sketched_image
    res_coeffs = solve_gram(inverse, diagonal, sketched_res)
    precond_residual = (
        residual - jnp.sum(ysketch * to_column(res_coeffs, WIDTH), axis=0, keepdims=True)
    ) / precond_shift
    which = iota((8, LANES), 0)
    pack = jnp.where(
        which == 0, alpha * direction, jnp.where(which == 1, residual, precond_residual)
    )
    out_ref[...] = pltpu.roll(pack, ((4 - me_ref[0] % 4) % 4) * WIDTH, 1)


def exchange(value, axis):
    return lax.all_to_all(value, axis, 0, 0, tiled=True)


def shards(blocks, block_rows, block_cols, sketch, theta, rhs):
    values = blocks[0, 0]
    rows_idx = block_rows[0, 0]
    cols_idx = block_cols[0, 0]
    omega = sketch.T
    theta_pieces = theta.reshape(ROW_PARTS, PIECE)
    rhs_line = rhs.reshape(1, LOCAL)
    my_row = lax.axis_index("row").astype(jnp.int32).reshape(1)
    my_col = lax.axis_index("col").astype(jnp.int32).reshape(1)
    shape = jax.ShapeDtypeStruct
    work = 2 * BLOCKS * ORDER * ORDER

    with jax.named_scope("sketch_cols"):
        terms = call(
            sketch_body,
            [smem(), smem(), vmem(), vmem()],
            shape((ROW_PARTS, WIDTH, PIECE), F32),
            flops=work * WIDTH,
            name="sketch_cols",
        )(rows_idx, cols_idx, omega, values)
        parts = exchange(terms, "row")
    with jax.named_scope("scaled"):
        scaled = call(
            scale_body,
            [smem(), vmem(), vmem()],
            shape((ROW_PARTS, WIDTH, PIECE), BF16),
            name="scaled",
        )(my_row, parts, theta_pieces)
        scaled = exchange(scaled, "row")
    with jax.named_scope("ysketch"):
        terms = call(
            forward_body,
            [smem(), smem(), vmem(), vmem()],
            shape((COL_PARTS, 8, LANES), F32),
            flops=work * WIDTH,
            name="ysketch",
        )(rows_idx, cols_idx, scaled, values)
        parts = exchange(terms, "col")
        parts = call(
            spread_body, [vmem()], shape((COL_PARTS, 8, LANES), F32), name="ysketch_spread"
        )(parts)
        tiles = exchange(parts, "col")
    with jax.named_scope("gram"):
        ysketch, terms = call(
            gram_body,
            [smem(), smem(), vmem(), vmem(), vmem(), vmem()],
            (shape((WIDTH, LOCAL), F32), shape((ROW_PARTS, WIDTH + 8, PIECE + LANES), F32)),
            scratch=[
                pltpu.VMEM((LANES, LOCAL), F32),
                pltpu.VMEM((3 * WIDTH + 16, LOCAL), BF16),
                pltpu.VMEM((LOCAL // ORDER, 3 * WIDTH + 16, ORDER), F32),
            ],
            flops=work * WIDTH * 3,
            name="gram",
        )(rows_idx, cols_idx, tiles, omega, rhs_line, values)
        parts = exchange(terms, "row")
    with jax.named_scope("image_scaled"):
        terms, keep = call(
            factor_body,
            [smem(), vmem(), vmem()],
            (shape((4 * ROW_PARTS, LANES), F32), shape((2 * WIDTH + 24, LANES), F32)),
            name="image_scaled",
        )(my_row, parts, theta_pieces)
        parts = exchange(terms.reshape(ROW_PARTS, 4, LANES), "row").reshape(4 * ROW_PARTS, LANES)
    with jax.named_scope("image"):
        terms = call(
            image_body,
            [smem(), smem(), vmem(), vmem()],
            shape((2 * COL_PARTS, LANES), F32),
            scratch=[
                pltpu.VMEM((LOCAL // ORDER, 16, ORDER), BF16),
                pltpu.VMEM((LOCAL // ORDER, 8, ORDER), F32),
            ],
            flops=work,
            name="image",
        )(rows_idx, cols_idx, parts, values)
        parts = exchange(terms.reshape(COL_PARTS, 2, LANES), "col").reshape(2 * COL_PARTS, LANES)
    with jax.named_scope("step"):
        out = call(
            step_body,
            [smem(), vmem(), vmem(), vmem(), vmem()],
            shape((8, LANES), F32),
            name="step",
        )(my_col, parts, keep, ysketch, rhs_line)
    share = LOCAL // COL_PARTS
    return (out[0, :share], out[1, :share], out[2, :share])


def solution(mesh):
    in_specs = (
        P("row", "col", None, None, None),
        P("row", "col", None),
        P("row", "col", None),
        P("row", None),
        P("col"),
        P("row"),
    )
    out_specs = (P(("row", "col")), P(("row", "col")), P(("row", "col")))
    return jax.shard_map(shards, mesh=mesh, in_specs=in_specs, out_specs=out_specs, check_vma=False)
```

```python
import jax
import jax.numpy as jnp
from jax import lax
from jax.experimental import pallas as pl
from jax.experimental.pallas import tpu as pltpu
from jax.sharding import PartitionSpec as P

precond_shift = 1.0
regularize = 0.5

F32 = jnp.float32
BF16 = jnp.bfloat16
HIGHEST = lax.Precision.HIGHEST
LANES = 128
CORES = 2
X_PARTS = 4
Y_PARTS = 4
Z_PARTS = 16
COL_PARTS = Y_PARTS * Z_PARTS
BLOCKS = 8
ORDER = 512
LOCAL = 2048
WIDTH = 32
HALF = LOCAL // CORES
HALF_TILES = HALF // LANES
TILES = LOCAL // LANES
GROUPS = WIDTH // 8
IMAGE_TILES = GROUPS * HALF_TILES + 1
SENT_TILES = IMAGE_TILES + 3
VMEM_LIMIT = 24 * 1024 * 1024

NT = (((1,), (1,)), ((), ()))


def vmem():
    return pl.BlockSpec(memory_space=pltpu.VMEM)


def hbm():
    return pl.BlockSpec(memory_space=pltpu.HBM)


def smem():
    return pl.BlockSpec(memory_space=pltpu.SMEM)


def iota(shape, axis):
    return lax.broadcasted_iota(jnp.int32, shape, axis)


def call(body, in_specs, out_shape, scratch=(), flops=0, name=None):
    out_specs = jax.tree.map(lambda _: vmem(), out_shape)
    return pl.pallas_call(
        body,
        in_specs=in_specs,
        out_specs=out_specs,
        out_shape=out_shape,
        scratch_shapes=list(scratch),
        compiler_params=pltpu.CompilerParams(vmem_limit_bytes=VMEM_LIMIT),
        cost_estimate=pl.CostEstimate(flops=flops, bytes_accessed=1 << 20, transcendentals=0),
        name=name,
    )


def sketch_body(
    rows_hbm, cols_hbm, omega_hbm, blocks_hbm, out_ref, blocks_ref, rows_ref, cols_ref, omega_ref, sems
):
    copies = [
        pltpu.make_async_copy(rows_hbm, rows_ref, sems.at[0]),
        pltpu.make_async_copy(cols_hbm, cols_ref, sems.at[1]),
        pltpu.make_async_copy(omega_hbm, omega_ref, sems.at[2]),
    ]
    for n in range(BLOCKS):
        copies.append(pltpu.make_async_copy(blocks_hbm.at[n], blocks_ref.at[n], sems.at[3 + n]))
    for copy in copies:
        copy.start()
    out_ref[...] = jnp.zeros(out_ref.shape, F32)
    for copy in copies[:3]:
        copy.wait()
    for n in range(BLOCKS):
        copies[3 + n].wait()
        start = pl.multiple_of(rows_ref[0, n] * ORDER, ORDER)
        place = pl.multiple_of(cols_ref[0, n] % 2 * ORDER, ORDER)
        out_ref[cols_ref[0, n] // 2, :, pl.ds(place, ORDER)] += jnp.dot(
            omega_ref[:, pl.ds(start, ORDER)], blocks_ref[n], preferred_element_type=F32
        )


def pair_body(core_ref, parts_ref, out_ref):
    half = core_ref[0]
    total = (parts_ref[half] + parts_ref[CORES + half]).astype(BF16)
    for i in range(X_PARTS):
        out_ref[i] = total


def scale_body(core_ref, parts_ref, theta_ref, out_ref):
    total = parts_ref[0].astype(F32)
    for i in range(1, X_PARTS):
        total += parts_ref[i].astype(F32)
    out_ref[...] = (theta_ref[pl.ds(core_ref[0], 1), :] * total).astype(BF16)


def forward_body(rows_ref, cols_ref, scaled_ref, blocks_ref, out_ref):
    out_ref[...] = jnp.zeros(out_ref.shape, F32)
    for n in range(BLOCKS):
        place = pl.multiple_of(cols_ref[n] % 2 * ORDER, ORDER)
        left = scaled_ref[cols_ref[n] // 2, :, pl.ds(place, ORDER)]
        product = lax.dot_general(left, blocks_ref[n], NT, preferred_element_type=F32)
        first = rows_ref[n] * (ORDER // LANES)
        for g in range(GROUPS):
            for q in range(ORDER // LANES):
                out_ref[g, first + q] += product[8 * g : 8 * g + 8, LANES * q : LANES * (q + 1)]


def pack_square(square):
    packed = square[0:8]
    for g in range(1, GROUPS):
        packed += pltpu.roll(square[8 * g : 8 * g + 8], WIDTH * g, 1)
    return packed


def unpack_square(packed):
    lane = iota((8, LANES), 1)
    parts = [packed] + [pltpu.roll(packed, LANES - WIDTH * g, 1) for g in range(1, GROUPS)]
    return jnp.concatenate([jnp.where(lane < WIDTH, part, 0.0) for part in parts], axis=0)


def gram_body(
    rows_ref, cols_ref, tiles_ref, omega_ref, rhs_ref, blocks_ref, y_ref, out_ref, all_ref, cut_ref, acc_ref
):
    for g in range(GROUPS):
        for t in range(TILES):
            y_ref[8 * g : 8 * g + 8, LANES * t : LANES * (t + 1)] = tiles_ref[g, t]
    omega = omega_ref[...].astype(F32)
    ysketch = y_ref[...] + regularize * omega
    y_ref[...] = ysketch
    top = ysketch.astype(BF16)
    rest = ysketch - top.astype(F32)
    middle = rest.astype(BF16)
    low = (rest - middle.astype(F32)).astype(BF16)
    cut_ref[0:WIDTH, :] = top
    cut_ref[WIDTH : 2 * WIDTH, :] = middle
    cut_ref[2 * WIDTH : 3 * WIDTH, :] = low
    rhs = rhs_ref[...]
    rhs_top = rhs.astype(BF16).astype(F32)
    rhs_rest = rhs - rhs_top
    rhs_middle = rhs_rest.astype(BF16).astype(F32)
    rhs_low = rhs_rest - rhs_middle
    spot = iota((16, LOCAL), 0)
    rhs_cut = jnp.where(
        spot == 0, rhs_top, jnp.where(spot == 1, rhs_middle, jnp.where(spot == 2, rhs_low, 0.0))
    )
    cut_ref[3 * WIDTH :, :] = rhs_cut.astype(BF16)
    all_ref[0:WIDTH, :] = ysketch
    all_ref[WIDTH : 2 * WIDTH, :] = omega
    all_ref[2 * WIDTH :, :] = jnp.where(iota((LANES - 2 * WIDTH, LOCAL), 0) == 0, rhs, 0.0)

    products = lax.dot_general(
        all_ref[0 : 2 * WIDTH + 8, :], all_ref[...], NT, precision=HIGHEST, preferred_element_type=F32
    )
    lane = iota((WIDTH, LANES), 1)
    upper = products[0:WIDTH]
    middle = products[WIDTH : 2 * WIDTH]
    cross = jnp.where(lane < WIDTH, 0.5 * (middle + pltpu.roll(upper, LANES - WIDTH, 1)), 0.0)
    gram = jnp.where(lane < WIDTH, upper, 0.0) + precond_shift * cross
    out_ref[CORES * IMAGE_TILES] = pack_square(gram)
    out_ref[CORES * IMAGE_TILES + 1] = pack_square(cross)
    out_ref[CORES * IMAGE_TILES + 2] = products[2 * WIDTH :]

    acc_ref[...] = jnp.zeros(acc_ref.shape, F32)
    for n in range(BLOCKS):
        start = pl.multiple_of(rows_ref[n] * ORDER, ORDER)
        acc_ref[cols_ref[n]] += jnp.dot(
            cut_ref[:, pl.ds(start, ORDER)], blocks_ref[n], preferred_element_type=F32
        )
    spot = iota((8, LANES), 0)
    per_block = ORDER // LANES
    for h in range(CORES):
        rhs_tile = jnp.zeros((8, LANES), F32)
        for t in range(HALF_TILES):
            j = h * (HALF_TILES // per_block) + t // per_block
            at = LANES * (t % per_block)
            for g in range(GROUPS):
                out_ref[h * IMAGE_TILES + g * HALF_TILES + t] = acc_ref[
                    j, 8 * g : 8 * g + 8, at : at + LANES
                ] + (
                    acc_ref[j, WIDTH + 8 * g : WIDTH + 8 * g + 8, at : at + LANES]
                    + acc_ref[j, 2 * WIDTH + 8 * g : 2 * WIDTH + 8 * g + 8, at : at + LANES]
                )
            line = jnp.sum(acc_ref[j, 3 * WIDTH :, at : at + LANES], axis=0, keepdims=True)
            rhs_tile = jnp.where(spot == t, line, rhs_tile)
        out_ref[h * IMAGE_TILES + IMAGE_TILES - 1] = rhs_tile


def pair_image_body(core_ref, parts_ref, out_ref):
    first = core_ref[0] * IMAGE_TILES
    for k in range(SENT_TILES):
        at = first + k if k < IMAGE_TILES else (CORES - 1) * IMAGE_TILES + k
        tile = parts_ref[0, at] + parts_ref[1, at]
        for i in range(X_PARTS):
            out_ref[i, k] = tile


def to_column(row, shift):
    lane = iota((WIDTH, LANES), 1)
    return jnp.sum(
        jnp.where(lane == iota((WIDTH, LANES), 0) + shift, row, 0.0), axis=1, keepdims=True
    )


def to_row(column, shift):
    lane = iota((WIDTH, LANES), 1)
    return jnp.sum(
        jnp.where(lane == iota((WIDTH, LANES), 0) + shift, column, 0.0), axis=0, keepdims=True
    )


def solve_gram(inverse, diagonal, row):
    half = jnp.sum(inverse * pltpu.roll(row, WIDTH, 1), axis=1, keepdims=True) / diagonal
    return jnp.sum(inverse * half, axis=0, keepdims=True)


def factor_body(core_ref, parts_ref, theta_ref, out_ref, keep_ref, sum_ref):
    sum_ref[...] = (parts_ref[0] + parts_ref[1]) + (parts_ref[2] + parts_ref[3])
    gram = unpack_square(sum_ref[IMAGE_TILES])
    cross = unpack_square(sum_ref[IMAGE_TILES + 1])
    tail = sum_ref[IMAGE_TILES + 2]
    lane = iota((WIDTH, LANES), 1)
    spot = iota((WIDTH, LANES), 0)
    work = jnp.where(lane == spot + WIDTH, 1.0, gram)
    for k in range(WIDTH - 1):
        pivot = work[k : k + 1, :]
        scaled_pivot = pivot / pivot[:, k : k + 1]
        work = work - jnp.where(spot > k, work[:, k : k + 1], 0.0) * scaled_pivot
    diagonal = jnp.sum(jnp.where(lane == spot, work, 0.0), axis=1, keepdims=True)
    inverse = jnp.where((lane >= WIDTH) & (lane < 2 * WIDTH), work, 0.0)

    sketched_rhs = jnp.where(iota((1, LANES), 1) < WIDTH, tail[0:1], 0.0)
    coeffs = solve_gram(inverse, diagonal, sketched_rhs)
    column = to_column(coeffs, WIDTH)
    crossed = jnp.sum(cross * column, axis=0, keepdims=True)

    row = iota((8, LANES), 0)
    image = sum_ref[IMAGE_TILES - 1]
    for t in range(HALF_TILES):
        part = sum_ref[t] * column[0:8]
        for g in range(1, GROUPS):
            part += sum_ref[g * HALF_TILES + t] * column[8 * g : 8 * g + 8]
        image -= jnp.where(row == t, jnp.sum(part, axis=0, keepdims=True), 0.0)
    scaled = (theta_ref[core_ref[0]] * image).astype(BF16).astype(F32)
    groups = []
    for g in range(GROUPS):
        part = sum_ref[g * HALF_TILES] * scaled[0:1]
        for t in range(1, HALF_TILES):
            part += sum_ref[g * HALF_TILES + t] * scaled[t : t + 1]
        groups.append(jnp.sum(part, axis=1, keepdims=True))
    sketched = to_row(jnp.concatenate(groups, axis=0), 0)
    curvature = jnp.sum(jnp.sum(image * scaled, axis=0, keepdims=True), axis=1, keepdims=True)
    out_ref[0] = scaled
    out_ref[1] = jnp.where(
        row == 0, jnp.where(iota((8, LANES), 1) == WIDTH, curvature, sketched), 0.0
    )
    keep_ref[0:WIDTH, :] = inverse
    keep_ref[WIDTH : 2 * WIDTH, :] = jnp.broadcast_to(diagonal, (WIDTH, LANES))
    keep_ref[2 * WIDTH : 2 * WIDTH + 8, :] = tail
    keep_ref[2 * WIDTH + 8 : 2 * WIDTH + 16, :] = jnp.broadcast_to(coeffs, (8, LANES))
    keep_ref[2 * WIDTH + 16 :, :] = jnp.broadcast_to(crossed, (8, LANES))


def image_body(rows_ref, cols_ref, parts_ref, blocks_ref, out_ref, scaled_ref, acc_ref):
    sums = parts_ref[0, 1, 0:1, :] + parts_ref[1, 1, 0:1, :]
    per_block = ORDER // LANES
    for j in range(LOCAL // ORDER):
        h, first = j // 2, j % 2 * per_block
        line = jnp.concatenate(
            [parts_ref[h, 0, first + q : first + q + 1, :] for q in range(per_block)], axis=1
        )
        scaled_ref[j] = jnp.broadcast_to(line, (16, ORDER)).astype(BF16)
    acc_ref[...] = jnp.zeros(acc_ref.shape, F32)
    for n in range(BLOCKS):
        product = lax.dot_general(
            scaled_ref[cols_ref[n]], blocks_ref[n], NT, preferred_element_type=F32
        )
        acc_ref[rows_ref[n]] += product[0:8]
    even = iota((8, LANES), 0) % 2 == 0
    for t in range(TILES):
        at = LANES * (t % per_block)
        out_ref[8 * t : 8 * t + 8, :] = jnp.where(
            even, acc_ref[t // per_block, :, at : at + LANES], sums
        )


def step_body(me_ref, parts_ref, keep_ref, y_ref, rhs_ref, out_ref):
    total = parts_ref[0:8, :]
    for i in range(1, COL_PARTS // 4):
        total += parts_ref[8 * i : 8 * i + 8, :]
    even = iota((8, LANES), 0) % 2 == 0
    image_rows = jnp.sum(jnp.where(even, total, 0.0), axis=0, keepdims=True)
    sums = jnp.sum(jnp.where(even, 0.0, total), axis=0, keepdims=True)

    lane = iota((1, LANES), 1)
    first = lane < WIDTH
    inverse = keep_ref[0:WIDTH, :]
    diagonal = keep_ref[WIDTH : 2 * WIDTH, 0:1]
    tail = keep_ref[2 * WIDTH : 2 * WIDTH + 1, :]
    coeffs = keep_ref[2 * WIDTH + 8 : 2 * WIDTH + 9, :]
    crossed = keep_ref[2 * WIDTH + 16 : 2 * WIDTH + 17, :]
    sketched_rhs = jnp.where(first, tail, 0.0)
    square = jnp.sum(jnp.where(lane == 2 * WIDTH, tail, 0.0), axis=1, keepdims=True)
    along = square - jnp.sum(pltpu.roll(sketched_rhs, WIDTH, 1) * coeffs, axis=1, keepdims=True)
    length = along - jnp.sum(pltpu.roll(crossed, WIDTH, 1) * coeffs, axis=1, keepdims=True)
    curvature = jnp.sum(jnp.where(lane == WIDTH, sums, 0.0), axis=1, keepdims=True) + regularize * length
    alpha = along / curvature

    start = pl.multiple_of((me_ref[0] // 4) * LANES, LANES)
    ysketch = y_ref[:, pl.ds(start, LANES)]
    rhs = rhs_ref[:, pl.ds(start, LANES)]
    direction = (rhs - jnp.sum(ysketch * to_column(coeffs, WIDTH), axis=0, keepdims=True)) / precond_shift
    image = image_rows + regularize * direction
    residual = rhs - alpha * image
    sketched_image = jnp.where(first, sums, 0.0) + regularize * crossed
    sketched_res = sketched_rhs - alpha * sketched_image
    res_coeffs = solve_gram(inverse, diagonal, sketched_res)
    precond_residual = (
        residual - jnp.sum(ysketch * to_column(res_coeffs, WIDTH), axis=0, keepdims=True)
    ) / precond_shift
    which = iota((8, LANES), 0)
    pack = jnp.where(
        which == 0, alpha * direction, jnp.where(which == 1, residual, precond_residual)
    )
    out_ref[...] = pltpu.roll(pack, ((4 - me_ref[0] % 4) % 4) * WIDTH, 1)


def exchange(value, axis):
    return lax.all_to_all(value, axis, 0, 0, tiled=True)


def copies(value, count):
    return jnp.broadcast_to(value[None], (count,) + value.shape)


def shards(blocks, block_rows, block_cols, sketch, theta, rhs):
    values = blocks[0, 0]
    rows_idx = block_rows[0, 0]
    cols_idx = block_cols[0, 0]
    omega = sketch.T
    rhs_line = rhs.reshape(1, LOCAL)
    my_core = lax.axis_index("core").astype(jnp.int32).reshape(1)
    my_col = lax.axis_index(("y", "z")).astype(jnp.int32).reshape(1)
    shape = jax.ShapeDtypeStruct
    work = 2 * BLOCKS * ORDER * ORDER

    with jax.named_scope("sketch_cols"):
        terms, values = call(
            sketch_body,
            [hbm(), hbm(), hbm(), hbm()],
            (shape((CORES, WIDTH, HALF), F32), shape(values.shape, BF16)),
            scratch=[
                pltpu.SMEM((1, BLOCKS), jnp.int32),
                pltpu.SMEM((1, BLOCKS), jnp.int32),
                pltpu.VMEM((WIDTH, LOCAL), BF16),
                pltpu.SemaphoreType.DMA((3 + BLOCKS,)),
            ],
            flops=work * WIDTH,
            name="sketch_cols",
        )(block_rows[0], block_cols[0], omega, values)
        parts = lax.all_gather(terms, "core", tiled=True)
        parts = call(
            pair_body, [smem(), vmem()], shape((X_PARTS, WIDTH, HALF), BF16), name="pair"
        )(my_core, parts)
        parts = exchange(parts, "x")
    with jax.named_scope("scaled"):
        scaled = call(
            scale_body, [smem(), vmem(), vmem()], shape((WIDTH, HALF), BF16), name="scaled"
        )(my_core, parts, theta.reshape(CORES, HALF))
        scaled = lax.all_gather(scaled, "core")
    with jax.named_scope("ysketch"):
        terms = call(
            forward_body,
            [smem(), smem(), vmem(), vmem()],
            shape((GROUPS, TILES, 8, LANES), F32),
            flops=work * WIDTH,
            name="ysketch",
        )(rows_idx, cols_idx, scaled, values)
        parts = jnp.sum(exchange(terms, "y"), axis=0)
        parts = jnp.sum(exchange(parts, "z"), axis=0)
        parts = exchange(copies(parts, Z_PARTS), "z")
        tiles = exchange(copies(parts, Y_PARTS), "y")
    with jax.named_scope("gram"):
        ysketch, terms = call(
            gram_body,
            [smem(), smem(), vmem(), vmem(), vmem(), vmem()],
            (shape((WIDTH, LOCAL), F32), shape((CORES * IMAGE_TILES + 3, 8, LANES), F32)),
            scratch=[
                pltpu.VMEM((LANES, LOCAL), F32),
                pltpu.VMEM((3 * WIDTH + 16, LOCAL), BF16),
                pltpu.VMEM((LOCAL // ORDER, 3 * WIDTH + 16, ORDER), F32),
            ],
            flops=work * WIDTH * 3,
            name="gram",
        )(rows_idx, cols_idx, tiles, omega, rhs_line, values)
        parts = lax.all_gather(terms, "core")
        parts = call(
            pair_image_body,
            [smem(), vmem()],
            shape((X_PARTS, SENT_TILES, 8, LANES), F32),
            name="pair_image",
        )(my_core, parts)
        parts = exchange(parts, "x")
    with jax.named_scope("image_scaled"):
        terms, keep = call(
            factor_body,
            [smem(), vmem(), vmem()],
            (shape((2, 8, LANES), F32), shape((2 * WIDTH + 24, LANES), F32)),
            scratch=[pltpu.VMEM((SENT_TILES, 8, LANES), F32)],
            name="image_scaled",
        )(my_core, parts, theta.reshape(CORES, HALF_TILES, LANES))
        parts = lax.all_gather(terms, "core")
    with jax.named_scope("image"):
        terms = call(
            image_body,
            [smem(), smem(), vmem(), vmem()],
            shape((2 * COL_PARTS, LANES), F32),
            scratch=[
                pltpu.VMEM((LOCAL // ORDER, 16, ORDER), BF16),
                pltpu.VMEM((LOCAL // ORDER, 8, ORDER), F32),
            ],
            flops=work,
            name="image",
        )(rows_idx, cols_idx, parts, values)
        parts = exchange(terms.reshape(COL_PARTS, 2, LANES), ("y", "z")).reshape(2 * COL_PARTS, LANES)
    with jax.named_scope("step"):
        out = call(
            step_body,
            [smem(), vmem(), vmem(), vmem(), vmem()],
            shape((8, LANES), F32),
            name="step",
        )(my_col, parts, keep, ysketch, rhs_line)
    share = LOCAL // COL_PARTS
    return (out[0, :share], out[1, :share], out[2, :share])


def solution(mesh):
    row, col = ("x", "core"), ("y", "z")
    fine = jax.sharding.Mesh(
        mesh.devices.reshape(X_PARTS, CORES, Y_PARTS, Z_PARTS), ("x", "core", "y", "z")
    )
    in_specs = (
        P(row, col, None, None, None),
        P(row, col, None),
        P(row, col, None),
        P(row, None),
        P(col),
        P(row),
    )
    out_specs = (P(row + col), P(row + col), P(row + col))
    return jax.shard_map(shards, mesh=fine, in_specs=in_specs, out_specs=out_specs, check_vma=False)
```

```python
import jax
import jax.numpy as jnp
from jax import lax
from jax.experimental import pallas as pl
from jax.experimental.pallas import tpu as pltpu
from jax.sharding import PartitionSpec as P

precond_shift = 1.0
regularize = 0.5

F32 = jnp.float32
BF16 = jnp.bfloat16
HIGHEST = lax.Precision.HIGHEST
LANES = 128
CORES = 2
X_PARTS = 4
Y_PARTS = 4
Z_PARTS = 16
COL_PARTS = Y_PARTS * Z_PARTS
BLOCKS = 8
ORDER = 512
LOCAL = 2048
WIDTH = 32
HALF = LOCAL // CORES
HALF_TILES = HALF // LANES
TILES = LOCAL // LANES
GROUPS = WIDTH // 8
IMAGE_TILES = GROUPS * HALF_TILES + 1
SENT_TILES = IMAGE_TILES + 3
VMEM_LIMIT = 24 * 1024 * 1024
FIRST_LIMIT = 64 * 1024 * 1024 - 64 * 1024

NT = (((1,), (1,)), ((), ()))


def vmem():
    return pl.BlockSpec(memory_space=pltpu.VMEM)


def hbm():
    return pl.BlockSpec(memory_space=pltpu.HBM)


def smem():
    return pl.BlockSpec(memory_space=pltpu.SMEM)


def iota(shape, axis):
    return lax.broadcasted_iota(jnp.int32, shape, axis)


def call(body, in_specs, out_shape, scratch=(), flops=0, name=None, limit=VMEM_LIMIT):
    out_specs = jax.tree.map(lambda _: vmem(), out_shape)
    return pl.pallas_call(
        body,
        in_specs=in_specs,
        out_specs=out_specs,
        out_shape=out_shape,
        scratch_shapes=list(scratch),
        compiler_params=pltpu.CompilerParams(vmem_limit_bytes=limit),
        cost_estimate=pl.CostEstimate(flops=flops, bytes_accessed=1 << 20, transcendentals=0),
        name=name,
    )


def sketch_body(
    rows_hbm, cols_hbm, omega_hbm, blocks_hbm, out_ref, rows_ref, cols_ref, omega_ref, blocks_ref, sems
):
    first = [
        pltpu.make_async_copy(rows_hbm, rows_ref, sems.at[BLOCKS]),
        pltpu.make_async_copy(cols_hbm, cols_ref, sems.at[BLOCKS + 1]),
        pltpu.make_async_copy(omega_hbm, omega_ref, sems.at[BLOCKS + 2]),
    ]
    for copy in first:
        copy.start()
    arrivals = [
        pltpu.make_async_copy(blocks_hbm.at[n], blocks_ref.at[n], sems.at[n]) for n in range(BLOCKS)
    ]
    for copy in arrivals:
        copy.start()
    out_ref[...] = jnp.zeros(out_ref.shape, F32)
    for copy in first:
        copy.wait()
    for n in range(BLOCKS):
        arrivals[n].wait()
        start = pl.multiple_of(rows_ref[0, n] * ORDER, ORDER)
        place = pl.multiple_of(cols_ref[0, n] % 2 * ORDER, ORDER)
        out_ref[cols_ref[0, n] // 2, :, pl.ds(place, ORDER)] += jnp.dot(
            omega_ref[:, pl.ds(start, ORDER)], blocks_ref[n], preferred_element_type=F32
        )


def pair_body(core_ref, parts_ref, out_ref):
    half = core_ref[0]
    total = parts_ref[0, half] + parts_ref[1, half]
    for i in range(X_PARTS):
        out_ref[i] = total


def scale_body(core_ref, parts_ref, theta_ref, out_ref):
    total = (parts_ref[0] + parts_ref[1]) + (parts_ref[2] + parts_ref[3])
    tile = theta_ref[core_ref[0]]
    theta = jnp.concatenate([tile[t : t + 1, :] for t in range(HALF_TILES)], axis=1)
    out_ref[...] = (theta * total).astype(BF16)


def forward_body(rows_ref, cols_ref, scaled_ref, blocks_ref, out_ref):
    out_ref[...] = jnp.zeros(out_ref.shape, F32)
    for n in range(BLOCKS):
        place = pl.multiple_of(cols_ref[n] % 2 * ORDER, ORDER)
        left = scaled_ref[cols_ref[n] // 2, :, pl.ds(place, ORDER)]
        product = lax.dot_general(left, blocks_ref[n], NT, preferred_element_type=F32)
        first = rows_ref[n] * (ORDER // LANES)
        for g in range(GROUPS):
            for q in range(ORDER // LANES):
                out_ref[g, first + q] += product[8 * g : 8 * g + 8, LANES * q : LANES * (q + 1)]


def gather_body(parts_ref, out_ref):
    out_ref[...] = (parts_ref[0] + parts_ref[1]) + (parts_ref[2] + parts_ref[3])


def copy_body(part_ref, out_ref):
    for i in range(Y_PARTS):
        out_ref[i] = part_ref[...]


def spread_body(parts_ref, out_ref):
    sums = [parts_ref[i] for i in range(Z_PARTS)]
    while len(sums) > 1:
        sums = [a + b for a, b in zip(sums[::2], sums[1::2])]
    for i in range(Z_PARTS):
        out_ref[i] = sums[0]


def pack_square(square):
    packed = square[0:8]
    for g in range(1, GROUPS):
        packed += pltpu.roll(square[8 * g : 8 * g + 8], WIDTH * g, 1)
    return packed


def unpack_square(packed):
    lane = iota((8, LANES), 1)
    parts = [packed] + [pltpu.roll(packed, LANES - WIDTH * g, 1) for g in range(1, GROUPS)]
    return jnp.concatenate([jnp.where(lane < WIDTH, part, 0.0) for part in parts], axis=0)


def gram_body(
    rows_ref,
    cols_ref,
    tiles_ref,
    omega_ref,
    rhs_ref,
    blocks_ref,
    y_ref,
    out_ref,
    all_ref,
    cut_ref,
    acc_ref,
):
    for g in range(GROUPS):
        for t in range(TILES):
            y_ref[8 * g : 8 * g + 8, LANES * t : LANES * (t + 1)] = tiles_ref[g, t]
    omega = omega_ref[...].astype(F32)
    ysketch = y_ref[...] + regularize * omega
    y_ref[...] = ysketch
    top = ysketch.astype(BF16)
    rest = ysketch - top.astype(F32)
    middle = rest.astype(BF16)
    low = (rest - middle.astype(F32)).astype(BF16)
    cut_ref[0:WIDTH, :] = top
    cut_ref[WIDTH : 2 * WIDTH, :] = middle
    cut_ref[2 * WIDTH : 3 * WIDTH, :] = low
    rhs = rhs_ref[...]
    rhs_top = rhs.astype(BF16).astype(F32)
    rhs_rest = rhs - rhs_top
    rhs_middle = rhs_rest.astype(BF16).astype(F32)
    rhs_low = rhs_rest - rhs_middle
    spot = iota((16, LOCAL), 0)
    rhs_cut = jnp.where(
        spot == 0, rhs_top, jnp.where(spot == 1, rhs_middle, jnp.where(spot == 2, rhs_low, 0.0))
    )
    cut_ref[3 * WIDTH :, :] = rhs_cut.astype(BF16)
    all_ref[0:WIDTH, :] = ysketch
    all_ref[WIDTH : 2 * WIDTH, :] = omega
    all_ref[2 * WIDTH :, :] = jnp.where(iota((LANES - 2 * WIDTH, LOCAL), 0) == 0, rhs, 0.0)

    products = lax.dot_general(
        all_ref[0 : 2 * WIDTH + 8, :], all_ref[...], NT, precision=HIGHEST, preferred_element_type=F32
    )
    lane = iota((WIDTH, LANES), 1)
    upper = products[0:WIDTH]
    middle = products[WIDTH : 2 * WIDTH]
    cross = jnp.where(lane < WIDTH, 0.5 * (middle + pltpu.roll(upper, LANES - WIDTH, 1)), 0.0)
    gram = jnp.where(lane < WIDTH, upper, 0.0) + precond_shift * cross
    out_ref[CORES * IMAGE_TILES] = pack_square(gram)
    out_ref[CORES * IMAGE_TILES + 1] = pack_square(cross)
    out_ref[CORES * IMAGE_TILES + 2] = products[2 * WIDTH :]

    acc_ref[...] = jnp.zeros(acc_ref.shape, F32)
    for n in range(BLOCKS):
        start = pl.multiple_of(rows_ref[n] * ORDER, ORDER)
        acc_ref[cols_ref[n]] += jnp.dot(
            cut_ref[:, pl.ds(start, ORDER)], blocks_ref[n], preferred_element_type=F32
        )
    spot = iota((8, LANES), 0)
    per_block = ORDER // LANES
    for h in range(CORES):
        rhs_tile = jnp.zeros((8, LANES), F32)
        for t in range(HALF_TILES):
            j = h * (HALF_TILES // per_block) + t // per_block
            at = LANES * (t % per_block)
            for g in range(GROUPS):
                out_ref[h * IMAGE_TILES + g * HALF_TILES + t] = acc_ref[
                    j, 8 * g : 8 * g + 8, at : at + LANES
                ] + (
                    acc_ref[j, WIDTH + 8 * g : WIDTH + 8 * g + 8, at : at + LANES]
                    + acc_ref[j, 2 * WIDTH + 8 * g : 2 * WIDTH + 8 * g + 8, at : at + LANES]
                )
            line = jnp.sum(acc_ref[j, 3 * WIDTH :, at : at + LANES], axis=0, keepdims=True)
            rhs_tile = jnp.where(spot == t, line, rhs_tile)
        out_ref[h * IMAGE_TILES + IMAGE_TILES - 1] = rhs_tile


def pair_image_body(core_ref, parts_ref, out_ref):
    first = core_ref[0] * IMAGE_TILES
    for k in range(SENT_TILES):
        at = first + k if k < IMAGE_TILES else (CORES - 1) * IMAGE_TILES + k
        tile = parts_ref[0, at] + parts_ref[1, at]
        for i in range(X_PARTS):
            out_ref[i, k] = tile


def to_column(row, shift):
    lane = iota((WIDTH, LANES), 1)
    return jnp.sum(
        jnp.where(lane == iota((WIDTH, LANES), 0) + shift, row, 0.0), axis=1, keepdims=True
    )


def to_row(column, shift):
    lane = iota((WIDTH, LANES), 1)
    return jnp.sum(
        jnp.where(lane == iota((WIDTH, LANES), 0) + shift, column, 0.0), axis=0, keepdims=True
    )


def eliminate(work, panel):
    spot = iota((WIDTH, LANES), 0)
    for k in range(0, WIDTH, panel):
        rows = [work[k + i : k + i + 1, :] for i in range(panel)]
        columns = [jnp.broadcast_to(work[:, k + i : k + i + 1], work.shape) for i in range(panel)]
        square = [
            [jnp.broadcast_to(rows[i][:, k + j : k + j + 1], (1, LANES)) for j in range(panel)]
            for i in range(panel)
        ]
        update = jnp.zeros(work.shape, F32)
        for i in range(panel):
            reciprocal = 1.0 / square[i][i]
            for j in range(i + 1, panel):
                factor = square[i][j] * reciprocal
                rows[j] = rows[j] - factor * rows[i]
                columns[j] = columns[j] - factor * columns[i]
                for m in range(j, panel):
                    square[j][m] = square[j][m] - factor * square[i][m]
            update += columns[i] * (rows[i] * reciprocal)
        work = jnp.where(spot >= k + panel, work - update, work)
        for i in range(1, panel):
            work = jnp.where(spot == k + i, rows[i], work)
    return work


def solve_gram(inverse, diagonal, row):
    half = jnp.sum(inverse * pltpu.roll(row, WIDTH, 1), axis=1, keepdims=True) / diagonal
    return jnp.sum(inverse * half, axis=0, keepdims=True)


def factor_body(core_ref, parts_ref, theta_ref, out_ref, keep_ref, sum_ref):
    sum_ref[...] = (parts_ref[0] + parts_ref[1]) + (parts_ref[2] + parts_ref[3])
    gram = unpack_square(sum_ref[IMAGE_TILES])
    cross = unpack_square(sum_ref[IMAGE_TILES + 1])
    tail = sum_ref[IMAGE_TILES + 2]
    lane = iota((WIDTH, LANES), 1)
    spot = iota((WIDTH, LANES), 0)
    work = eliminate(jnp.where(lane == spot + WIDTH, 1.0, gram), 4)
    diagonal = jnp.sum(jnp.where(lane == spot, work, 0.0), axis=1, keepdims=True)
    inverse = jnp.where((lane >= WIDTH) & (lane < 2 * WIDTH), work, 0.0)

    sketched_rhs = jnp.where(iota((1, LANES), 1) < WIDTH, tail[0:1], 0.0)
    coeffs = solve_gram(inverse, diagonal, sketched_rhs)
    column = to_column(coeffs, WIDTH)
    crossed = jnp.sum(cross * column, axis=0, keepdims=True)

    row = iota((8, LANES), 0)
    image = sum_ref[IMAGE_TILES - 1]
    for t in range(HALF_TILES):
        part = sum_ref[t] * column[0:8]
        for g in range(1, GROUPS):
            part += sum_ref[g * HALF_TILES + t] * column[8 * g : 8 * g + 8]
        image -= jnp.where(row == t, jnp.sum(part, axis=0, keepdims=True), 0.0)
    scaled = (theta_ref[core_ref[0]] * image).astype(BF16).astype(F32)
    groups = []
    for g in range(GROUPS):
        part = sum_ref[g * HALF_TILES] * scaled[0:1]
        for t in range(1, HALF_TILES):
            part += sum_ref[g * HALF_TILES + t] * scaled[t : t + 1]
        groups.append(jnp.sum(part, axis=1, keepdims=True))
    sketched = to_row(jnp.concatenate(groups, axis=0), 0)
    curvature = jnp.sum(jnp.sum(image * scaled, axis=0, keepdims=True), axis=1, keepdims=True)
    out_ref[0] = scaled
    out_ref[1] = jnp.where(
        row == 0, jnp.where(iota((8, LANES), 1) == WIDTH, curvature, sketched), 0.0
    )
    keep_ref[0:WIDTH, :] = inverse
    keep_ref[WIDTH : 2 * WIDTH, :] = jnp.broadcast_to(diagonal, (WIDTH, LANES))
    keep_ref[2 * WIDTH : 2 * WIDTH + 8, :] = tail
    keep_ref[2 * WIDTH + 8 : 2 * WIDTH + 16, :] = jnp.broadcast_to(coeffs, (8, LANES))
    keep_ref[2 * WIDTH + 16 :, :] = jnp.broadcast_to(crossed, (8, LANES))


def image_body(rows_ref, cols_ref, parts_ref, blocks_ref, out_ref, scaled_ref, acc_ref):
    sums = parts_ref[0, 1, 0:1, :] + parts_ref[1, 1, 0:1, :]
    per_block = ORDER // LANES
    for j in range(LOCAL // ORDER):
        h, first = j // 2, j % 2 * per_block
        line = jnp.concatenate(
            [parts_ref[h, 0, first + q : first + q + 1, :] for q in range(per_block)], axis=1
        )
        scaled_ref[j] = jnp.broadcast_to(line, (16, ORDER)).astype(BF16)
    acc_ref[...] = jnp.zeros(acc_ref.shape, F32)
    for n in range(BLOCKS):
        product = lax.dot_general(
            scaled_ref[cols_ref[n]], blocks_ref[n], NT, preferred_element_type=F32
        )
        acc_ref[rows_ref[n]] += product[0:8]
    lane = iota((8, LANES), 1)
    shares = LANES // WIDTH
    sums = jnp.broadcast_to(pltpu.roll(sums, WIDTH, 1), (8, LANES))
    row = iota((8, LANES), 0)
    for u in range(TILES // 2):
        pack = sums
        for v in range(2):
            t = 2 * u + v
            at = LANES * (t % per_block)
            tile = acc_ref[t // per_block, :, at : at + LANES]
            for q in range(shares):
                turned = tile if q == 0 else pltpu.roll(tile, LANES - WIDTH * q, 1)
                pack = jnp.where((lane < WIDTH) & (row == shares * v + q), turned, pack)
        out_ref[8 * u : 8 * u + 8, :] = pack


def step_body(me_ref, parts_ref, keep_ref, y_ref, rhs_ref, solution_ref, residual_ref, precond_ref):
    total = parts_ref[0:8, :]
    for i in range(1, COL_PARTS // 8):
        total += parts_ref[8 * i : 8 * i + 8, :]
    image_rows = jnp.sum(total, axis=0, keepdims=True)
    sums = pltpu.roll(image_rows, LANES - WIDTH, 1)

    lane = iota((1, LANES), 1)
    first = lane < WIDTH
    inverse = keep_ref[0:WIDTH, :]
    diagonal = keep_ref[WIDTH : 2 * WIDTH, 0:1]
    tail = keep_ref[2 * WIDTH : 2 * WIDTH + 1, :]
    coeffs = keep_ref[2 * WIDTH + 8 : 2 * WIDTH + 9, :]
    crossed = keep_ref[2 * WIDTH + 16 : 2 * WIDTH + 17, :]
    sketched_rhs = jnp.where(first, tail, 0.0)
    square = jnp.sum(jnp.where(lane == 2 * WIDTH, tail, 0.0), axis=1, keepdims=True)
    along = square - jnp.sum(pltpu.roll(sketched_rhs, WIDTH, 1) * coeffs, axis=1, keepdims=True)
    length = along - jnp.sum(pltpu.roll(crossed, WIDTH, 1) * coeffs, axis=1, keepdims=True)
    curvature = jnp.sum(jnp.where(lane == WIDTH, sums, 0.0), axis=1, keepdims=True) + regularize * length
    alpha = along / curvature

    start = pl.multiple_of((me_ref[0] // 4) * LANES, LANES)
    turn = ((4 - me_ref[0] % 4) % 4) * WIDTH
    ysketch = pltpu.roll(y_ref[:, pl.ds(start, LANES)], turn, 1)
    rhs = pltpu.roll(rhs_ref[:, pl.ds(start, LANES)], turn, 1)
    direction = (rhs - jnp.sum(ysketch * to_column(coeffs, WIDTH), axis=0, keepdims=True)) / precond_shift
    image = image_rows + regularize * direction
    residual = rhs - alpha * image
    sketched_image = jnp.where(first, sums, 0.0) + regularize * crossed
    sketched_res = sketched_rhs - alpha * sketched_image
    res_coeffs = solve_gram(inverse, diagonal, sketched_res)
    precond_residual = (
        residual - jnp.sum(ysketch * to_column(res_coeffs, WIDTH), axis=0, keepdims=True)
    ) / precond_shift
    solution_ref[...] = (alpha * direction)[0, :WIDTH]
    residual_ref[...] = residual[0, :WIDTH]
    precond_ref[...] = precond_residual[0, :WIDTH]


def exchange(value, axis):
    return lax.all_to_all(value, axis, 0, 0, tiled=True)


def shards(blocks, block_rows, block_cols, sketch, theta, rhs):
    values = blocks[0, 0]
    rows_idx = block_rows[0, 0]
    cols_idx = block_cols[0, 0]
    omega = sketch.T
    rhs_line = rhs.reshape(1, LOCAL)
    theta_tiles = theta.reshape(CORES, HALF_TILES, LANES)
    my_core = lax.axis_index("core").astype(jnp.int32).reshape(1)
    my_col = lax.axis_index(("y", "z")).astype(jnp.int32).reshape(1)
    shape = jax.ShapeDtypeStruct
    work = 2 * BLOCKS * ORDER * ORDER

    with jax.named_scope("sketch_cols"):
        terms = call(
            sketch_body,
            [hbm(), hbm(), hbm(), hbm()],
            shape((CORES, WIDTH, HALF), F32),
            scratch=[
                pltpu.SMEM((1, BLOCKS), jnp.int32),
                pltpu.SMEM((1, BLOCKS), jnp.int32),
                pltpu.VMEM((WIDTH, LOCAL), BF16),
                pltpu.VMEM(values.shape, BF16),
                pltpu.SemaphoreType.DMA((BLOCKS + 3,)),
            ],
            flops=work * WIDTH,
            name="sketch_cols",
            limit=FIRST_LIMIT,
        )(block_rows[0], block_cols[0], omega, values)
        parts = lax.all_gather(terms, "core")
        parts = call(
            pair_body, [smem(), vmem()], shape((X_PARTS, WIDTH, HALF), F32), name="pair"
        )(my_core, parts)
        parts = exchange(parts, "x")
    with jax.named_scope("scaled"):
        scaled = call(
            scale_body, [smem(), vmem(), vmem()], shape((WIDTH, HALF), BF16), name="scaled"
        )(my_core, parts, theta_tiles)
        scaled = lax.all_gather(scaled, "core")
    with jax.named_scope("ysketch"):
        terms = call(
            forward_body,
            [smem(), smem(), vmem(), vmem()],
            shape((GROUPS, TILES, 8, LANES), F32),
            flops=work * WIDTH,
            name="ysketch",
        )(rows_idx, cols_idx, scaled, values)
        parts = exchange(terms, "y")
        parts = call(gather_body, [vmem()], shape((Z_PARTS, 8, LANES), F32), name="gather")(parts)
        parts = call(
            spread_body,
            [vmem()],
            shape((Z_PARTS, 8, LANES), F32),
            name="spread",
        )(exchange(parts, "z"))
        parts = exchange(parts, "z")
        tiles = call(
            copy_body, [vmem()], shape((Y_PARTS, Z_PARTS, 8, LANES), F32), name="copies"
        )(parts)
        tiles = exchange(tiles, "y")
    with jax.named_scope("gram"):
        ysketch, terms = call(
            gram_body,
            [smem(), smem(), vmem(), vmem(), vmem(), vmem()],
            (shape((WIDTH, LOCAL), F32), shape((CORES * IMAGE_TILES + 3, 8, LANES), F32)),
            scratch=[
                pltpu.VMEM((LANES, LOCAL), F32),
                pltpu.VMEM((3 * WIDTH + 16, LOCAL), BF16),
                pltpu.VMEM((LOCAL // ORDER, 3 * WIDTH + 16, ORDER), F32),
            ],
            flops=work * WIDTH * 3,
            name="gram",
        )(rows_idx, cols_idx, tiles, omega, rhs_line, values)
        parts = lax.all_gather(terms, "core")
        parts = call(
            pair_image_body,
            [smem(), vmem()],
            shape((X_PARTS, SENT_TILES, 8, LANES), F32),
            name="pair_image",
        )(my_core, parts)
        parts = exchange(parts, "x")
    with jax.named_scope("image_scaled"):
        terms, keep = call(
            factor_body,
            [smem(), vmem(), vmem()],
            (shape((2, 8, LANES), F32), shape((2 * WIDTH + 24, LANES), F32)),
            scratch=[pltpu.VMEM((SENT_TILES, 8, LANES), F32)],
            name="image_scaled",
        )(my_core, parts, theta_tiles)
        parts = lax.all_gather(terms, "core")
    with jax.named_scope("image"):
        terms = call(
            image_body,
            [smem(), smem(), vmem(), vmem()],
            shape((COL_PARTS, LANES), F32),
            scratch=[
                pltpu.VMEM((LOCAL // ORDER, 16, ORDER), BF16),
                pltpu.VMEM((LOCAL // ORDER, 8, ORDER), F32),
            ],
            flops=work,
            name="image",
        )(rows_idx, cols_idx, parts, values)
        parts = exchange(terms, ("y", "z"))
    with jax.named_scope("step"):
        share = shape((LOCAL // COL_PARTS,), F32)
        return call(
            step_body,
            [smem(), vmem(), vmem(), vmem(), vmem()],
            (share, share, share),
            name="step",
        )(my_col, parts, keep, ysketch, rhs_line)


def solution(mesh):
    row, col = ("x", "core"), ("y", "z")
    fine = jax.sharding.Mesh(
        mesh.devices.reshape(X_PARTS, CORES, Y_PARTS, Z_PARTS), ("x", "core", "y", "z")
    )
    in_specs = (
        P(row, col, None, None, None),
        P(row, col, None),
        P(row, col, None),
        P(row, None),
        P(col),
        P(row),
    )
    out_specs = (P(row + col), P(row + col), P(row + col))
    return jax.shard_map(shards, mesh=fine, in_specs=in_specs, out_specs=out_specs, check_vma=False)
```

```python
import jax
import jax.numpy as jnp
from jax import lax
from jax.experimental import pallas as pl
from jax.experimental.pallas import tpu as pltpu
from jax.sharding import PartitionSpec as P

precond_shift = 1.0
regularize = 0.5

F32 = jnp.float32
BF16 = jnp.bfloat16
HIGHEST = lax.Precision.HIGHEST
LANES = 128
CORES = 2
X_PARTS = 4
Y_PARTS = 4
FAR_PARTS = 4
NEAR_PARTS = 4
COL_PARTS = Y_PARTS * FAR_PARTS * NEAR_PARTS
BLOCKS = 8
ORDER = 512
LOCAL = 2048
WIDTH = 32
HALF = LOCAL // CORES
HALF_TILES = HALF // LANES
TILES = LOCAL // LANES
GROUPS = WIDTH // 8
SHARES = Y_PARTS * NEAR_PARTS
SHARE_TILES = GROUPS * TILES // SHARES
IMAGE_TILES = GROUPS * HALF_TILES + 1
SENT_TILES = IMAGE_TILES + 3
VMEM_LIMIT = 24 * 1024 * 1024

NT = (((1,), (1,)), ((), ()))


def vmem():
    return pl.BlockSpec(memory_space=pltpu.VMEM)


def smem():
    return pl.BlockSpec(memory_space=pltpu.SMEM)


def iota(shape, axis):
    return lax.broadcasted_iota(jnp.int32, shape, axis)


def call(body, in_specs, out_shape, scratch=(), flops=0, name=None):
    out_specs = jax.tree.map(lambda _: vmem(), out_shape)
    return pl.pallas_call(
        body,
        in_specs=in_specs,
        out_specs=out_specs,
        out_shape=out_shape,
        scratch_shapes=list(scratch),
        compiler_params=pltpu.CompilerParams(vmem_limit_bytes=VMEM_LIMIT),
        cost_estimate=pl.CostEstimate(flops=flops, bytes_accessed=1 << 20, transcendentals=0),
        name=name,
    )


def sketch_body(rows_ref, cols_ref, omega_ref, blocks_ref, out_ref):
    out_ref[...] = jnp.zeros(out_ref.shape, F32)
    for n in range(BLOCKS):
        start = pl.multiple_of(rows_ref[n] * ORDER, ORDER)
        place = pl.multiple_of(cols_ref[n] % 2 * ORDER, ORDER)
        out_ref[cols_ref[n] // 2, :, pl.ds(place, ORDER)] += jnp.dot(
            omega_ref[:, pl.ds(start, ORDER)], blocks_ref[n], preferred_element_type=F32
        )


def pair_body(core_ref, parts_ref, out_ref):
    half = core_ref[0]
    total = parts_ref[0, half] + parts_ref[1, half]
    for i in range(X_PARTS):
        out_ref[i] = total


def scale_body(core_ref, parts_ref, theta_ref, out_ref):
    total = (parts_ref[0] + parts_ref[1]) + (parts_ref[2] + parts_ref[3])
    tile = theta_ref[core_ref[0]]
    theta = jnp.concatenate([tile[t : t + 1, :] for t in range(HALF_TILES)], axis=1)
    out_ref[...] = (theta * total).astype(BF16)


def forward_body(rows_ref, cols_ref, scaled_ref, blocks_ref, out_ref):
    out_ref[...] = jnp.zeros(out_ref.shape, F32)
    for n in range(BLOCKS):
        place = pl.multiple_of(cols_ref[n] % 2 * ORDER, ORDER)
        left = scaled_ref[cols_ref[n] // 2, :, pl.ds(place, ORDER)]
        product = lax.dot_general(left, blocks_ref[n], NT, preferred_element_type=F32)
        for g in range(GROUPS):
            for q in range(ORDER // LANES):
                out_ref[g * (LOCAL // ORDER) + rows_ref[n], q] += product[8 * g : 8 * g + 8, LANES * q : LANES * (q + 1)]


def spread_body(parts_ref, out_ref):
    sums = [parts_ref[i] for i in range(parts_ref.shape[0])]
    while len(sums) > 1:
        sums = [a + b for a, b in zip(sums[::2], sums[1::2])]
    for i in range(out_ref.shape[0]):
        out_ref[i] = sums[0]


def pack_square(square):
    packed = square[0:8]
    for g in range(1, GROUPS):
        packed += pltpu.roll(square[8 * g : 8 * g + 8], WIDTH * g, 1)
    return packed


def unpack_square(packed):
    lane = iota((8, LANES), 1)
    parts = [packed] + [pltpu.roll(packed, LANES - WIDTH * g, 1) for g in range(1, GROUPS)]
    return jnp.concatenate([jnp.where(lane < WIDTH, part, 0.0) for part in parts], axis=0)


def gram_body(
    rows_ref,
    cols_ref,
    tiles_ref,
    omega_ref,
    rhs_ref,
    blocks_ref,
    y_ref,
    out_ref,
    all_ref,
    cut_ref,
    acc_ref,
):
    for g in range(GROUPS):
        for t in range(TILES):
            y_ref[8 * g : 8 * g + 8, LANES * t : LANES * (t + 1)] = tiles_ref[(g * TILES + t) // SHARE_TILES, t % SHARE_TILES]
    omega = omega_ref[...].astype(F32)
    ysketch = y_ref[...] + regularize * omega
    y_ref[...] = ysketch
    top = ysketch.astype(BF16)
    rest = ysketch - top.astype(F32)
    middle = rest.astype(BF16)
    low = (rest - middle.astype(F32)).astype(BF16)
    cut_ref[0:WIDTH, :] = top
    cut_ref[WIDTH : 2 * WIDTH, :] = middle
    cut_ref[2 * WIDTH : 3 * WIDTH, :] = low
    rhs = rhs_ref[...]
    rhs_top = rhs.astype(BF16).astype(F32)
    rhs_rest = rhs - rhs_top
    rhs_middle = rhs_rest.astype(BF16).astype(F32)
    rhs_low = rhs_rest - rhs_middle
    spot = iota((16, LOCAL), 0)
    rhs_cut = jnp.where(
        spot == 0, rhs_top, jnp.where(spot == 1, rhs_middle, jnp.where(spot == 2, rhs_low, 0.0))
    )
    cut_ref[3 * WIDTH :, :] = rhs_cut.astype(BF16)
    all_ref[0:WIDTH, :] = ysketch
    all_ref[WIDTH : 2 * WIDTH, :] = omega
    all_ref[2 * WIDTH :, :] = jnp.where(iota((LANES - 2 * WIDTH, LOCAL), 0) == 0, rhs, 0.0)

    products = lax.dot_general(
        all_ref[0 : 2 * WIDTH + 8, :], all_ref[...], NT, precision=HIGHEST, preferred_element_type=F32
    )
    lane = iota((WIDTH, LANES), 1)
    upper = products[0:WIDTH]
    middle = products[WIDTH : 2 * WIDTH]
    cross = jnp.where(lane < WIDTH, 0.5 * (middle + pltpu.roll(upper, LANES - WIDTH, 1)), 0.0)
    gram = jnp.where(lane < WIDTH, upper, 0.0) + precond_shift * cross
    out_ref[CORES * IMAGE_TILES] = pack_square(gram)
    out_ref[CORES * IMAGE_TILES + 1] = pack_square(cross)
    out_ref[CORES * IMAGE_TILES + 2] = products[2 * WIDTH :]

    acc_ref[...] = jnp.zeros(acc_ref.shape, F32)
    for n in range(BLOCKS):
        start = pl.multiple_of(rows_ref[n] * ORDER, ORDER)
        acc_ref[cols_ref[n]] += jnp.dot(
            cut_ref[:, pl.ds(start, ORDER)], blocks_ref[n], preferred_element_type=F32
        )
    spot = iota((8, LANES), 0)
    per_block = ORDER // LANES
    for h in range(CORES):
        rhs_tile = jnp.zeros((8, LANES), F32)
        for t in range(HALF_TILES):
            j = h * (HALF_TILES // per_block) + t // per_block
            at = LANES * (t % per_block)
            for g in range(GROUPS):
                out_ref[h * IMAGE_TILES + g * HALF_TILES + t] = acc_ref[
                    j, 8 * g : 8 * g + 8, at : at + LANES
                ] + (
                    acc_ref[j, WIDTH + 8 * g : WIDTH + 8 * g + 8, at : at + LANES]
                    + acc_ref[j, 2 * WIDTH + 8 * g : 2 * WIDTH + 8 * g + 8, at : at + LANES]
                )
            line = jnp.sum(acc_ref[j, 3 * WIDTH :, at : at + LANES], axis=0, keepdims=True)
            rhs_tile = jnp.where(spot == t, line, rhs_tile)
        out_ref[h * IMAGE_TILES + IMAGE_TILES - 1] = rhs_tile


def pair_image_body(core_ref, parts_ref, out_ref):
    first = core_ref[0] * IMAGE_TILES
    for k in range(SENT_TILES):
        at = first + k if k < IMAGE_TILES else (CORES - 1) * IMAGE_TILES + k
        tile = parts_ref[0, at] + parts_ref[1, at]
        for i in range(X_PARTS):
            out_ref[i, k] = tile


def to_column(row, shift):
    lane = iota((WIDTH, LANES), 1)
    return jnp.sum(
        jnp.where(lane == iota((WIDTH, LANES), 0) + shift, row, 0.0), axis=1, keepdims=True
    )


def to_row(column, shift):
    lane = iota((WIDTH, LANES), 1)
    return jnp.sum(
        jnp.where(lane == iota((WIDTH, LANES), 0) + shift, column, 0.0), axis=0, keepdims=True
    )


def eliminate(work, panel):
    spot = iota((WIDTH, LANES), 0)
    for k in range(0, WIDTH, panel):
        rows = [work[k + i : k + i + 1, :] for i in range(panel)]
        columns = [jnp.broadcast_to(work[:, k + i : k + i + 1], work.shape) for i in range(panel)]
        square = [
            [jnp.broadcast_to(rows[i][:, k + j : k + j + 1], (1, LANES)) for j in range(panel)]
            for i in range(panel)
        ]
        update = jnp.zeros(work.shape, F32)
        for i in range(panel):
            reciprocal = 1.0 / square[i][i]
            for j in range(i + 1, panel):
                factor = square[i][j] * reciprocal
                rows[j] = rows[j] - factor * rows[i]
                columns[j] = columns[j] - factor * columns[i]
                for m in range(j, panel):
                    square[j][m] = square[j][m] - factor * square[i][m]
            update += columns[i] * (rows[i] * reciprocal)
        work = jnp.where(spot >= k + panel, work - update, work)
        for i in range(1, panel):
            work = jnp.where(spot == k + i, rows[i], work)
    return work


def solve_gram(inverse, diagonal, row):
    half = jnp.sum(inverse * pltpu.roll(row, WIDTH, 1), axis=1, keepdims=True) / diagonal
    return jnp.sum(inverse * half, axis=0, keepdims=True)


def factor_body(core_ref, parts_ref, theta_ref, out_ref, keep_ref, sum_ref):
    sum_ref[...] = (parts_ref[0] + parts_ref[1]) + (parts_ref[2] + parts_ref[3])
    gram = unpack_square(sum_ref[IMAGE_TILES])
    cross = unpack_square(sum_ref[IMAGE_TILES + 1])
    tail = sum_ref[IMAGE_TILES + 2]
    lane = iota((WIDTH, LANES), 1)
    spot = iota((WIDTH, LANES), 0)
    work = eliminate(jnp.where(lane == spot + WIDTH, 1.0, gram), 4)
    diagonal = jnp.sum(jnp.where(lane == spot, work, 0.0), axis=1, keepdims=True)
    inverse = jnp.where((lane >= WIDTH) & (lane < 2 * WIDTH), work, 0.0)

    sketched_rhs = jnp.where(iota((1, LANES), 1) < WIDTH, tail[0:1], 0.0)
    coeffs = solve_gram(inverse, diagonal, sketched_rhs)
    column = to_column(coeffs, WIDTH)
    crossed = jnp.sum(cross * column, axis=0, keepdims=True)

    row = iota((8, LANES), 0)
    image = sum_ref[IMAGE_TILES - 1]
    for t in range(HALF_TILES):
        part = sum_ref[t] * column[0:8]
        for g in range(1, GROUPS):
            part += sum_ref[g * HALF_TILES + t] * column[8 * g : 8 * g + 8]
        image -= jnp.where(row == t, jnp.sum(part, axis=0, keepdims=True), 0.0)
    scaled = (theta_ref[core_ref[0]] * image).astype(BF16).astype(F32)
    groups = []
    for g in range(GROUPS):
        part = sum_ref[g * HALF_TILES] * scaled[0:1]
        for t in range(1, HALF_TILES):
            part += sum_ref[g * HALF_TILES + t] * scaled[t : t + 1]
        groups.append(jnp.sum(part, axis=1, keepdims=True))
    sketched = to_row(jnp.concatenate(groups, axis=0), 0)
    curvature = jnp.sum(jnp.sum(image * scaled, axis=0, keepdims=True), axis=1, keepdims=True)
    out_ref[0] = scaled
    out_ref[1] = jnp.where(
        row == 0, jnp.where(iota((8, LANES), 1) == WIDTH, curvature, sketched), 0.0
    )
    keep_ref[0:WIDTH, :] = inverse
    keep_ref[WIDTH : 2 * WIDTH, :] = jnp.broadcast_to(diagonal, (WIDTH, LANES))
    keep_ref[2 * WIDTH : 2 * WIDTH + 8, :] = tail
    keep_ref[2 * WIDTH + 8 : 2 * WIDTH + 16, :] = jnp.broadcast_to(coeffs, (8, LANES))
    keep_ref[2 * WIDTH + 16 :, :] = jnp.broadcast_to(crossed, (8, LANES))


def image_body(rows_ref, cols_ref, parts_ref, blocks_ref, out_ref, scaled_ref, acc_ref):
    sums = parts_ref[0, 1, 0:1, :] + parts_ref[1, 1, 0:1, :]
    per_block = ORDER // LANES
    for j in range(LOCAL // ORDER):
        h, first = j // 2, j % 2 * per_block
        line = jnp.concatenate(
            [parts_ref[h, 0, first + q : first + q + 1, :] for q in range(per_block)], axis=1
        )
        scaled_ref[j] = jnp.broadcast_to(line, (16, ORDER)).astype(BF16)
    acc_ref[...] = jnp.zeros(acc_ref.shape, F32)
    for n in range(BLOCKS):
        product = lax.dot_general(
            scaled_ref[cols_ref[n]], blocks_ref[n], NT, preferred_element_type=F32
        )
        acc_ref[rows_ref[n]] += product[0:8]
    lane = iota((8, LANES), 1)
    shares = LANES // WIDTH
    sums = jnp.broadcast_to(pltpu.roll(sums, WIDTH, 1), (8, LANES))
    row = iota((8, LANES), 0)
    for u in range(TILES // 2):
        pack = sums
        for v in range(2):
            t = 2 * u + v
            at = LANES * (t % per_block)
            tile = acc_ref[t // per_block, :, at : at + LANES]
            for q in range(shares):
                turned = tile if q == 0 else pltpu.roll(tile, LANES - WIDTH * q, 1)
                pack = jnp.where((lane < WIDTH) & (row == shares * v + q), turned, pack)
        out_ref[8 * u : 8 * u + 8, :] = pack


def step_body(me_ref, parts_ref, keep_ref, y_ref, rhs_ref, solution_ref, residual_ref, precond_ref):
    total = parts_ref[0:8, :]
    for i in range(1, COL_PARTS // 8):
        total += parts_ref[8 * i : 8 * i + 8, :]
    image_rows = jnp.sum(total, axis=0, keepdims=True)
    sums = pltpu.roll(image_rows, LANES - WIDTH, 1)

    lane = iota((1, LANES), 1)
    first = lane < WIDTH
    inverse = keep_ref[0:WIDTH, :]
    diagonal = keep_ref[WIDTH : 2 * WIDTH, 0:1]
    tail = keep_ref[2 * WIDTH : 2 * WIDTH + 1, :]
    coeffs = keep_ref[2 * WIDTH + 8 : 2 * WIDTH + 9, :]
    crossed = keep_ref[2 * WIDTH + 16 : 2 * WIDTH + 17, :]
    sketched_rhs = jnp.where(first, tail, 0.0)
    square = jnp.sum(jnp.where(lane == 2 * WIDTH, tail, 0.0), axis=1, keepdims=True)
    along = square - jnp.sum(pltpu.roll(sketched_rhs, WIDTH, 1) * coeffs, axis=1, keepdims=True)
    length = along - jnp.sum(pltpu.roll(crossed, WIDTH, 1) * coeffs, axis=1, keepdims=True)
    curvature = jnp.sum(jnp.where(lane == WIDTH, sums, 0.0), axis=1, keepdims=True) + regularize * length
    alpha = along / curvature

    start = pl.multiple_of((me_ref[0] // 4) * LANES, LANES)
    turn = ((4 - me_ref[0] % 4) % 4) * WIDTH
    ysketch = pltpu.roll(y_ref[:, pl.ds(start, LANES)], turn, 1)
    rhs = pltpu.roll(rhs_ref[:, pl.ds(start, LANES)], turn, 1)
    direction = (rhs - jnp.sum(ysketch * to_column(coeffs, WIDTH), axis=0, keepdims=True)) / precond_shift
    image = image_rows + regularize * direction
    residual = rhs - alpha * image
    sketched_image = jnp.where(first, sums, 0.0) + regularize * crossed
    sketched_res = sketched_rhs - alpha * sketched_image
    res_coeffs = solve_gram(inverse, diagonal, sketched_res)
    precond_residual = (
        residual - jnp.sum(ysketch * to_column(res_coeffs, WIDTH), axis=0, keepdims=True)
    ) / precond_shift
    solution_ref[...] = (alpha * direction)[0, :WIDTH]
    residual_ref[...] = residual[0, :WIDTH]
    precond_ref[...] = precond_residual[0, :WIDTH]


def exchange(value, axis):
    return lax.all_to_all(value, axis, 0, 0, tiled=True)


def shards(blocks, block_rows, block_cols, sketch, theta, rhs):
    values = blocks[0, 0]
    rows_idx = block_rows[0, 0]
    cols_idx = block_cols[0, 0]
    omega = sketch.T
    rhs_line = rhs.reshape(1, LOCAL)
    theta_tiles = theta.reshape(CORES, HALF_TILES, LANES)
    my_core = lax.axis_index("core").astype(jnp.int32).reshape(1)
    my_col = lax.axis_index(("y", "far", "near")).astype(jnp.int32).reshape(1)
    shape = jax.ShapeDtypeStruct
    work = 2 * BLOCKS * ORDER * ORDER

    with jax.named_scope("sketch_cols"):
        terms = call(
            sketch_body,
            [smem(), smem(), vmem(), vmem()],
            shape((CORES, WIDTH, HALF), F32),
            flops=work * WIDTH,
            name="sketch_cols",
        )(rows_idx, cols_idx, omega, values)
        parts = lax.all_gather(terms, "core")
        parts = call(
            pair_body, [smem(), vmem()], shape((X_PARTS, WIDTH, HALF), F32), name="pair"
        )(my_core, parts)
        parts = exchange(parts, "x")
    with jax.named_scope("scaled"):
        scaled = call(
            scale_body, [smem(), vmem(), vmem()], shape((WIDTH, HALF), BF16), name="scaled"
        )(my_core, parts, theta_tiles)
        scaled = lax.all_gather(scaled, "core")
    with jax.named_scope("ysketch"):
        terms = call(
            forward_body,
            [smem(), smem(), vmem(), vmem()],
            shape((SHARES, SHARE_TILES, 8, LANES), F32),
            flops=work * WIDTH,
            name="ysketch",
        )(rows_idx, cols_idx, scaled, values)
        share = (SHARE_TILES, 8, LANES)
        parts = exchange(terms, ("y", "near"))
        parts = call(
            spread_body, [vmem()], shape((FAR_PARTS,) + share, F32), name="ysketch_near"
        )(parts)
        parts = exchange(parts, "far")
        parts = call(
            spread_body, [vmem()], shape((SHARES,) + share, F32), name="ysketch_far"
        )(parts)
        tiles = exchange(parts, ("y", "near"))
    with jax.named_scope("gram"):
        ysketch, terms = call(
            gram_body,
            [smem(), smem(), vmem(), vmem(), vmem(), vmem()],
            (shape((WIDTH, LOCAL), F32), shape((CORES * IMAGE_TILES + 3, 8, LANES), F32)),
            scratch=[
                pltpu.VMEM((LANES, LOCAL), F32),
                pltpu.VMEM((3 * WIDTH + 16, LOCAL), BF16),
                pltpu.VMEM((LOCAL // ORDER, 3 * WIDTH + 16, ORDER), F32),
            ],
            flops=work * WIDTH * 3,
            name="gram",
        )(rows_idx, cols_idx, tiles, omega, rhs_line, values)
        parts = lax.all_gather(terms, "core")
        parts = call(
            pair_image_body,
            [smem(), vmem()],
            shape((X_PARTS, SENT_TILES, 8, LANES), F32),
            name="pair_image",
        )(my_core, parts)
        parts = exchange(parts, "x")
    with jax.named_scope("image_scaled"):
        terms, keep = call(
            factor_body,
            [smem(), vmem(), vmem()],
            (shape((2, 8, LANES), F32), shape((2 * WIDTH + 24, LANES), F32)),
            scratch=[pltpu.VMEM((SENT_TILES, 8, LANES), F32)],
            name="image_scaled",
        )(my_core, parts, theta_tiles)
        parts = lax.all_gather(terms, "core")
    with jax.named_scope("image"):
        terms = call(
            image_body,
            [smem(), smem(), vmem(), vmem()],
            shape((COL_PARTS, LANES), F32),
            scratch=[
                pltpu.VMEM((LOCAL // ORDER, 16, ORDER), BF16),
                pltpu.VMEM((LOCAL // ORDER, 8, ORDER), F32),
            ],
            flops=work,
            name="image",
        )(rows_idx, cols_idx, parts, values)
        parts = exchange(terms, ("y", "far", "near"))
    with jax.named_scope("step"):
        share = shape((LOCAL // COL_PARTS,), F32)
        return call(
            step_body,
            [smem(), vmem(), vmem(), vmem(), vmem()],
            (share, share, share),
            name="step",
        )(my_col, parts, keep, ysketch, rhs_line)


def solution(mesh):
    row, col = ("x", "core"), ("y", "far", "near")
    fine = jax.sharding.Mesh(
        mesh.devices.reshape(X_PARTS, CORES, Y_PARTS, FAR_PARTS, NEAR_PARTS),
        ("x", "core", "y", "far", "near"),
    )
    in_specs = (
        P(row, col, None, None, None),
        P(row, col, None),
        P(row, col, None),
        P(row, None),
        P(col),
        P(row),
    )
    out_specs = (P(row + col), P(row + col), P(row + col))
    return jax.shard_map(shards, mesh=fine, in_specs=in_specs, out_specs=out_specs, check_vma=False)
```

```python
import jax
import jax.numpy as jnp
from jax import lax
from jax.experimental import pallas as pl
from jax.experimental.pallas import tpu as pltpu
from jax.sharding import PartitionSpec as P

precond_shift = 1.0
regularize = 0.5

F32 = jnp.float32
BF16 = jnp.bfloat16
HIGHEST = lax.Precision.HIGHEST
LANES = 128
CORES = 2
X_PARTS = 4
Y_PARTS = 4
ROW_PARTS = X_PARTS * CORES
FAR_PARTS = 4
NEAR_PARTS = 4
COL_PARTS = Y_PARTS * FAR_PARTS * NEAR_PARTS
BLOCKS = 8
ORDER = 512
LOCAL = 2048
WIDTH = 32
HALF = LOCAL // CORES
HALF_TILES = HALF // LANES
TILES = LOCAL // LANES
GROUPS = WIDTH // 8
SHARES = Y_PARTS * NEAR_PARTS
SHARE_TILES = GROUPS * TILES // SHARES
VMEM_LIMIT = 24 * 1024 * 1024

NT = (((1,), (1,)), ((), ()))


def vmem():
    return pl.BlockSpec(memory_space=pltpu.VMEM)


def smem():
    return pl.BlockSpec(memory_space=pltpu.SMEM)


def iota(shape, axis):
    return lax.broadcasted_iota(jnp.int32, shape, axis)


def call(body, in_specs, out_shape, scratch=(), flops=0, name=None):
    out_specs = jax.tree.map(lambda _: vmem(), out_shape)
    return pl.pallas_call(
        body,
        in_specs=in_specs,
        out_specs=out_specs,
        out_shape=out_shape,
        scratch_shapes=list(scratch),
        compiler_params=pltpu.CompilerParams(vmem_limit_bytes=VMEM_LIMIT),
        cost_estimate=pl.CostEstimate(flops=flops, bytes_accessed=1 << 20, transcendentals=0),
        name=name,
    )


def sketch_body(rows_ref, cols_ref, omega_ref, blocks_ref, out_ref):
    out_ref[...] = jnp.zeros(out_ref.shape, F32)
    for n in range(BLOCKS):
        start = pl.multiple_of(rows_ref[n] * ORDER, ORDER)
        place = pl.multiple_of(cols_ref[n] % 2 * ORDER, ORDER)
        out_ref[cols_ref[n] // 2, :, pl.ds(place, ORDER)] += jnp.dot(
            omega_ref[:, pl.ds(start, ORDER)], blocks_ref[n], preferred_element_type=F32
        )


def pair_body(core_ref, parts_ref, out_ref):
    half = core_ref[0]
    total = parts_ref[0, half] + parts_ref[1, half]
    for i in range(X_PARTS):
        out_ref[i] = total


def scale_body(core_ref, parts_ref, theta_ref, out_ref):
    total = (parts_ref[0] + parts_ref[1]) + (parts_ref[2] + parts_ref[3])
    tile = theta_ref[core_ref[0]]
    theta = jnp.concatenate([tile[t : t + 1, :] for t in range(HALF_TILES)], axis=1)
    out_ref[...] = (theta * total).astype(BF16)


def forward_body(rows_ref, cols_ref, scaled_ref, blocks_ref, out_ref):
    out_ref[...] = jnp.zeros(out_ref.shape, F32)
    for n in range(BLOCKS):
        place = pl.multiple_of(cols_ref[n] % 2 * ORDER, ORDER)
        left = scaled_ref[cols_ref[n] // 2, :, pl.ds(place, ORDER)]
        product = lax.dot_general(left, blocks_ref[n], NT, preferred_element_type=F32)
        for g in range(GROUPS):
            for q in range(ORDER // LANES):
                out_ref[g * (LOCAL // ORDER) + rows_ref[n], q] += product[8 * g : 8 * g + 8, LANES * q : LANES * (q + 1)]


def spread_body(parts_ref, out_ref):
    sums = [parts_ref[i] for i in range(parts_ref.shape[0])]
    while len(sums) > 1:
        sums = [a + b for a, b in zip(sums[::2], sums[1::2])]
    for i in range(out_ref.shape[0]):
        out_ref[i] = sums[0]


def pack_square(square):
    packed = square[0:8]
    for g in range(1, GROUPS):
        packed += pltpu.roll(square[8 * g : 8 * g + 8], WIDTH * g, 1)
    return packed


def unpack_square(packed):
    lane = iota((8, LANES), 1)
    parts = [packed] + [pltpu.roll(packed, LANES - WIDTH * g, 1) for g in range(1, GROUPS)]
    return jnp.concatenate([jnp.where(lane < WIDTH, part, 0.0) for part in parts], axis=0)


def gram_body(tiles_ref, omega_ref, rhs_ref, y_ref, out_ref, all_ref):
    for g in range(GROUPS):
        for t in range(TILES):
            y_ref[8 * g : 8 * g + 8, LANES * t : LANES * (t + 1)] = tiles_ref[
                (g * TILES + t) // SHARE_TILES, t % SHARE_TILES
            ]
    omega = omega_ref[...].astype(F32)
    ysketch = y_ref[...] + regularize * omega
    y_ref[...] = ysketch
    all_ref[0:WIDTH, :] = ysketch
    all_ref[WIDTH : 2 * WIDTH, :] = omega
    all_ref[2 * WIDTH :, :] = jnp.where(
        iota((LANES - 2 * WIDTH, LOCAL), 0) == 0, rhs_ref[...], 0.0
    )
    products = lax.dot_general(
        all_ref[0 : 2 * WIDTH + 8, :], all_ref[...], NT, precision=HIGHEST, preferred_element_type=F32
    )
    lane = iota((WIDTH, LANES), 1)
    upper = products[0:WIDTH]
    cross = 0.5 * (products[WIDTH : 2 * WIDTH] + pltpu.roll(upper, LANES - WIDTH, 1))
    gram = pack_square(jnp.where(lane < WIDTH, upper + precond_shift * cross, 0.0))
    for i in range(ROW_PARTS):
        out_ref[i, 0] = gram
        out_ref[i, 1] = products[2 * WIDTH :]


def to_column(row, shift):
    lane = iota((WIDTH, LANES), 1)
    return jnp.sum(
        jnp.where(lane == iota((WIDTH, LANES), 0) + shift, row, 0.0), axis=1, keepdims=True
    )


def to_row(column, shift):
    lane = iota((WIDTH, LANES), 1)
    return jnp.sum(
        jnp.where(lane == iota((WIDTH, LANES), 0) + shift, column, 0.0), axis=0, keepdims=True
    )


def eliminate(work, panel):
    spot = iota((WIDTH, LANES), 0)
    for k in range(0, WIDTH, panel):
        rows = [work[k + i : k + i + 1, :] for i in range(panel)]
        columns = [jnp.broadcast_to(work[:, k + i : k + i + 1], work.shape) for i in range(panel)]
        square = [
            [jnp.broadcast_to(rows[i][:, k + j : k + j + 1], (1, LANES)) for j in range(panel)]
            for i in range(panel)
        ]
        update = jnp.zeros(work.shape, F32)
        for i in range(panel):
            reciprocal = 1.0 / square[i][i]
            for j in range(i + 1, panel):
                factor = square[i][j] * reciprocal
                rows[j] = rows[j] - factor * rows[i]
                columns[j] = columns[j] - factor * columns[i]
                for m in range(j, panel):
                    square[j][m] = square[j][m] - factor * square[i][m]
            update += columns[i] * (rows[i] * reciprocal)
        work = jnp.where(spot >= k + panel, work - update, work)
        for i in range(1, panel):
            work = jnp.where(spot == k + i, rows[i], work)
    return work


def solve_gram(inverse, diagonal, row):
    half = jnp.sum(inverse * pltpu.roll(row, WIDTH, 1), axis=1, keepdims=True) / diagonal
    return jnp.sum(inverse * half, axis=0, keepdims=True)


def factor_body(
    rows_ref, cols_ref, parts_ref, y_ref, rhs_ref, blocks_ref, out_ref, keep_ref, direction_ref, low_ref, acc_ref
):
    total = parts_ref[0]
    for i in range(1, ROW_PARTS):
        total += parts_ref[i]
    lane = iota((WIDTH, LANES), 1)
    spot = iota((WIDTH, LANES), 0)
    work = eliminate(jnp.where(lane == spot + WIDTH, 1.0, unpack_square(total[0])), 4)
    diagonal = jnp.sum(jnp.where(lane == spot, work, 0.0), axis=1, keepdims=True)
    inverse = jnp.where((lane >= WIDTH) & (lane < 2 * WIDTH), work, 0.0)
    sketched_rhs = jnp.where(iota((1, LANES), 1) < WIDTH, total[1, 0:1], 0.0)
    coeffs = solve_gram(inverse, diagonal, sketched_rhs)

    ysketch = y_ref[...]
    rhs = rhs_ref[...]
    direction = (
        rhs - jnp.sum(ysketch * to_column(coeffs, WIDTH), axis=0, keepdims=True)
    ) / precond_shift
    direction_ref[...] = direction
    low_ref[...] = jnp.broadcast_to(direction, low_ref.shape).astype(BF16)

    acc_ref[...] = jnp.zeros(acc_ref.shape, F32)
    for n in range(BLOCKS):
        start = pl.multiple_of(rows_ref[n] * ORDER, ORDER)
        product = jnp.dot(
            low_ref[:, pl.ds(start, ORDER)], blocks_ref[n], preferred_element_type=F32
        )
        acc_ref[cols_ref[n]] += product[0:8]
    row = iota((8, LANES), 0)
    per_block = ORDER // LANES
    for h in range(CORES):
        tile = jnp.zeros((8, LANES), F32)
        for t in range(HALF_TILES):
            j = h * (HALF_TILES // per_block) + t // per_block
            at = LANES * (t % per_block)
            tile = jnp.where(row == t, acc_ref[j, :, at : at + LANES], tile)
        for i in range(ROW_PARTS):
            out_ref[i, h] = tile

    sketched = to_row(jnp.sum(ysketch * direction, axis=1, keepdims=True), WIDTH)
    length = jnp.sum(direction * direction, axis=1, keepdims=True)
    along = jnp.sum(rhs * direction, axis=1, keepdims=True)
    line = iota((1, LANES), 1)
    sums = regularize * jnp.where(line == 2 * WIDTH, length, sketched)
    sums = jnp.where(line == 2 * WIDTH + 1, along, sums)
    keep_ref[0:WIDTH, :] = inverse
    keep_ref[WIDTH : 2 * WIDTH, :] = jnp.broadcast_to(diagonal, (WIDTH, LANES))
    keep_ref[2 * WIDTH : 2 * WIDTH + 8, :] = jnp.broadcast_to(sketched_rhs, (8, LANES))
    keep_ref[2 * WIDTH + 8 :, :] = jnp.broadcast_to(sums, (8, LANES))


def image_body(
    rows_ref, cols_ref, parts_ref, theta_ref, y_ref, direction_ref, blocks_ref, out_ref, scaled_ref, acc_ref
):
    total = parts_ref[0]
    for i in range(1, ROW_PARTS):
        total += parts_ref[i]
    scaled = theta_ref[...] * total
    per_block = ORDER // LANES
    for j in range(LOCAL // ORDER):
        h, first = j // 2, j % 2 * per_block
        line = jnp.concatenate(
            [scaled[h, first + q : first + q + 1, :] for q in range(per_block)], axis=1
        )
        scaled_ref[j] = jnp.broadcast_to(line, (16, ORDER)).astype(BF16)
    acc_ref[...] = jnp.zeros(acc_ref.shape, F32)
    for n in range(BLOCKS):
        product = lax.dot_general(
            scaled_ref[cols_ref[n]], blocks_ref[n], NT, preferred_element_type=F32
        )
        acc_ref[rows_ref[n]] += product[0:8]

    whole = jnp.concatenate([acc_ref[r, 0:1, :] for r in range(LOCAL // ORDER)], axis=1)
    sketched = to_row(jnp.sum(y_ref[...] * whole, axis=1, keepdims=True), WIDTH)
    curvature = jnp.sum(direction_ref[...] * whole, axis=1, keepdims=True)
    sums = jnp.where(iota((1, LANES), 1) == 2 * WIDTH, curvature, sketched)
    sums = jnp.broadcast_to(sums, (8, LANES))
    lane = iota((8, LANES), 1)
    row = iota((8, LANES), 0)
    shares = LANES // WIDTH
    for u in range(TILES // 2):
        pack = sums
        for v in range(2):
            t = 2 * u + v
            at = LANES * (t % per_block)
            tile = acc_ref[t // per_block, :, at : at + LANES]
            for q in range(shares):
                turned = tile if q == 0 else pltpu.roll(tile, LANES - WIDTH * q, 1)
                pack = jnp.where((lane < WIDTH) & (row == shares * v + q), turned, pack)
        out_ref[8 * u : 8 * u + 8, :] = pack


def sums_body(parts_ref, keep_ref, out_ref):
    total = parts_ref[0:8, :]
    for i in range(1, COL_PARTS // 8):
        total += parts_ref[8 * i : 8 * i + 8, :]
    line = jnp.sum(total, axis=0, keepdims=True)
    out_ref[...] = jnp.broadcast_to(line + keep_ref[2 * WIDTH + 8 : 2 * WIDTH + 9, :], (8, LANES))


def step_body(
    me_ref, mine_ref, parts_ref, keep_ref, y_ref, rhs_ref, direction_ref, solution_ref, residual_ref, precond_ref
):
    sums = jnp.sum(parts_ref[...], axis=0, keepdims=True)
    lane = iota((1, LANES), 1)
    inverse = keep_ref[0:WIDTH, :]
    diagonal = keep_ref[WIDTH : 2 * WIDTH, 0:1]
    sketched_rhs = keep_ref[2 * WIDTH : 2 * WIDTH + 1, :]
    curvature = jnp.sum(jnp.where(lane == 2 * WIDTH, sums, 0.0), axis=1, keepdims=True)
    along = jnp.sum(jnp.where(lane == 2 * WIDTH + 1, sums, 0.0), axis=1, keepdims=True)
    alpha = along / curvature

    start = pl.multiple_of((me_ref[0] // 4) * LANES, LANES)
    turn = ((4 - me_ref[0] % 4) % 4) * WIDTH
    ysketch = pltpu.roll(y_ref[:, pl.ds(start, LANES)], turn, 1)
    rhs = pltpu.roll(rhs_ref[:, pl.ds(start, LANES)], turn, 1)
    direction = pltpu.roll(direction_ref[:, pl.ds(start, LANES)], turn, 1)
    image = mine_ref[0:1, :] + regularize * direction
    residual = rhs - alpha * image
    sketched_image = jnp.where(lane < WIDTH, pltpu.roll(sums, LANES - WIDTH, 1), 0.0)
    res_coeffs = solve_gram(inverse, diagonal, sketched_rhs - alpha * sketched_image)
    precond_residual = (
        residual - jnp.sum(ysketch * to_column(res_coeffs, WIDTH), axis=0, keepdims=True)
    ) / precond_shift
    solution_ref[...] = (alpha * direction)[0, :WIDTH]
    residual_ref[...] = residual[0, :WIDTH]
    precond_ref[...] = precond_residual[0, :WIDTH]


def exchange(value, axis):
    return lax.all_to_all(value, axis, 0, 0, tiled=True)


def shards(blocks, block_rows, block_cols, sketch, theta, rhs):
    values = blocks[0, 0]
    rows_idx = block_rows[0, 0]
    cols_idx = block_cols[0, 0]
    omega = sketch.T
    rhs_line = rhs.reshape(1, LOCAL)
    theta_tiles = theta.reshape(CORES, HALF_TILES, LANES)
    my_core = lax.axis_index("core").astype(jnp.int32).reshape(1)
    my_col = lax.axis_index(("y", "far", "near")).astype(jnp.int32).reshape(1)
    shape = jax.ShapeDtypeStruct
    work = 2 * BLOCKS * ORDER * ORDER

    with jax.named_scope("sketch_cols"):
        terms = call(
            sketch_body,
            [smem(), smem(), vmem(), vmem()],
            shape((CORES, WIDTH, HALF), F32),
            flops=work * WIDTH,
            name="sketch_cols",
        )(rows_idx, cols_idx, omega, values)
        parts = lax.all_gather(terms, "core")
        parts = call(
            pair_body, [smem(), vmem()], shape((X_PARTS, WIDTH, HALF), F32), name="pair"
        )(my_core, parts)
        parts = exchange(parts, "x")
    with jax.named_scope("scaled"):
        scaled = call(
            scale_body, [smem(), vmem(), vmem()], shape((WIDTH, HALF), BF16), name="scaled"
        )(my_core, parts, theta_tiles)
        scaled = lax.all_gather(scaled, "core")
    with jax.named_scope("ysketch"):
        terms = call(
            forward_body,
            [smem(), smem(), vmem(), vmem()],
            shape((SHARES, SHARE_TILES, 8, LANES), F32),
            flops=work * WIDTH,
            name="ysketch",
        )(rows_idx, cols_idx, scaled, values)
        share = (SHARE_TILES, 8, LANES)
        parts = exchange(terms, ("y", "near"))
        parts = call(
            spread_body, [vmem()], shape((FAR_PARTS,) + share, F32), name="ysketch_near"
        )(parts)
        parts = exchange(parts, "far")
        parts = call(
            spread_body, [vmem()], shape((SHARES,) + share, F32), name="ysketch_far"
        )(parts)
        tiles = exchange(parts, ("y", "near"))
    with jax.named_scope("gram"):
        ysketch, terms = call(
            gram_body,
            [vmem(), vmem(), vmem()],
            (shape((WIDTH, LOCAL), F32), shape((ROW_PARTS, 2, 8, LANES), F32)),
            scratch=[pltpu.VMEM((LANES, LOCAL), F32)],
            name="gram",
        )(tiles, omega, rhs_line)
        parts = exchange(terms, ("x", "core"))
    with jax.named_scope("direction"):
        terms, keep, direction = call(
            factor_body,
            [smem(), smem(), vmem(), vmem(), vmem(), vmem()],
            (
                shape((ROW_PARTS, CORES, HALF_TILES, LANES), F32),
                shape((2 * WIDTH + 16, LANES), F32),
                shape((1, LOCAL), F32),
            ),
            scratch=[
                pltpu.VMEM((16, LOCAL), BF16),
                pltpu.VMEM((LOCAL // ORDER, 8, ORDER), F32),
            ],
            flops=work,
            name="direction",
        )(rows_idx, cols_idx, parts, ysketch, rhs_line, values)
        parts = exchange(terms, ("x", "core"))
    with jax.named_scope("image"):
        terms = call(
            image_body,
            [smem(), smem(), vmem(), vmem(), vmem(), vmem(), vmem()],
            shape((COL_PARTS, LANES), F32),
            scratch=[
                pltpu.VMEM((LOCAL // ORDER, 16, ORDER), BF16),
                pltpu.VMEM((LOCAL // ORDER, 8, ORDER), F32),
            ],
            flops=work,
            name="image",
        )(rows_idx, cols_idx, parts, theta_tiles, ysketch, direction, values)
        parts = exchange(terms, ("y", "far", "near"))
        terms = call(sums_body, [vmem(), vmem()], shape((ROW_PARTS, LANES), F32), name="sums")(
            parts, keep
        )
        parts = exchange(terms, ("x", "core"))
    with jax.named_scope("step"):
        share = shape((LOCAL // COL_PARTS,), F32)
        return call(
            step_body,
            [smem(), vmem(), vmem(), vmem(), vmem(), vmem(), vmem()],
            (share, share, share),
            name="step",
        )(my_col, terms, parts, keep, ysketch, rhs_line, direction)


def solution(mesh):
    row, col = ("x", "core"), ("y", "far", "near")
    fine = jax.sharding.Mesh(
        mesh.devices.reshape(X_PARTS, CORES, Y_PARTS, FAR_PARTS, NEAR_PARTS),
        ("x", "core", "y", "far", "near"),
    )
    in_specs = (
        P(row, col, None, None, None),
        P(row, col, None),
        P(row, col, None),
        P(row, None),
        P(col),
        P(row),
    )
    out_specs = (P(row + col), P(row + col), P(row + col))
    return jax.shard_map(shards, mesh=fine, in_specs=in_specs, out_specs=out_specs, check_vma=False)
```

```python
import jax
import jax.numpy as jnp
from jax import lax
from jax.experimental import pallas as pl
from jax.experimental.pallas import tpu as pltpu
from jax.sharding import PartitionSpec as P

precond_shift = 1.0
regularize = 0.5

F32 = jnp.float32
BF16 = jnp.bfloat16
I16 = jnp.int16
HIGHEST = lax.Precision.HIGHEST
LANES = 128
CORES = 2
X_PARTS = 4
Y_PARTS = 4
ROW_PARTS = X_PARTS * CORES
FAR_PARTS = 4
NEAR_PARTS = 4
COL_PARTS = Y_PARTS * FAR_PARTS * NEAR_PARTS
BLOCKS = 8
ORDER = 512
LOCAL = 2048
WIDTH = 32
TINY = 2.0**-100
HALF = LOCAL // CORES
HALF_TILES = HALF // LANES
TILES = LOCAL // LANES
GROUPS = WIDTH // 8
SHARES = Y_PARTS * NEAR_PARTS
SHARE_TILES = GROUPS * TILES // SHARES
VMEM_LIMIT = 24 * 1024 * 1024

NT = (((1,), (1,)), ((), ()))


def vmem():
    return pl.BlockSpec(memory_space=pltpu.VMEM)


def smem():
    return pl.BlockSpec(memory_space=pltpu.SMEM)


def iota(shape, axis):
    return lax.broadcasted_iota(jnp.int32, shape, axis)


def call(body, in_specs, out_shape, scratch=(), flops=0, name=None):
    out_specs = jax.tree.map(lambda _: vmem(), out_shape)
    return pl.pallas_call(
        body,
        in_specs=in_specs,
        out_specs=out_specs,
        out_shape=out_shape,
        scratch_shapes=list(scratch),
        compiler_params=pltpu.CompilerParams(vmem_limit_bytes=VMEM_LIMIT),
        cost_estimate=pl.CostEstimate(flops=flops, bytes_accessed=1 << 20, transcendentals=0),
        name=name,
    )


def sketch_body(places_ref, omega_ref, blocks_ref, out_ref):
    out_ref[...] = jnp.zeros(out_ref.shape, F32)
    for n in range(BLOCKS):
        start = pl.multiple_of(places_ref[n] * ORDER, ORDER)
        place = pl.multiple_of(places_ref[BLOCKS + n] % 2 * ORDER, ORDER)
        out_ref[places_ref[BLOCKS + n] // 2, :, pl.ds(place, ORDER)] += jnp.dot(
            omega_ref[:, pl.ds(start, ORDER)], blocks_ref[n], preferred_element_type=F32
        )


def scale_of(mantissa, power):
    return mantissa * jnp.exp2(power - 14.0)


def pair_body(core_ref, parts_ref, out_ref):
    half = core_ref[0]
    total = parts_ref[0, half] + parts_ref[1, half]
    largest = jnp.maximum(jnp.max(jnp.abs(total), axis=1, keepdims=True), TINY)
    power = jnp.ceil(jnp.log2(largest))
    mantissa = jnp.ceil(largest * jnp.exp2(14.0 - power))
    coded = jnp.round(total * (32000.0 / scale_of(mantissa, power))).astype(jnp.int32).astype(I16)
    unit = jnp.where(iota((WIDTH, LANES), 1) == 0, power, mantissa).astype(jnp.int32).astype(I16)
    for i in range(X_PARTS):
        out_ref[i, :, :HALF] = coded
        out_ref[i, :, HALF:] = unit


def scale_body(core_ref, parts_ref, theta_ref, out_ref):
    total = jnp.zeros(out_ref.shape, F32)
    for i in range(X_PARTS):
        unit = parts_ref[i, :, HALF:].astype(jnp.int32).astype(F32)
        coded = parts_ref[i, :, :HALF].astype(jnp.int32).astype(F32)
        total += coded * (scale_of(unit[:, 1:2], unit[:, 0:1]) / 32000.0)
    tile = theta_ref[core_ref[0]]
    theta = jnp.concatenate([tile[t : t + 1, :] for t in range(HALF_TILES)], axis=1)
    out_ref[...] = (theta * total).astype(BF16)


def forward_body(places_ref, scaled_ref, blocks_ref, out_ref):
    out_ref[...] = jnp.zeros(out_ref.shape, F32)
    for n in range(BLOCKS):
        place = pl.multiple_of(places_ref[BLOCKS + n] % 2 * ORDER, ORDER)
        left = scaled_ref[places_ref[BLOCKS + n] // 2, :, pl.ds(place, ORDER)]
        product = lax.dot_general(left, blocks_ref[n], NT, preferred_element_type=F32)
        for g in range(GROUPS):
            for q in range(ORDER // LANES):
                out_ref[g * (LOCAL // ORDER) + places_ref[n], q] += product[8 * g : 8 * g + 8, LANES * q : LANES * (q + 1)]


def spread_body(parts_ref, out_ref):
    sums = [parts_ref[i] for i in range(parts_ref.shape[0])]
    while len(sums) > 1:
        sums = [a + b for a, b in zip(sums[::2], sums[1::2])]
    for i in range(out_ref.shape[0]):
        out_ref[i] = sums[0]


def pack_square(square):
    packed = square[0:8]
    for g in range(1, GROUPS):
        packed += pltpu.roll(square[8 * g : 8 * g + 8], WIDTH * g, 1)
    return packed


def unpack_square(packed):
    lane = iota((8, LANES), 1)
    parts = [packed] + [pltpu.roll(packed, LANES - WIDTH * g, 1) for g in range(1, GROUPS)]
    return jnp.concatenate([jnp.where(lane < WIDTH, part, 0.0) for part in parts], axis=0)


def gram_body(tiles_ref, omega_ref, rhs_ref, y_ref, out_ref, all_ref):
    for g in range(GROUPS):
        for t in range(TILES):
            y_ref[8 * g : 8 * g + 8, LANES * t : LANES * (t + 1)] = tiles_ref[
                (g * TILES + t) // SHARE_TILES, t % SHARE_TILES
            ]
    omega = omega_ref[...].astype(F32)
    ysketch = y_ref[...] + regularize * omega
    y_ref[...] = ysketch
    all_ref[0:WIDTH, :] = ysketch
    all_ref[WIDTH : 2 * WIDTH, :] = omega
    all_ref[2 * WIDTH :, :] = jnp.where(
        iota((LANES - 2 * WIDTH, LOCAL), 0) == 0, rhs_ref[...], 0.0
    )
    products = lax.dot_general(
        all_ref[0 : 2 * WIDTH + 8, :], all_ref[...], NT, precision=HIGHEST, preferred_element_type=F32
    )
    lane = iota((WIDTH, LANES), 1)
    upper = products[0:WIDTH]
    cross = 0.5 * (products[WIDTH : 2 * WIDTH] + pltpu.roll(upper, LANES - WIDTH, 1))
    gram = pack_square(jnp.where(lane < WIDTH, upper + precond_shift * cross, 0.0))
    for i in range(ROW_PARTS):
        out_ref[i, 0] = gram
        out_ref[i, 1] = products[2 * WIDTH :]


def to_column(row, shift):
    lane = iota((WIDTH, LANES), 1)
    return jnp.sum(
        jnp.where(lane == iota((WIDTH, LANES), 0) + shift, row, 0.0), axis=1, keepdims=True
    )


def to_row(column, shift):
    lane = iota((WIDTH, LANES), 1)
    return jnp.sum(
        jnp.where(lane == iota((WIDTH, LANES), 0) + shift, column, 0.0), axis=0, keepdims=True
    )


def eliminate(work, panel):
    spot = iota((WIDTH, LANES), 0)
    for k in range(0, WIDTH, panel):
        rows = [work[k + i : k + i + 1, :] for i in range(panel)]
        columns = [jnp.broadcast_to(work[:, k + i : k + i + 1], work.shape) for i in range(panel)]
        square = [
            [jnp.broadcast_to(rows[i][:, k + j : k + j + 1], (1, LANES)) for j in range(panel)]
            for i in range(panel)
        ]
        update = jnp.zeros(work.shape, F32)
        for i in range(panel):
            reciprocal = 1.0 / square[i][i]
            for j in range(i + 1, panel):
                factor = square[i][j] * reciprocal
                rows[j] = rows[j] - factor * rows[i]
                columns[j] = columns[j] - factor * columns[i]
                for m in range(j, panel):
                    square[j][m] = square[j][m] - factor * square[i][m]
            update += columns[i] * (rows[i] * reciprocal)
        work = jnp.where(spot >= k + panel, work - update, work)
        for i in range(1, panel):
            work = jnp.where(spot == k + i, rows[i], work)
    return work


def solve_gram(inverse, diagonal, row):
    half = jnp.sum(inverse * pltpu.roll(row, WIDTH, 1), axis=1, keepdims=True) / diagonal
    return jnp.sum(inverse * half, axis=0, keepdims=True)


def factor_body(
    places_ref, parts_ref, y_ref, rhs_ref, blocks_ref, out_ref, keep_ref, direction_ref, low_ref, acc_ref
):
    total = parts_ref[0]
    for i in range(1, ROW_PARTS):
        total += parts_ref[i]
    lane = iota((WIDTH, LANES), 1)
    spot = iota((WIDTH, LANES), 0)
    work = eliminate(jnp.where(lane == spot + WIDTH, 1.0, unpack_square(total[0])), 4)
    diagonal = jnp.sum(jnp.where(lane == spot, work, 0.0), axis=1, keepdims=True)
    inverse = jnp.where((lane >= WIDTH) & (lane < 2 * WIDTH), work, 0.0)
    sketched_rhs = jnp.where(iota((1, LANES), 1) < WIDTH, total[1, 0:1], 0.0)
    coeffs = solve_gram(inverse, diagonal, sketched_rhs)

    ysketch = y_ref[...]
    rhs = rhs_ref[...]
    direction = (
        rhs - jnp.sum(ysketch * to_column(coeffs, WIDTH), axis=0, keepdims=True)
    ) / precond_shift
    direction_ref[...] = direction
    low_ref[...] = jnp.broadcast_to(direction, low_ref.shape).astype(BF16)

    acc_ref[...] = jnp.zeros(acc_ref.shape, F32)
    for n in range(BLOCKS):
        start = pl.multiple_of(places_ref[n] * ORDER, ORDER)
        product = jnp.dot(
            low_ref[:, pl.ds(start, ORDER)], blocks_ref[n], preferred_element_type=F32
        )
        acc_ref[places_ref[BLOCKS + n]] += product[0:8]
    row = iota((8, LANES), 0)
    per_block = ORDER // LANES
    for h in range(CORES):
        tile = jnp.zeros((8, LANES), F32)
        for t in range(HALF_TILES):
            j = h * (HALF_TILES // per_block) + t // per_block
            at = LANES * (t % per_block)
            tile = jnp.where(row == t, acc_ref[j, :, at : at + LANES], tile)
        for i in range(ROW_PARTS):
            out_ref[i, h] = tile

    sketched = to_row(jnp.sum(ysketch * direction, axis=1, keepdims=True), 3 * WIDTH)
    length = jnp.sum(direction * direction, axis=1, keepdims=True)
    along = jnp.sum(rhs * direction, axis=1, keepdims=True)
    line = iota((1, LANES), 1)
    sums = jnp.where(line == 2 * WIDTH + 1, length, sketched)
    sums = jnp.where(line == 2 * WIDTH + 2, along, sums)
    keep_ref[0:WIDTH, :] = inverse
    keep_ref[WIDTH : 2 * WIDTH, :] = jnp.broadcast_to(diagonal, (WIDTH, LANES))
    keep_ref[2 * WIDTH : 2 * WIDTH + 8, :] = jnp.broadcast_to(sketched_rhs, (8, LANES))
    keep_ref[2 * WIDTH + 8 :, :] = jnp.broadcast_to(sums, (8, LANES))


def image_body(
    places_ref,
    parts_ref,
    theta_ref,
    y_ref,
    direction_ref,
    keep_ref,
    blocks_ref,
    out_ref,
    sums_ref,
    scaled_ref,
    acc_ref,
):
    total = parts_ref[0]
    for i in range(1, ROW_PARTS):
        total += parts_ref[i]
    scaled = theta_ref[...] * total
    per_block = ORDER // LANES
    for j in range(LOCAL // ORDER):
        h, first = j // 2, j % 2 * per_block
        line = jnp.concatenate(
            [scaled[h, first + q : first + q + 1, :] for q in range(per_block)], axis=1
        )
        scaled_ref[j] = jnp.broadcast_to(line, (16, ORDER)).astype(BF16)
    acc_ref[...] = jnp.zeros(acc_ref.shape, F32)
    for n in range(BLOCKS):
        product = lax.dot_general(
            scaled_ref[places_ref[BLOCKS + n]], blocks_ref[n], NT, preferred_element_type=F32
        )
        acc_ref[places_ref[n]] += product[0:8]

    whole = jnp.concatenate([acc_ref[r, 0:1, :] for r in range(LOCAL // ORDER)], axis=1)
    sketched = to_row(jnp.sum(y_ref[...] * whole, axis=1, keepdims=True), WIDTH)
    curvature = jnp.sum(direction_ref[...] * whole, axis=1, keepdims=True)
    sums = jnp.where(iota((1, LANES), 1) == 2 * WIDTH, curvature, sketched)
    sums += keep_ref[2 * WIDTH + 8 : 2 * WIDTH + 9, :]
    sums_ref[...] = jnp.broadcast_to(sums, sums_ref.shape)
    row = iota((8, LANES), 0)
    for h in range(CORES):
        tile = jnp.zeros((8, LANES), F32)
        for t in range(HALF_TILES):
            r, at = (h * HALF_TILES + t) // per_block, LANES * (t % per_block)
            tile = jnp.where(row == t, acc_ref[r, :, at : at + LANES], tile)
        out_ref[h] = tile


def lines_body(image_ref, parts_ref, out_ref, sums_ref):
    sums = jnp.sum(parts_ref[...], axis=0, keepdims=True)
    sums_ref[...] = jnp.broadcast_to(sums, sums_ref.shape)
    lane = iota((8, LANES), 1)
    row = iota((8, LANES), 0)
    shares = LANES // WIDTH
    added = jnp.broadcast_to(
        jnp.where(iota((1, LANES), 1) <= 2 * WIDTH, sums, 0.0), (8, LANES)
    )
    for u in range(TILES // 2):
        pack = added
        for v in range(2):
            t = 2 * u + v
            line = image_ref[t // HALF_TILES, t % HALF_TILES : t % HALF_TILES + 1, :]
            for q in range(shares):
                turned = line if q == 0 else pltpu.roll(line, LANES - WIDTH * q, 1)
                pack = jnp.where((lane < WIDTH) & (row == shares * v + q), turned, pack)
        out_ref[8 * u : 8 * u + 8, :] = pack


def step_body(
    me_ref,
    parts_ref,
    sums_ref,
    keep_ref,
    y_ref,
    rhs_ref,
    direction_ref,
    solution_ref,
    residual_ref,
    precond_ref,
):
    total = parts_ref[0:8, :]
    for i in range(1, COL_PARTS // 8):
        total += parts_ref[8 * i : 8 * i + 8, :]
    total = jnp.sum(total, axis=0, keepdims=True)
    sums = sums_ref[0:1, :]
    lane = iota((1, LANES), 1)
    inverse = keep_ref[0:WIDTH, :]
    diagonal = keep_ref[WIDTH : 2 * WIDTH, 0:1]
    sketched_rhs = keep_ref[2 * WIDTH : 2 * WIDTH + 1, :]

    def pick(line, at):
        return jnp.sum(jnp.where(lane == at, line, 0.0), axis=1, keepdims=True)

    along = pick(sums, 2 * WIDTH + 2)
    curvature = pick(total, 2 * WIDTH) + regularize * pick(sums, 2 * WIDTH + 1)
    alpha = along / curvature

    start = pl.multiple_of((me_ref[0] // 4) * LANES, LANES)
    turn = ((4 - me_ref[0] % 4) % 4) * WIDTH
    ysketch = pltpu.roll(y_ref[:, pl.ds(start, LANES)], turn, 1)
    rhs = pltpu.roll(rhs_ref[:, pl.ds(start, LANES)], turn, 1)
    direction = pltpu.roll(direction_ref[:, pl.ds(start, LANES)], turn, 1)
    image = total + regularize * direction
    residual = rhs - alpha * image
    sketched_image = pltpu.roll(total, LANES - WIDTH, 1) + regularize * pltpu.roll(sums, WIDTH, 1)
    sketched_image = jnp.where(lane < WIDTH, sketched_image, 0.0)
    res_coeffs = solve_gram(inverse, diagonal, sketched_rhs - alpha * sketched_image)
    precond_residual = (
        residual - jnp.sum(ysketch * to_column(res_coeffs, WIDTH), axis=0, keepdims=True)
    ) / precond_shift
    solution_ref[...] = (alpha * direction)[0, :WIDTH]
    residual_ref[...] = residual[0, :WIDTH]
    precond_ref[...] = precond_residual[0, :WIDTH]


def exchange(value, axis):
    return lax.all_to_all(value, axis, 0, 0, tiled=True)


def shards(blocks, block_rows, block_cols, sketch, theta, rhs):
    values = blocks[0, 0]
    places = jnp.concatenate([block_rows[0, 0], block_cols[0, 0]])
    omega = sketch.T
    rhs_line = rhs.reshape(1, LOCAL)
    theta_tiles = theta.reshape(CORES, HALF_TILES, LANES)
    my_core = lax.axis_index("core").astype(jnp.int32).reshape(1)
    my_col = lax.axis_index(("y", "far", "near")).astype(jnp.int32).reshape(1)
    shape = jax.ShapeDtypeStruct
    work = 2 * BLOCKS * ORDER * ORDER

    with jax.named_scope("sketch_cols"):
        terms = call(
            sketch_body,
            [smem(), vmem(), vmem()],
            shape((CORES, WIDTH, HALF), F32),
            flops=work * WIDTH,
            name="sketch_cols",
        )(places, omega, values)
        parts = lax.all_gather(terms, "core")
        parts = call(
            pair_body, [smem(), vmem()], shape((X_PARTS, WIDTH, HALF + LANES), I16), name="pair"
        )(my_core, parts)
        parts = exchange(parts, "x")
    with jax.named_scope("scaled"):
        scaled = call(
            scale_body, [smem(), vmem(), vmem()], shape((WIDTH, HALF), BF16), name="scaled"
        )(my_core, parts, theta_tiles)
        scaled = lax.all_gather(scaled, "core")
    with jax.named_scope("ysketch"):
        terms = call(
            forward_body,
            [smem(), vmem(), vmem()],
            shape((SHARES, SHARE_TILES, 8, LANES), F32),
            flops=work * WIDTH,
            name="ysketch",
        )(places, scaled, values)
        share = (SHARE_TILES, 8, LANES)
        parts = exchange(terms, ("y", "near"))
        parts = call(
            spread_body, [vmem()], shape((FAR_PARTS,) + share, F32), name="ysketch_near"
        )(parts)
        parts = exchange(parts, "far")
        parts = call(
            spread_body, [vmem()], shape((SHARES,) + share, F32), name="ysketch_far"
        )(parts)
        tiles = exchange(parts, ("y", "near"))
    with jax.named_scope("gram"):
        ysketch, terms = call(
            gram_body,
            [vmem(), vmem(), vmem()],
            (shape((WIDTH, LOCAL), F32), shape((ROW_PARTS, 2, 8, LANES), F32)),
            scratch=[pltpu.VMEM((LANES, LOCAL), F32)],
            name="gram",
        )(tiles, omega, rhs_line)
        parts = exchange(terms, ("x", "core"))
    with jax.named_scope("direction"):
        terms, keep, direction = call(
            factor_body,
            [smem(), vmem(), vmem(), vmem(), vmem()],
            (
                shape((ROW_PARTS, CORES, HALF_TILES, LANES), F32),
                shape((2 * WIDTH + 16, LANES), F32),
                shape((1, LOCAL), F32),
            ),
            scratch=[
                pltpu.VMEM((16, LOCAL), BF16),
                pltpu.VMEM((LOCAL // ORDER, 8, ORDER), F32),
            ],
            flops=work,
            name="direction",
        )(places, parts, ysketch, rhs_line, values)
        parts = exchange(terms, ("x", "core"))
    with jax.named_scope("image"):
        image, terms = call(
            image_body,
            [smem()] + [vmem()] * 6,
            (shape((CORES, HALF_TILES, LANES), F32), shape((ROW_PARTS, LANES), F32)),
            scratch=[
                pltpu.VMEM((LOCAL // ORDER, 16, ORDER), BF16),
                pltpu.VMEM((LOCAL // ORDER, 8, ORDER), F32),
            ],
            flops=work,
            name="image",
        )(places, parts, theta_tiles, ysketch, direction, keep, values)
        parts = exchange(terms, ("x", "core"))
        terms, sums = call(
            lines_body,
            [vmem(), vmem()],
            (shape((COL_PARTS, LANES), F32), shape((8, LANES), F32)),
            name="lines",
        )(image, parts)
        parts = exchange(terms, ("y", "far", "near"))
    with jax.named_scope("step"):
        share = shape((LOCAL // COL_PARTS,), F32)
        return call(
            step_body,
            [smem(), vmem(), vmem(), vmem(), vmem(), vmem(), vmem()],
            (share, share, share),
            name="step",
        )(my_col, parts, sums, keep, ysketch, rhs_line, direction)


def solution(mesh):
    row, col = ("x", "core"), ("y", "far", "near")
    fine = jax.sharding.Mesh(
        mesh.devices.reshape(X_PARTS, CORES, Y_PARTS, FAR_PARTS, NEAR_PARTS),
        ("x", "core", "y", "far", "near"),
    )
    in_specs = (
        P(row, col, None, None, None),
        P(row, col, None),
        P(row, col, None),
        P(row, None),
        P(col),
        P(row),
    )
    out_specs = (P(row + col), P(row + col), P(row + col))
    return jax.shard_map(shards, mesh=fine, in_specs=in_specs, out_specs=out_specs, check_vma=False)
```

```python
import jax
import jax.numpy as jnp
from jax import lax
from jax.experimental import pallas as pl
from jax.experimental.pallas import tpu as pltpu
from jax.sharding import PartitionSpec as P

precond_shift = 1.0
regularize = 0.5

F32 = jnp.float32
BF16 = jnp.bfloat16
I16 = jnp.int16
HIGHEST = lax.Precision.HIGHEST
LANES = 128
CORES = 2
X_PARTS = 4
Y_PARTS = 4
ROW_PARTS = X_PARTS * CORES
FAR_PARTS = 4
NEAR_PARTS = 4
COL_PARTS = Y_PARTS * FAR_PARTS * NEAR_PARTS
BLOCKS = 8
ORDER = 512
LOCAL = 2048
WIDTH = 32
TINY = 2.0**-100
HALF = LOCAL // CORES
HALF_TILES = HALF // LANES
TILES = LOCAL // LANES
GROUPS = WIDTH // 8
SHARES = Y_PARTS * NEAR_PARTS
SHARE_TILES = GROUPS * TILES // SHARES
VMEM_LIMIT = 24 * 1024 * 1024

NT = (((1,), (1,)), ((), ()))


def vmem():
    return pl.BlockSpec(memory_space=pltpu.VMEM)


def smem():
    return pl.BlockSpec(memory_space=pltpu.SMEM)


def iota(shape, axis):
    return lax.broadcasted_iota(jnp.int32, shape, axis)


def call(body, in_specs, out_shape, scratch=(), flops=0, name=None):
    out_specs = jax.tree.map(lambda _: vmem(), out_shape)
    return pl.pallas_call(
        body,
        in_specs=in_specs,
        out_specs=out_specs,
        out_shape=out_shape,
        scratch_shapes=list(scratch),
        compiler_params=pltpu.CompilerParams(vmem_limit_bytes=VMEM_LIMIT),
        cost_estimate=pl.CostEstimate(flops=flops, bytes_accessed=1 << 20, transcendentals=0),
        name=name,
    )


def sketch_body(me_ref, places_ref, omega_ref, blocks_ref, out_ref):
    del me_ref
    out_ref[...] = jnp.zeros(out_ref.shape, F32)
    for n in range(BLOCKS):
        start = pl.multiple_of(places_ref[n] * ORDER, ORDER)
        place = pl.multiple_of(places_ref[BLOCKS + n] % 2 * ORDER, ORDER)
        out_ref[places_ref[BLOCKS + n] // 2, :, pl.ds(place, ORDER)] += jnp.dot(
            omega_ref[:, pl.ds(start, ORDER)], blocks_ref[n], preferred_element_type=F32
        )


def scale_of(mantissa, power):
    return mantissa * jnp.exp2(power - 14.0)


def unit_of(largest):
    largest = jnp.maximum(largest, TINY)
    power = jnp.ceil(jnp.log2(largest))
    return power, jnp.ceil(largest * jnp.exp2(14.0 - power))


def encode(tiles, power, mantissa):
    factor = 32000.0 / scale_of(mantissa, power)
    unit = jnp.where(iota((8, LANES), 1) == 0, power, mantissa)
    rows = jnp.concatenate([tile * factor for tile in tiles] + [unit], axis=0)
    return jnp.round(rows).astype(jnp.int32).astype(I16)


def decode(coded):
    rows = coded.astype(jnp.int32).astype(F32)
    unit = rows[8 * SHARE_TILES :]
    factor = scale_of(unit[:, 1:2], unit[:, 0:1]) / 32000.0
    return [rows[8 * q : 8 * q + 8] * factor for q in range(SHARE_TILES)]


def pair_body(me_ref, parts_ref, out_ref):
    half = lax.rem(me_ref[0], CORES)
    total = parts_ref[0, half] + parts_ref[1, half]
    power, mantissa = unit_of(jnp.max(jnp.abs(total), axis=1, keepdims=True))
    coded = jnp.round(total * (32000.0 / scale_of(mantissa, power))).astype(jnp.int32).astype(I16)
    unit = jnp.where(iota((WIDTH, LANES), 1) == 0, power, mantissa).astype(jnp.int32).astype(I16)
    for i in range(X_PARTS):
        out_ref[i, :, :HALF] = coded
        out_ref[i, :, HALF:] = unit


def scale_body(me_ref, parts_ref, theta_ref, out_ref):
    total = jnp.zeros(out_ref.shape, F32)
    for i in range(X_PARTS):
        unit = parts_ref[i, :, HALF:].astype(jnp.int32).astype(F32)
        coded = parts_ref[i, :, :HALF].astype(jnp.int32).astype(F32)
        total += coded * (scale_of(unit[:, 1:2], unit[:, 0:1]) / 32000.0)
    tile = theta_ref[lax.rem(me_ref[0], CORES)]
    theta = jnp.concatenate([tile[t : t + 1, :] for t in range(HALF_TILES)], axis=1)
    out_ref[...] = (theta * total).astype(BF16)


def forward_body(places_ref, scaled_ref, blocks_ref, out_ref, acc_ref):
    acc_ref[...] = jnp.zeros(acc_ref.shape, F32)
    for n in range(BLOCKS):
        place = pl.multiple_of(places_ref[BLOCKS + n] % 2 * ORDER, ORDER)
        left = scaled_ref[places_ref[BLOCKS + n] // 2, :, pl.ds(place, ORDER)]
        product = lax.dot_general(left, blocks_ref[n], NT, preferred_element_type=F32)
        for g in range(GROUPS):
            for q in range(ORDER // LANES):
                acc_ref[g * (LOCAL // ORDER) + places_ref[n], q] += product[
                    8 * g : 8 * g + 8, LANES * q : LANES * (q + 1)
                ]
    per_group = SHARES // GROUPS
    for g in range(GROUPS):
        part = acc_ref[per_group * g : per_group * (g + 1)]
        largest = jnp.max(jnp.max(jnp.max(jnp.abs(part), axis=0), axis=0), axis=1, keepdims=True)
        power, mantissa = unit_of(largest)
        for u in range(per_group):
            out_ref[per_group * g + u] = encode(
                [part[u, q] for q in range(SHARE_TILES)], power, mantissa
            )


def near_body(parts_ref, out_ref):
    sums = [decode(parts_ref[i]) for i in range(SHARES)]
    while len(sums) > 1:
        sums = [[a + b for a, b in zip(*pair)] for pair in zip(sums[::2], sums[1::2])]
    for i in range(FAR_PARTS):
        for q in range(SHARE_TILES):
            out_ref[i, q] = sums[0][q]


def far_body(parts_ref, out_ref):
    total = (parts_ref[0] + parts_ref[1]) + (parts_ref[2] + parts_ref[3])
    for i in range(SHARES):
        out_ref[i] = total


def pack_square(square):
    packed = square[0:8]
    for g in range(1, GROUPS):
        packed += pltpu.roll(square[8 * g : 8 * g + 8], WIDTH * g, 1)
    return packed


def unpack_square(packed):
    lane = iota((8, LANES), 1)
    parts = [packed] + [pltpu.roll(packed, LANES - WIDTH * g, 1) for g in range(1, GROUPS)]
    return jnp.concatenate([jnp.where(lane < WIDTH, part, 0.0) for part in parts], axis=0)


def gram_body(tiles_ref, omega_ref, rhs_ref, y_ref, out_ref, all_ref):
    for i in range(SHARES):
        g, first = i // (SHARES // GROUPS), i % (SHARES // GROUPS) * SHARE_TILES
        for q in range(SHARE_TILES):
            at = LANES * (first + q)
            y_ref[8 * g : 8 * g + 8, at : at + LANES] = tiles_ref[i, q]
    omega = omega_ref[...].astype(F32)
    ysketch = y_ref[...] + regularize * omega
    y_ref[...] = ysketch
    all_ref[0:WIDTH, :] = ysketch
    all_ref[WIDTH : 2 * WIDTH, :] = omega
    all_ref[2 * WIDTH :, :] = jnp.where(
        iota((LANES - 2 * WIDTH, LOCAL), 0) == 0, rhs_ref[...], 0.0
    )
    products = lax.dot_general(
        all_ref[0 : 2 * WIDTH + 8, :], all_ref[...], NT, precision=HIGHEST, preferred_element_type=F32
    )
    lane = iota((WIDTH, LANES), 1)
    upper = products[0:WIDTH]
    cross = 0.5 * (products[WIDTH : 2 * WIDTH] + pltpu.roll(upper, LANES - WIDTH, 1))
    gram = pack_square(jnp.where(lane < WIDTH, upper + precond_shift * cross, 0.0))
    for i in range(ROW_PARTS):
        out_ref[i, 0] = gram
        out_ref[i, 1] = products[2 * WIDTH :]


def to_column(row, shift):
    lane = iota((WIDTH, LANES), 1)
    return jnp.sum(
        jnp.where(lane == iota((WIDTH, LANES), 0) + shift, row, 0.0), axis=1, keepdims=True
    )


def to_row(column, shift):
    lane = iota((WIDTH, LANES), 1)
    return jnp.sum(
        jnp.where(lane == iota((WIDTH, LANES), 0) + shift, column, 0.0), axis=0, keepdims=True
    )


def eliminate(work, panel):
    spot = iota((WIDTH, LANES), 0)
    for k in range(0, WIDTH, panel):
        rows = [work[k + i : k + i + 1, :] for i in range(panel)]
        columns = [jnp.broadcast_to(work[:, k + i : k + i + 1], work.shape) for i in range(panel)]
        square = [
            [jnp.broadcast_to(rows[i][:, k + j : k + j + 1], (1, LANES)) for j in range(panel)]
            for i in range(panel)
        ]
        update = jnp.zeros(work.shape, F32)
        for i in range(panel):
            reciprocal = 1.0 / square[i][i]
            for j in range(i + 1, panel):
                factor = square[i][j] * reciprocal
                rows[j] = rows[j] - factor * rows[i]
                columns[j] = columns[j] - factor * columns[i]
                for m in range(j, panel):
                    square[j][m] = square[j][m] - factor * square[i][m]
            update += columns[i] * (rows[i] * reciprocal)
        work = jnp.where(spot >= k + panel, work - update, work)
        for i in range(1, panel):
            work = jnp.where(spot == k + i, rows[i], work)
    return work


def solve_gram(inverse, diagonal, row):
    half = jnp.sum(inverse * pltpu.roll(row, WIDTH, 1), axis=1, keepdims=True) / diagonal
    return jnp.sum(inverse * half, axis=0, keepdims=True)


def factor_body(
    places_ref, parts_ref, y_ref, rhs_ref, blocks_ref, out_ref, keep_ref, direction_ref, low_ref, acc_ref
):
    total = parts_ref[0]
    for i in range(1, ROW_PARTS):
        total += parts_ref[i]
    lane = iota((WIDTH, LANES), 1)
    spot = iota((WIDTH, LANES), 0)
    work = eliminate(jnp.where(lane == spot + WIDTH, 1.0, unpack_square(total[0])), 4)
    diagonal = jnp.sum(jnp.where(lane == spot, work, 0.0), axis=1, keepdims=True)
    inverse = jnp.where((lane >= WIDTH) & (lane < 2 * WIDTH), work, 0.0)
    sketched_rhs = jnp.where(iota((1, LANES), 1) < WIDTH, total[1, 0:1], 0.0)
    coeffs = solve_gram(inverse, diagonal, sketched_rhs)

    ysketch = y_ref[...]
    rhs = rhs_ref[...]
    direction = (
        rhs - jnp.sum(ysketch * to_column(coeffs, WIDTH), axis=0, keepdims=True)
    ) / precond_shift
    direction_ref[...] = direction
    low_ref[...] = jnp.broadcast_to(direction, low_ref.shape).astype(BF16)

    acc_ref[...] = jnp.zeros(acc_ref.shape, F32)
    for n in range(BLOCKS):
        start = pl.multiple_of(places_ref[n] * ORDER, ORDER)
        product = jnp.dot(
            low_ref[:, pl.ds(start, ORDER)], blocks_ref[n], preferred_element_type=F32
        )
        acc_ref[places_ref[BLOCKS + n]] += product[0:8]
    row = iota((8, LANES), 0)
    per_block = ORDER // LANES
    for h in range(CORES):
        tile = jnp.zeros((8, LANES), F32)
        for t in range(HALF_TILES):
            j = h * (HALF_TILES // per_block) + t // per_block
            at = LANES * (t % per_block)
            tile = jnp.where(row == t, acc_ref[j, :, at : at + LANES], tile)
        for i in range(ROW_PARTS):
            out_ref[i, h] = tile

    sketched = to_row(jnp.sum(ysketch * direction, axis=1, keepdims=True), 3 * WIDTH)
    length = jnp.sum(direction * direction, axis=1, keepdims=True)
    along = jnp.sum(rhs * direction, axis=1, keepdims=True)
    line = iota((1, LANES), 1)
    sums = jnp.where(line == 2 * WIDTH + 1, length, sketched)
    sums = jnp.where(line == 2 * WIDTH + 2, along, sums)
    keep_ref[0:WIDTH, :] = inverse
    keep_ref[WIDTH : 2 * WIDTH, :] = jnp.broadcast_to(diagonal, (WIDTH, LANES))
    keep_ref[2 * WIDTH : 2 * WIDTH + 8, :] = jnp.broadcast_to(sketched_rhs, (8, LANES))
    keep_ref[2 * WIDTH + 8 :, :] = jnp.broadcast_to(sums, (8, LANES))


def image_body(
    places_ref,
    parts_ref,
    theta_ref,
    y_ref,
    direction_ref,
    keep_ref,
    blocks_ref,
    out_ref,
    sums_ref,
    scaled_ref,
    acc_ref,
):
    total = parts_ref[0]
    for i in range(1, ROW_PARTS):
        total += parts_ref[i]
    scaled = theta_ref[...] * total
    per_block = ORDER // LANES
    for j in range(LOCAL // ORDER):
        h, first = j // 2, j % 2 * per_block
        line = jnp.concatenate(
            [scaled[h, first + q : first + q + 1, :] for q in range(per_block)], axis=1
        )
        scaled_ref[j] = jnp.broadcast_to(line, (16, ORDER)).astype(BF16)
    acc_ref[...] = jnp.zeros(acc_ref.shape, F32)
    for n in range(BLOCKS):
        product = lax.dot_general(
            scaled_ref[places_ref[BLOCKS + n]], blocks_ref[n], NT, preferred_element_type=F32
        )
        acc_ref[places_ref[n]] += product[0:8]

    whole = jnp.concatenate([acc_ref[r, 0:1, :] for r in range(LOCAL // ORDER)], axis=1)
    sketched = to_row(jnp.sum(y_ref[...] * whole, axis=1, keepdims=True), WIDTH)
    curvature = jnp.sum(direction_ref[...] * whole, axis=1, keepdims=True)
    sums = jnp.where(iota((1, LANES), 1) == 2 * WIDTH, curvature, sketched)
    sums += keep_ref[2 * WIDTH + 8 : 2 * WIDTH + 9, :]
    sums_ref[...] = jnp.broadcast_to(sums, sums_ref.shape)
    row = iota((8, LANES), 0)
    for h in range(CORES):
        tile = jnp.zeros((8, LANES), F32)
        for t in range(HALF_TILES):
            r, at = (h * HALF_TILES + t) // per_block, LANES * (t % per_block)
            tile = jnp.where(row == t, acc_ref[r, :, at : at + LANES], tile)
        out_ref[h] = tile


def lines_body(
    me_ref, image_ref, parts_ref, y_ref, rhs_ref, direction_ref, out_ref, sums_ref, mine_ref
):
    shares = LANES // WIDTH
    column = lax.div(me_ref[0], CORES)
    start = pl.multiple_of(lax.div(column, shares) * LANES, LANES)
    turn = lax.rem(shares - lax.rem(column, shares), shares) * WIDTH
    mine_ref[0:WIDTH, :] = pltpu.roll(y_ref[:, pl.ds(start, LANES)], turn, 1)
    rhs = jnp.broadcast_to(rhs_ref[:, pl.ds(start, LANES)], (8, LANES))
    mine_ref[WIDTH : WIDTH + 8, :] = pltpu.roll(rhs, turn, 1)
    direction = jnp.broadcast_to(direction_ref[:, pl.ds(start, LANES)], (8, LANES))
    mine_ref[WIDTH + 8 :, :] = pltpu.roll(direction, turn, 1)
    sums = jnp.sum(parts_ref[...], axis=0, keepdims=True)
    sums_ref[...] = jnp.broadcast_to(sums, sums_ref.shape)
    lane = iota((8, LANES), 1)
    row = iota((8, LANES), 0)
    shares = LANES // WIDTH
    added = jnp.broadcast_to(
        jnp.where(iota((1, LANES), 1) <= 2 * WIDTH, sums, 0.0), (8, LANES)
    )
    for u in range(TILES // 2):
        pack = added
        for v in range(2):
            t = 2 * u + v
            line = image_ref[t // HALF_TILES, t % HALF_TILES : t % HALF_TILES + 1, :]
            for q in range(shares):
                turned = line if q == 0 else pltpu.roll(line, LANES - WIDTH * q, 1)
                pack = jnp.where((lane < WIDTH) & (row == shares * v + q), turned, pack)
        out_ref[8 * u : 8 * u + 8, :] = pack


def step_body(
    parts_ref, sums_ref, keep_ref, mine_ref, solution_ref, residual_ref, precond_ref
):
    total = parts_ref[0:8, :]
    for i in range(1, COL_PARTS // 8):
        total += parts_ref[8 * i : 8 * i + 8, :]
    total = jnp.sum(total, axis=0, keepdims=True)
    sums = sums_ref[0:1, :]
    lane = iota((1, LANES), 1)
    inverse = keep_ref[0:WIDTH, :]
    diagonal = keep_ref[WIDTH : 2 * WIDTH, 0:1]
    sketched_rhs = keep_ref[2 * WIDTH : 2 * WIDTH + 1, :]

    def pick(line, at):
        return jnp.sum(jnp.where(lane == at, line, 0.0), axis=1, keepdims=True)

    along = pick(sums, 2 * WIDTH + 2)
    curvature = pick(total, 2 * WIDTH) + regularize * pick(sums, 2 * WIDTH + 1)
    alpha = along / curvature

    ysketch = mine_ref[0:WIDTH, :]
    rhs = mine_ref[WIDTH : WIDTH + 1, :]
    direction = mine_ref[WIDTH + 8 : WIDTH + 9, :]
    image = total + regularize * direction
    residual = rhs - alpha * image
    sketched_image = pltpu.roll(total, LANES - WIDTH, 1) + regularize * pltpu.roll(sums, WIDTH, 1)
    sketched_image = jnp.where(lane < WIDTH, sketched_image, 0.0)
    res_coeffs = solve_gram(inverse, diagonal, sketched_rhs - alpha * sketched_image)
    precond_residual = (
        residual - jnp.sum(ysketch * to_column(res_coeffs, WIDTH), axis=0, keepdims=True)
    ) / precond_shift
    solution_ref[...] = (alpha * direction)[0, :WIDTH]
    residual_ref[...] = residual[0, :WIDTH]
    precond_ref[...] = precond_residual[0, :WIDTH]


def exchange(value, axis):
    return lax.all_to_all(value, axis, 0, 0, tiled=True)


def shards(blocks, block_rows, block_cols, sketch, theta, rhs):
    values = blocks[0, 0]
    omega = sketch.T
    rhs_line = rhs.reshape(1, LOCAL)
    theta_tiles = theta.reshape(CORES, HALF_TILES, LANES)
    places = jnp.concatenate([block_rows[0, 0], block_cols[0, 0]])
    me = lax.axis_index("core") + CORES * lax.axis_index(("y", "far", "near"))
    me = me.astype(jnp.int32).reshape(1)
    shape = jax.ShapeDtypeStruct
    work = 2 * BLOCKS * ORDER * ORDER

    with jax.named_scope("sketch_cols"):
        terms = call(
            sketch_body,
            [smem(), smem(), vmem(), vmem()],
            shape((CORES, WIDTH, HALF), F32),
            flops=work * WIDTH,
            name="sketch_cols",
        )(me, places, omega, values)
        parts = lax.all_gather(terms, "core")
        parts = call(
            pair_body, [smem(), vmem()], shape((X_PARTS, WIDTH, HALF + LANES), I16), name="pair"
        )(me, parts)
        parts = exchange(parts, "x")
    with jax.named_scope("scaled"):
        scaled = call(
            scale_body, [smem(), vmem(), vmem()], shape((WIDTH, HALF), BF16), name="scaled"
        )(me, parts, theta_tiles)
        scaled = lax.all_gather(scaled, "core")
    with jax.named_scope("ysketch"):
        terms = call(
            forward_body,
            [smem(), vmem(), vmem()],
            shape((SHARES, 8 * SHARE_TILES + 8, LANES), I16),
            scratch=[pltpu.VMEM((SHARES, SHARE_TILES, 8, LANES), F32)],
            flops=work * WIDTH,
            name="ysketch",
        )(places, scaled, values)
        parts = exchange(terms, ("y", "near"))
        parts = call(
            near_body,
            [vmem()],
            shape((FAR_PARTS, SHARE_TILES, 8, LANES), F32),
            name="ysketch_near",
        )(parts)
        parts = exchange(parts, "far")
        parts = call(
            far_body,
            [vmem()],
            shape((SHARES, SHARE_TILES, 8, LANES), F32),
            name="ysketch_far",
        )(parts)
        tiles = exchange(parts, ("y", "near"))
    with jax.named_scope("gram"):
        ysketch, terms = call(
            gram_body,
            [vmem(), vmem(), vmem()],
            (shape((WIDTH, LOCAL), F32), shape((ROW_PARTS, 2, 8, LANES), F32)),
            scratch=[pltpu.VMEM((LANES, LOCAL), F32)],
            name="gram",
        )(tiles, omega, rhs_line)
        parts = exchange(terms, ("x", "core"))
    with jax.named_scope("direction"):
        terms, keep, direction = call(
            factor_body,
            [smem(), vmem(), vmem(), vmem(), vmem()],
            (
                shape((ROW_PARTS, CORES, HALF_TILES, LANES), F32),
                shape((2 * WIDTH + 16, LANES), F32),
                shape((1, LOCAL), F32),
            ),
            scratch=[
                pltpu.VMEM((16, LOCAL), BF16),
                pltpu.VMEM((LOCAL // ORDER, 8, ORDER), F32),
            ],
            flops=work,
            name="direction",
        )(places, parts, ysketch, rhs_line, values)
        parts = exchange(terms, ("x", "core"))
    with jax.named_scope("image"):
        image, terms = call(
            image_body,
            [smem()] + [vmem()] * 6,
            (shape((CORES, HALF_TILES, LANES), F32), shape((ROW_PARTS, LANES), F32)),
            scratch=[
                pltpu.VMEM((LOCAL // ORDER, 16, ORDER), BF16),
                pltpu.VMEM((LOCAL // ORDER, 8, ORDER), F32),
            ],
            flops=work,
            name="image",
        )(places, parts, theta_tiles, ysketch, direction, keep, values)
        parts = exchange(terms, ("x", "core"))
        terms, sums, mine = call(
            lines_body,
            [smem()] + [vmem()] * 5,
            (
                shape((COL_PARTS, LANES), F32),
                shape((8, LANES), F32),
                shape((WIDTH + 16, LANES), F32),
            ),
            name="lines",
        )(me, image, parts, ysketch, rhs_line, direction)
        parts = exchange(terms, ("y", "far", "near"))
    with jax.named_scope("step"):
        share = shape((LOCAL // COL_PARTS,), F32)
        return call(
            step_body,
            [vmem()] * 4,
            (share, share, share),
            name="step",
        )(parts, sums, keep, mine)


def solution(mesh):
    row, col = ("x", "core"), ("y", "far", "near")
    fine = jax.sharding.Mesh(
        mesh.devices.reshape(X_PARTS, CORES, Y_PARTS, FAR_PARTS, NEAR_PARTS),
        ("x", "core", "y", "far", "near"),
    )
    in_specs = (
        P(row, col, None, None, None),
        P(row, col, None),
        P(row, col, None),
        P(row, None),
        P(col),
        P(row),
    )
    out_specs = (P(row + col), P(row + col), P(row + col))
    return jax.shard_map(shards, mesh=fine, in_specs=in_specs, out_specs=out_specs, check_vma=False)
```

```python
import jax
import jax.numpy as jnp
from jax import lax
from jax.experimental import pallas as pl
from jax.experimental.pallas import tpu as pltpu
from jax.sharding import PartitionSpec as P

precond_shift = 1.0
regularize = 0.5

F32 = jnp.float32
BF16 = jnp.bfloat16
I16 = jnp.int16
HIGHEST = lax.Precision.HIGHEST
LANES = 128
CORES = 2
X_PARTS = 4
Y_PARTS = 4
ROW_PARTS = X_PARTS * CORES
FAR_PARTS = 4
NEAR_PARTS = 4
COL_PARTS = Y_PARTS * FAR_PARTS * NEAR_PARTS
BLOCKS = 8
ORDER = 512
LOCAL = 2048
WIDTH = 32
TINY = 2.0**-100
HALF = LOCAL // CORES
HALF_TILES = HALF // LANES
TILES = LOCAL // LANES
GROUPS = WIDTH // 8
SHARES = Y_PARTS * NEAR_PARTS
SHARE_TILES = GROUPS * TILES // SHARES
VMEM_LIMIT = 24 * 1024 * 1024

NT = (((1,), (1,)), ((), ()))


def vmem():
    return pl.BlockSpec(memory_space=pltpu.VMEM)


def smem():
    return pl.BlockSpec(memory_space=pltpu.SMEM)


def iota(shape, axis):
    return lax.broadcasted_iota(jnp.int32, shape, axis)


def call(body, in_specs, out_shape, scratch=(), flops=0, name=None):
    out_specs = jax.tree.map(lambda _: vmem(), out_shape)
    return pl.pallas_call(
        body,
        in_specs=in_specs,
        out_specs=out_specs,
        out_shape=out_shape,
        scratch_shapes=list(scratch),
        compiler_params=pltpu.CompilerParams(vmem_limit_bytes=VMEM_LIMIT),
        cost_estimate=pl.CostEstimate(flops=flops, bytes_accessed=1 << 20, transcendentals=0),
        name=name,
    )


def place_of(places_ref, n):
    return lax.bitwise_and(lax.shift_right_logical(places_ref[0], 2 * n), 3)


def sketch_body(me_ref, places_ref, omega_ref, blocks_ref, out_ref):
    del me_ref
    out_ref[...] = jnp.zeros(out_ref.shape, F32)
    for n in range(BLOCKS):
        start = pl.multiple_of(place_of(places_ref, n) * ORDER, ORDER)
        place = pl.multiple_of(place_of(places_ref, BLOCKS + n) % 2 * ORDER, ORDER)
        out_ref[place_of(places_ref, BLOCKS + n) // 2, :, pl.ds(place, ORDER)] += jnp.dot(
            omega_ref[:, pl.ds(start, ORDER)], blocks_ref[n], preferred_element_type=F32
        )


def scale_of(mantissa, power):
    return mantissa * jnp.exp2(power - 14.0)


def unit_of(largest):
    largest = jnp.maximum(largest, TINY)
    power = jnp.ceil(jnp.log2(largest))
    return power, jnp.ceil(largest * jnp.exp2(14.0 - power))


def encode(tiles, power, mantissa):
    factor = 32000.0 / scale_of(mantissa, power)
    unit = jnp.where(iota((8, LANES), 1) == 0, power, mantissa)
    rows = jnp.concatenate([tile * factor for tile in tiles] + [unit], axis=0)
    return jnp.round(rows).astype(jnp.int32).astype(I16)


def decode(coded):
    rows = coded.astype(jnp.int32).astype(F32)
    unit = rows[8 * SHARE_TILES :]
    factor = scale_of(unit[:, 1:2], unit[:, 0:1]) / 32000.0
    return [rows[8 * q : 8 * q + 8] * factor for q in range(SHARE_TILES)]


def pair_body(me_ref, parts_ref, out_ref):
    half = lax.rem(me_ref[0], CORES)
    total = parts_ref[0, half] + parts_ref[1, half]
    power, mantissa = unit_of(jnp.max(jnp.abs(total), axis=1, keepdims=True))
    coded = jnp.round(total * (32000.0 / scale_of(mantissa, power))).astype(jnp.int32).astype(I16)
    unit = jnp.where(iota((WIDTH, LANES), 1) == 0, power, mantissa).astype(jnp.int32).astype(I16)
    for i in range(X_PARTS):
        out_ref[i, :, :HALF] = coded
        out_ref[i, :, HALF:] = unit


def scale_body(me_ref, parts_ref, theta_ref, out_ref):
    total = jnp.zeros(out_ref.shape, F32)
    for i in range(X_PARTS):
        unit = parts_ref[i, :, HALF:].astype(jnp.int32).astype(F32)
        coded = parts_ref[i, :, :HALF].astype(jnp.int32).astype(F32)
        total += coded * (scale_of(unit[:, 1:2], unit[:, 0:1]) / 32000.0)
    tile = theta_ref[lax.rem(me_ref[0], CORES)]
    theta = jnp.concatenate([tile[t : t + 1, :] for t in range(HALF_TILES)], axis=1)
    out_ref[...] = (theta * total).astype(BF16)


def forward_body(places_ref, scaled_ref, blocks_ref, out_ref, acc_ref):
    acc_ref[...] = jnp.zeros(acc_ref.shape, F32)
    for n in range(BLOCKS):
        place = pl.multiple_of(place_of(places_ref, BLOCKS + n) % 2 * ORDER, ORDER)
        left = scaled_ref[place_of(places_ref, BLOCKS + n) // 2, :, pl.ds(place, ORDER)]
        product = lax.dot_general(left, blocks_ref[n], NT, preferred_element_type=F32)
        for g in range(GROUPS):
            for q in range(ORDER // LANES):
                acc_ref[g * (LOCAL // ORDER) + place_of(places_ref, n), q] += product[
                    8 * g : 8 * g + 8, LANES * q : LANES * (q + 1)
                ]
    per_group = SHARES // GROUPS
    for g in range(GROUPS):
        part = acc_ref[per_group * g : per_group * (g + 1)]
        largest = jnp.max(jnp.max(jnp.max(jnp.abs(part), axis=0), axis=0), axis=1, keepdims=True)
        power, mantissa = unit_of(largest)
        for u in range(per_group):
            out_ref[per_group * g + u] = encode(
                [part[u, q] for q in range(SHARE_TILES)], power, mantissa
            )


def near_body(parts_ref, out_ref):
    sums = [decode(parts_ref[i]) for i in range(SHARES)]
    while len(sums) > 1:
        sums = [[a + b for a, b in zip(*pair)] for pair in zip(sums[::2], sums[1::2])]
    for i in range(FAR_PARTS):
        for q in range(SHARE_TILES):
            out_ref[i, q] = sums[0][q]


def far_body(parts_ref, out_ref):
    total = (parts_ref[0] + parts_ref[1]) + (parts_ref[2] + parts_ref[3])
    for i in range(SHARES):
        out_ref[i] = total


def pack_square(square):
    packed = square[0:8]
    for g in range(1, GROUPS):
        packed += pltpu.roll(square[8 * g : 8 * g + 8], WIDTH * g, 1)
    return packed


def unpack_square(packed):
    lane = iota((8, LANES), 1)
    parts = [packed] + [pltpu.roll(packed, LANES - WIDTH * g, 1) for g in range(1, GROUPS)]
    return jnp.concatenate([jnp.where(lane < WIDTH, part, 0.0) for part in parts], axis=0)


def gram_body(tiles_ref, omega_ref, rhs_ref, y_ref, out_ref, all_ref):
    for i in range(SHARES):
        g, first = i // (SHARES // GROUPS), i % (SHARES // GROUPS) * SHARE_TILES
        for q in range(SHARE_TILES):
            at = LANES * (first + q)
            y_ref[8 * g : 8 * g + 8, at : at + LANES] = tiles_ref[i, q]
    omega = omega_ref[...].astype(F32)
    ysketch = y_ref[...] + regularize * omega
    y_ref[...] = ysketch
    all_ref[0:WIDTH, :] = ysketch
    all_ref[WIDTH : 2 * WIDTH, :] = omega
    all_ref[2 * WIDTH :, :] = jnp.where(
        iota((LANES - 2 * WIDTH, LOCAL), 0) == 0, rhs_ref[...], 0.0
    )
    products = lax.dot_general(
        all_ref[0 : 2 * WIDTH + 8, :], all_ref[...], NT, precision=HIGHEST, preferred_element_type=F32
    )
    lane = iota((WIDTH, LANES), 1)
    upper = products[0:WIDTH]
    cross = 0.5 * (products[WIDTH : 2 * WIDTH] + pltpu.roll(upper, LANES - WIDTH, 1))
    gram = pack_square(jnp.where(lane < WIDTH, upper + precond_shift * cross, 0.0))
    for i in range(ROW_PARTS):
        out_ref[i, 0] = gram
        out_ref[i, 1] = products[2 * WIDTH :]


def to_column(row, shift):
    lane = iota((WIDTH, LANES), 1)
    return jnp.sum(
        jnp.where(lane == iota((WIDTH, LANES), 0) + shift, row, 0.0), axis=1, keepdims=True
    )


def to_row(column, shift):
    lane = iota((WIDTH, LANES), 1)
    return jnp.sum(
        jnp.where(lane == iota((WIDTH, LANES), 0) + shift, column, 0.0), axis=0, keepdims=True
    )


def eliminate(work, panel):
    spot = iota((WIDTH, LANES), 0)
    for k in range(0, WIDTH, panel):
        rows = [work[k + i : k + i + 1, :] for i in range(panel)]
        columns = [jnp.broadcast_to(work[:, k + i : k + i + 1], work.shape) for i in range(panel)]
        square = [
            [jnp.broadcast_to(rows[i][:, k + j : k + j + 1], (1, LANES)) for j in range(panel)]
            for i in range(panel)
        ]
        update = jnp.zeros(work.shape, F32)
        for i in range(panel):
            reciprocal = 1.0 / square[i][i]
            for j in range(i + 1, panel):
                factor = square[i][j] * reciprocal
                rows[j] = rows[j] - factor * rows[i]
                columns[j] = columns[j] - factor * columns[i]
                for m in range(j, panel):
                    square[j][m] = square[j][m] - factor * square[i][m]
            update += columns[i] * (rows[i] * reciprocal)
        work = jnp.where(spot >= k + panel, work - update, work)
        for i in range(1, panel):
            work = jnp.where(spot == k + i, rows[i], work)
    return work


def solve_gram(inverse, diagonal, row):
    half = jnp.sum(inverse * pltpu.roll(row, WIDTH, 1), axis=1, keepdims=True) / diagonal
    return jnp.sum(inverse * half, axis=0, keepdims=True)


def factor_body(
    places_ref, parts_ref, y_ref, rhs_ref, blocks_ref, out_ref, keep_ref, direction_ref, low_ref, acc_ref
):
    total = parts_ref[0]
    for i in range(1, ROW_PARTS):
        total += parts_ref[i]
    lane = iota((WIDTH, LANES), 1)
    spot = iota((WIDTH, LANES), 0)
    work = eliminate(jnp.where(lane == spot + WIDTH, 1.0, unpack_square(total[0])), 8)
    diagonal = jnp.sum(jnp.where(lane == spot, work, 0.0), axis=1, keepdims=True)
    inverse = jnp.where((lane >= WIDTH) & (lane < 2 * WIDTH), work, 0.0)
    sketched_rhs = jnp.where(iota((1, LANES), 1) < WIDTH, total[1, 0:1], 0.0)
    coeffs = solve_gram(inverse, diagonal, sketched_rhs)

    ysketch = y_ref[...]
    rhs = rhs_ref[...]
    direction = (
        rhs - jnp.sum(ysketch * to_column(coeffs, WIDTH), axis=0, keepdims=True)
    ) / precond_shift
    direction_ref[...] = direction
    low_ref[...] = jnp.broadcast_to(direction, low_ref.shape).astype(BF16)

    acc_ref[...] = jnp.zeros(acc_ref.shape, F32)
    for n in range(BLOCKS):
        start = pl.multiple_of(place_of(places_ref, n) * ORDER, ORDER)
        product = jnp.dot(
            low_ref[:, pl.ds(start, ORDER)], blocks_ref[n], preferred_element_type=F32
        )
        acc_ref[place_of(places_ref, BLOCKS + n)] += product[0:8]
    row = iota((8, LANES), 0)
    per_block = ORDER // LANES
    for h in range(CORES):
        tile = jnp.zeros((8, LANES), F32)
        for t in range(HALF_TILES):
            j = h * (HALF_TILES // per_block) + t // per_block
            at = LANES * (t % per_block)
            tile = jnp.where(row == t, acc_ref[j, :, at : at + LANES], tile)
        for i in range(ROW_PARTS):
            out_ref[i, h] = tile

    sketched = to_row(jnp.sum(ysketch * direction, axis=1, keepdims=True), 3 * WIDTH)
    length = jnp.sum(direction * direction, axis=1, keepdims=True)
    along = jnp.sum(rhs * direction, axis=1, keepdims=True)
    line = iota((1, LANES), 1)
    sums = jnp.where(line == 2 * WIDTH + 1, length, sketched)
    sums = jnp.where(line == 2 * WIDTH + 2, along, sums)
    keep_ref[0:WIDTH, :] = inverse
    keep_ref[WIDTH : 2 * WIDTH, :] = jnp.broadcast_to(diagonal, (WIDTH, LANES))
    keep_ref[2 * WIDTH : 2 * WIDTH + 8, :] = jnp.broadcast_to(sketched_rhs, (8, LANES))
    keep_ref[2 * WIDTH + 8 :, :] = jnp.broadcast_to(sums, (8, LANES))


def image_body(
    places_ref,
    parts_ref,
    theta_ref,
    y_ref,
    direction_ref,
    keep_ref,
    blocks_ref,
    out_ref,
    sums_ref,
    scaled_ref,
    acc_ref,
):
    total = parts_ref[0]
    for i in range(1, ROW_PARTS):
        total += parts_ref[i]
    scaled = theta_ref[...] * total
    per_block = ORDER // LANES
    for j in range(LOCAL // ORDER):
        h, first = j // 2, j % 2 * per_block
        line = jnp.concatenate(
            [scaled[h, first + q : first + q + 1, :] for q in range(per_block)], axis=1
        )
        scaled_ref[j] = jnp.broadcast_to(line, (16, ORDER)).astype(BF16)
    acc_ref[...] = jnp.zeros(acc_ref.shape, F32)
    for n in range(BLOCKS):
        product = lax.dot_general(
            scaled_ref[place_of(places_ref, BLOCKS + n)], blocks_ref[n], NT, preferred_element_type=F32
        )
        acc_ref[place_of(places_ref, n)] += product[0:8]

    whole = jnp.concatenate([acc_ref[r, 0:1, :] for r in range(LOCAL // ORDER)], axis=1)
    sketched = to_row(jnp.sum(y_ref[...] * whole, axis=1, keepdims=True), WIDTH)
    curvature = jnp.sum(direction_ref[...] * whole, axis=1, keepdims=True)
    sums = jnp.where(iota((1, LANES), 1) == 2 * WIDTH, curvature, sketched)
    sums += keep_ref[2 * WIDTH + 8 : 2 * WIDTH + 9, :]
    sums_ref[...] = jnp.broadcast_to(sums, sums_ref.shape)
    row = iota((8, LANES), 0)
    for h in range(CORES):
        tile = jnp.zeros((8, LANES), F32)
        for t in range(HALF_TILES):
            r, at = (h * HALF_TILES + t) // per_block, LANES * (t % per_block)
            tile = jnp.where(row == t, acc_ref[r, :, at : at + LANES], tile)
        out_ref[h] = tile


def lines_body(
    me_ref, image_ref, parts_ref, y_ref, rhs_ref, direction_ref, out_ref, sums_ref, mine_ref
):
    shares = LANES // WIDTH
    column = lax.div(me_ref[0], CORES)
    start = pl.multiple_of(lax.div(column, shares) * LANES, LANES)
    turn = lax.rem(shares - lax.rem(column, shares), shares) * WIDTH
    mine_ref[0:WIDTH, :] = pltpu.roll(y_ref[:, pl.ds(start, LANES)], turn, 1)
    rhs = jnp.broadcast_to(rhs_ref[:, pl.ds(start, LANES)], (8, LANES))
    mine_ref[WIDTH : WIDTH + 8, :] = pltpu.roll(rhs, turn, 1)
    direction = jnp.broadcast_to(direction_ref[:, pl.ds(start, LANES)], (8, LANES))
    mine_ref[WIDTH + 8 :, :] = pltpu.roll(direction, turn, 1)
    sums = jnp.sum(parts_ref[...], axis=0, keepdims=True)
    sums_ref[...] = jnp.broadcast_to(sums, sums_ref.shape)
    lane = iota((8, LANES), 1)
    row = iota((8, LANES), 0)
    shares = LANES // WIDTH
    added = jnp.broadcast_to(
        jnp.where(iota((1, LANES), 1) <= 2 * WIDTH, sums, 0.0), (8, LANES)
    )
    for u in range(TILES // 2):
        pack = added
        for v in range(2):
            t = 2 * u + v
            line = image_ref[t // HALF_TILES, t % HALF_TILES : t % HALF_TILES + 1, :]
            for q in range(shares):
                turned = line if q == 0 else pltpu.roll(line, LANES - WIDTH * q, 1)
                pack = jnp.where((lane < WIDTH) & (row == shares * v + q), turned, pack)
        out_ref[8 * u : 8 * u + 8, :] = pack


def step_body(
    parts_ref, sums_ref, keep_ref, mine_ref, solution_ref, residual_ref, precond_ref
):
    total = parts_ref[0:8, :]
    for i in range(1, COL_PARTS // 8):
        total += parts_ref[8 * i : 8 * i + 8, :]
    total = jnp.sum(total, axis=0, keepdims=True)
    sums = sums_ref[0:1, :]
    lane = iota((1, LANES), 1)
    inverse = keep_ref[0:WIDTH, :]
    diagonal = keep_ref[WIDTH : 2 * WIDTH, 0:1]
    sketched_rhs = keep_ref[2 * WIDTH : 2 * WIDTH + 1, :]

    def pick(line, at):
        return jnp.sum(jnp.where(lane == at, line, 0.0), axis=1, keepdims=True)

    along = pick(sums, 2 * WIDTH + 2)
    curvature = pick(total, 2 * WIDTH) + regularize * pick(sums, 2 * WIDTH + 1)
    alpha = along / curvature

    ysketch = mine_ref[0:WIDTH, :]
    rhs = mine_ref[WIDTH : WIDTH + 1, :]
    direction = mine_ref[WIDTH + 8 : WIDTH + 9, :]
    image = total + regularize * direction
    residual = rhs - alpha * image
    sketched_image = pltpu.roll(total, LANES - WIDTH, 1) + regularize * pltpu.roll(sums, WIDTH, 1)
    sketched_image = jnp.where(lane < WIDTH, sketched_image, 0.0)
    res_coeffs = solve_gram(inverse, diagonal, sketched_rhs - alpha * sketched_image)
    precond_residual = (
        residual - jnp.sum(ysketch * to_column(res_coeffs, WIDTH), axis=0, keepdims=True)
    ) / precond_shift
    solution_ref[...] = (alpha * direction)[0, :WIDTH]
    residual_ref[...] = residual[0, :WIDTH]
    precond_ref[...] = precond_residual[0, :WIDTH]


def exchange(value, axis):
    return lax.all_to_all(value, axis, 0, 0, tiled=True)


def shards(blocks, block_rows, block_cols, sketch, theta, rhs):
    values = blocks[0, 0]
    omega = sketch.T
    rhs_line = rhs.reshape(1, LOCAL)
    theta_tiles = theta.reshape(CORES, HALF_TILES, LANES)
    places = jnp.concatenate([block_rows[0, 0], block_cols[0, 0]])
    places = jnp.sum(jnp.left_shift(places, 2 * jnp.arange(2 * BLOCKS, dtype=jnp.int32)))
    me = lax.axis_index("core") + CORES * lax.axis_index(("y", "far", "near"))
    me = me.astype(jnp.int32)
    places = (places + lax.shift_right_arithmetic(me, 30)).reshape(1)
    me = me.reshape(1)
    shape = jax.ShapeDtypeStruct
    work = 2 * BLOCKS * ORDER * ORDER

    with jax.named_scope("sketch_cols"):
        terms = call(
            sketch_body,
            [smem(), smem(), vmem(), vmem()],
            shape((CORES, WIDTH, HALF), F32),
            flops=work * WIDTH,
            name="sketch_cols",
        )(me, places, omega, values)
        parts = lax.all_gather(terms, "core")
        parts = call(
            pair_body, [smem(), vmem()], shape((X_PARTS, WIDTH, HALF + LANES), I16), name="pair"
        )(me, parts)
        parts = exchange(parts, "x")
    with jax.named_scope("scaled"):
        scaled = call(
            scale_body, [smem(), vmem(), vmem()], shape((WIDTH, HALF), BF16), name="scaled"
        )(me, parts, theta_tiles)
        scaled = lax.all_gather(scaled, "core")
    with jax.named_scope("ysketch"):
        terms = call(
            forward_body,
            [smem(), vmem(), vmem()],
            shape((SHARES, 8 * SHARE_TILES + 8, LANES), I16),
            scratch=[pltpu.VMEM((SHARES, SHARE_TILES, 8, LANES), F32)],
            flops=work * WIDTH,
            name="ysketch",
        )(places, scaled, values)
        parts = exchange(terms, ("y", "near"))
        parts = call(
            near_body,
            [vmem()],
            shape((FAR_PARTS, SHARE_TILES, 8, LANES), F32),
            name="ysketch_near",
        )(parts)
        parts = exchange(parts, "far")
        parts = call(
            far_body,
            [vmem()],
            shape((SHARES, SHARE_TILES, 8, LANES), F32),
            name="ysketch_far",
        )(parts)
        tiles = exchange(parts, ("y", "near"))
    with jax.named_scope("gram"):
        ysketch, terms = call(
            gram_body,
            [vmem(), vmem(), vmem()],
            (shape((WIDTH, LOCAL), F32), shape((ROW_PARTS, 2, 8, LANES), F32)),
            scratch=[pltpu.VMEM((LANES, LOCAL), F32)],
            name="gram",
        )(tiles, omega, rhs_line)
        parts = exchange(terms, ("x", "core"))
    with jax.named_scope("direction"):
        terms, keep, direction = call(
            factor_body,
            [smem(), vmem(), vmem(), vmem(), vmem()],
            (
                shape((ROW_PARTS, CORES, HALF_TILES, LANES), F32),
                shape((2 * WIDTH + 16, LANES), F32),
                shape((1, LOCAL), F32),
            ),
            scratch=[
                pltpu.VMEM((16, LOCAL), BF16),
                pltpu.VMEM((LOCAL // ORDER, 8, ORDER), F32),
            ],
            flops=work,
            name="direction",
        )(places, parts, ysketch, rhs_line, values)
        parts = exchange(terms, ("x", "core"))
    with jax.named_scope("image"):
        image, terms = call(
            image_body,
            [smem()] + [vmem()] * 6,
            (shape((CORES, HALF_TILES, LANES), F32), shape((ROW_PARTS, LANES), F32)),
            scratch=[
                pltpu.VMEM((LOCAL // ORDER, 16, ORDER), BF16),
                pltpu.VMEM((LOCAL // ORDER, 8, ORDER), F32),
            ],
            flops=work,
            name="image",
        )(places, parts, theta_tiles, ysketch, direction, keep, values)
        parts = exchange(terms, ("x", "core"))
        terms, sums, mine = call(
            lines_body,
            [smem()] + [vmem()] * 5,
            (
                shape((COL_PARTS, LANES), F32),
                shape((8, LANES), F32),
                shape((WIDTH + 16, LANES), F32),
            ),
            name="lines",
        )(me, image, parts, ysketch, rhs_line, direction)
        parts = exchange(terms, ("y", "far", "near"))
    with jax.named_scope("step"):
        share = shape((LOCAL // COL_PARTS,), F32)
        return call(
            step_body,
            [vmem()] * 4,
            (share, share, share),
            name="step",
        )(parts, sums, keep, mine)


def solution(mesh):
    row, col = ("x", "core"), ("y", "far", "near")
    fine = jax.sharding.Mesh(
        mesh.devices.reshape(X_PARTS, CORES, Y_PARTS, FAR_PARTS, NEAR_PARTS),
        ("x", "core", "y", "far", "near"),
    )
    in_specs = (
        P(row, col, None, None, None),
        P(row, col, None),
        P(row, col, None),
        P(row, None),
        P(col),
        P(row),
    )
    out_specs = (P(row + col), P(row + col), P(row + col))
    return jax.shard_map(shards, mesh=fine, in_specs=in_specs, out_specs=out_specs, check_vma=False)
```

```python
import jax
import jax.numpy as jnp
from jax import lax
from jax.experimental import pallas as pl
from jax.experimental.pallas import tpu as pltpu
from jax.sharding import PartitionSpec as P

precond_shift = 1.0
regularize = 0.5

F32 = jnp.float32
BF16 = jnp.bfloat16
I16 = jnp.int16
HIGHEST = lax.Precision.HIGHEST
LANES = 128
CORES = 2
X_PARTS = 4
Y_PARTS = 4
ROW_PARTS = X_PARTS * CORES
FAR_PARTS = 4
NEAR_PARTS = 4
COL_PARTS = Y_PARTS * FAR_PARTS * NEAR_PARTS
BLOCKS = 8
ORDER = 512
LOCAL = 2048
WIDTH = 32
TINY = 2.0**-100
HALF = LOCAL // CORES
HALF_TILES = HALF // LANES
TILES = LOCAL // LANES
GROUPS = WIDTH // 8
SHARES = Y_PARTS * NEAR_PARTS
SHARE_TILES = GROUPS * TILES // SHARES
VMEM_LIMIT = 24 * 1024 * 1024

NT = (((1,), (1,)), ((), ()))


def vmem():
    return pl.BlockSpec(memory_space=pltpu.VMEM)


def smem():
    return pl.BlockSpec(memory_space=pltpu.SMEM)


def iota(shape, axis):
    return lax.broadcasted_iota(jnp.int32, shape, axis)


def call(body, in_specs, out_shape, scratch=(), flops=0, name=None):
    out_specs = jax.tree.map(lambda _: vmem(), out_shape)
    return pl.pallas_call(
        body,
        in_specs=in_specs,
        out_specs=out_specs,
        out_shape=out_shape,
        scratch_shapes=list(scratch),
        compiler_params=pltpu.CompilerParams(vmem_limit_bytes=VMEM_LIMIT),
        cost_estimate=pl.CostEstimate(flops=flops, bytes_accessed=1 << 20, transcendentals=0),
        name=name,
    )


def place_of(places_ref, n):
    return lax.bitwise_and(lax.shift_right_logical(places_ref[0], 2 * n), 3)


def sketch_body(me_ref, places_ref, omega_ref, blocks_ref, out_ref):
    del me_ref
    out_ref[...] = jnp.zeros(out_ref.shape, F32)
    for n in range(BLOCKS):
        start = pl.multiple_of(place_of(places_ref, n) * ORDER, ORDER)
        place = pl.multiple_of(place_of(places_ref, BLOCKS + n) % 2 * ORDER, ORDER)
        out_ref[place_of(places_ref, BLOCKS + n) // 2, :, pl.ds(place, ORDER)] += jnp.dot(
            omega_ref[:, pl.ds(start, ORDER)], blocks_ref[n], preferred_element_type=F32
        )


def scale_of(mantissa, power):
    return mantissa * jnp.exp2(power - 14.0)


def unit_of(largest):
    largest = jnp.maximum(largest, TINY)
    power = jnp.ceil(jnp.log2(largest))
    return power, jnp.ceil(largest * jnp.exp2(14.0 - power))


def encode(tiles, power, mantissa):
    factor = 32000.0 / scale_of(mantissa, power)
    unit = jnp.where(iota((8, LANES), 1) == 0, power, mantissa)
    rows = jnp.concatenate([tile * factor for tile in tiles] + [unit], axis=0)
    return jnp.round(rows).astype(jnp.int32).astype(I16)


def decode(coded):
    rows = coded.astype(jnp.int32).astype(F32)
    unit = rows[8 * SHARE_TILES :]
    factor = scale_of(unit[:, 1:2], unit[:, 0:1]) / 32000.0
    return [rows[8 * q : 8 * q + 8] * factor for q in range(SHARE_TILES)]


def pair_body(me_ref, parts_ref, out_ref):
    half = lax.rem(me_ref[0], CORES)
    total = parts_ref[0, half] + parts_ref[1, half]
    power, mantissa = unit_of(jnp.max(jnp.abs(total), axis=1, keepdims=True))
    coded = jnp.round(total * (32000.0 / scale_of(mantissa, power))).astype(jnp.int32).astype(I16)
    unit = jnp.where(iota((WIDTH, LANES), 1) == 0, power, mantissa).astype(jnp.int32).astype(I16)
    for i in range(X_PARTS):
        out_ref[i, :, :HALF] = coded
        out_ref[i, :, HALF:] = unit


def scale_body(me_ref, parts_ref, theta_ref, out_ref):
    total = jnp.zeros(out_ref.shape, F32)
    for i in range(X_PARTS):
        unit = parts_ref[i, :, HALF:].astype(jnp.int32).astype(F32)
        coded = parts_ref[i, :, :HALF].astype(jnp.int32).astype(F32)
        total += coded * (scale_of(unit[:, 1:2], unit[:, 0:1]) / 32000.0)
    tile = theta_ref[lax.rem(me_ref[0], CORES)]
    theta = jnp.concatenate([tile[t : t + 1, :] for t in range(HALF_TILES)], axis=1)
    out_ref[...] = (theta * total).astype(BF16)


def forward_body(places_ref, scaled_ref, blocks_ref, out_ref, acc_ref):
    acc_ref[...] = jnp.zeros(acc_ref.shape, F32)
    for n in range(BLOCKS):
        place = pl.multiple_of(place_of(places_ref, BLOCKS + n) % 2 * ORDER, ORDER)
        left = scaled_ref[place_of(places_ref, BLOCKS + n) // 2, :, pl.ds(place, ORDER)]
        product = lax.dot_general(left, blocks_ref[n], NT, preferred_element_type=F32)
        for g in range(GROUPS):
            for q in range(ORDER // LANES):
                acc_ref[g * (LOCAL // ORDER) + place_of(places_ref, n), q] += product[
                    8 * g : 8 * g + 8, LANES * q : LANES * (q + 1)
                ]
    per_group = SHARES // GROUPS
    for g in range(GROUPS):
        part = acc_ref[per_group * g : per_group * (g + 1)]
        largest = jnp.max(jnp.max(jnp.max(jnp.abs(part), axis=0), axis=0), axis=1, keepdims=True)
        power, mantissa = unit_of(largest)
        for u in range(per_group):
            out_ref[per_group * g + u] = encode(
                [part[u, q] for q in range(SHARE_TILES)], power, mantissa
            )


def near_body(parts_ref, out_ref):
    sums = [decode(parts_ref[i]) for i in range(SHARES)]
    while len(sums) > 1:
        sums = [[a + b for a, b in zip(*pair)] for pair in zip(sums[::2], sums[1::2])]
    total = sums[0]
    largest = jnp.abs(total[0])
    for tile in total[1:]:
        largest = jnp.maximum(largest, jnp.abs(tile))
    power, mantissa = unit_of(jnp.max(largest, axis=1, keepdims=True))
    coded = encode(total, power, mantissa)
    for i in range(FAR_PARTS):
        out_ref[i] = coded


def far_body(parts_ref, out_ref):
    parts = [decode(parts_ref[i]) for i in range(FAR_PARTS)]
    total = [(a + b) + (c + d) for a, b, c, d in zip(*parts)]
    for i in range(SHARES):
        for q in range(SHARE_TILES):
            out_ref[i, q] = total[q]


def pack_square(square):
    packed = square[0:8]
    for g in range(1, GROUPS):
        packed += pltpu.roll(square[8 * g : 8 * g + 8], WIDTH * g, 1)
    return packed


def unpack_square(packed):
    lane = iota((8, LANES), 1)
    parts = [packed] + [pltpu.roll(packed, LANES - WIDTH * g, 1) for g in range(1, GROUPS)]
    return jnp.concatenate([jnp.where(lane < WIDTH, part, 0.0) for part in parts], axis=0)


def gram_body(tiles_ref, omega_ref, rhs_ref, y_ref, out_ref, all_ref):
    for i in range(SHARES):
        g, first = i // (SHARES // GROUPS), i % (SHARES // GROUPS) * SHARE_TILES
        for q in range(SHARE_TILES):
            at = LANES * (first + q)
            y_ref[8 * g : 8 * g + 8, at : at + LANES] = tiles_ref[i, q]
    omega = omega_ref[...].astype(F32)
    ysketch = y_ref[...] + regularize * omega
    y_ref[...] = ysketch
    all_ref[0:WIDTH, :] = ysketch
    all_ref[WIDTH : 2 * WIDTH, :] = omega
    all_ref[2 * WIDTH :, :] = jnp.where(
        iota((LANES - 2 * WIDTH, LOCAL), 0) == 0, rhs_ref[...], 0.0
    )
    products = lax.dot_general(
        all_ref[0 : 2 * WIDTH + 8, :], all_ref[...], NT, precision=HIGHEST, preferred_element_type=F32
    )
    lane = iota((WIDTH, LANES), 1)
    upper = products[0:WIDTH]
    cross = 0.5 * (products[WIDTH : 2 * WIDTH] + pltpu.roll(upper, LANES - WIDTH, 1))
    gram = pack_square(jnp.where(lane < WIDTH, upper + precond_shift * cross, 0.0))
    for i in range(ROW_PARTS):
        out_ref[i, 0] = gram
        out_ref[i, 1] = products[2 * WIDTH :]


def to_column(row, shift):
    lane = iota((WIDTH, LANES), 1)
    return jnp.sum(
        jnp.where(lane == iota((WIDTH, LANES), 0) + shift, row, 0.0), axis=1, keepdims=True
    )


def to_row(column, shift):
    lane = iota((WIDTH, LANES), 1)
    return jnp.sum(
        jnp.where(lane == iota((WIDTH, LANES), 0) + shift, column, 0.0), axis=0, keepdims=True
    )


def eliminate(work, panel):
    spot = iota((WIDTH, LANES), 0)
    for k in range(0, WIDTH, panel):
        rows = [work[k + i : k + i + 1, :] for i in range(panel)]
        columns = [jnp.broadcast_to(work[:, k + i : k + i + 1], work.shape) for i in range(panel)]
        square = [
            [jnp.broadcast_to(rows[i][:, k + j : k + j + 1], (1, LANES)) for j in range(panel)]
            for i in range(panel)
        ]
        update = jnp.zeros(work.shape, F32)
        for i in range(panel):
            reciprocal = 1.0 / square[i][i]
            for j in range(i + 1, panel):
                factor = square[i][j] * reciprocal
                rows[j] = rows[j] - factor * rows[i]
                columns[j] = columns[j] - factor * columns[i]
                for m in range(j, panel):
                    square[j][m] = square[j][m] - factor * square[i][m]
            update += columns[i] * (rows[i] * reciprocal)
        work = jnp.where(spot >= k + panel, work - update, work)
        for i in range(1, panel):
            work = jnp.where(spot == k + i, rows[i], work)
    return work


def solve_gram(inverse, diagonal, row):
    half = jnp.sum(inverse * pltpu.roll(row, WIDTH, 1), axis=1, keepdims=True) / diagonal
    return jnp.sum(inverse * half, axis=0, keepdims=True)


def factor_body(
    places_ref, parts_ref, y_ref, rhs_ref, blocks_ref, out_ref, keep_ref, direction_ref, low_ref, acc_ref
):
    total = parts_ref[0]
    for i in range(1, ROW_PARTS):
        total += parts_ref[i]
    lane = iota((WIDTH, LANES), 1)
    spot = iota((WIDTH, LANES), 0)
    work = eliminate(jnp.where(lane == spot + WIDTH, 1.0, unpack_square(total[0])), 8)
    diagonal = jnp.sum(jnp.where(lane == spot, work, 0.0), axis=1, keepdims=True)
    inverse = jnp.where((lane >= WIDTH) & (lane < 2 * WIDTH), work, 0.0)
    sketched_rhs = jnp.where(iota((1, LANES), 1) < WIDTH, total[1, 0:1], 0.0)
    coeffs = solve_gram(inverse, diagonal, sketched_rhs)

    ysketch = y_ref[...]
    rhs = rhs_ref[...]
    direction = (
        rhs - jnp.sum(ysketch * to_column(coeffs, WIDTH), axis=0, keepdims=True)
    ) / precond_shift
    direction_ref[...] = direction
    low_ref[...] = jnp.broadcast_to(direction, low_ref.shape).astype(BF16)

    acc_ref[...] = jnp.zeros(acc_ref.shape, F32)
    for n in range(BLOCKS):
        start = pl.multiple_of(place_of(places_ref, n) * ORDER, ORDER)
        product = jnp.dot(
            low_ref[:, pl.ds(start, ORDER)], blocks_ref[n], preferred_element_type=F32
        )
        acc_ref[place_of(places_ref, BLOCKS + n)] += product[0:8]
    row = iota((8, LANES), 0)
    per_block = ORDER // LANES
    for h in range(CORES):
        tile = jnp.zeros((8, LANES), F32)
        for t in range(HALF_TILES):
            j = h * (HALF_TILES // per_block) + t // per_block
            at = LANES * (t % per_block)
            tile = jnp.where(row == t, acc_ref[j, :, at : at + LANES], tile)
        for i in range(ROW_PARTS):
            out_ref[i, h] = tile

    sketched = to_row(jnp.sum(ysketch * direction, axis=1, keepdims=True), 3 * WIDTH)
    length = jnp.sum(direction * direction, axis=1, keepdims=True)
    along = jnp.sum(rhs * direction, axis=1, keepdims=True)
    line = iota((1, LANES), 1)
    sums = jnp.where(line == 2 * WIDTH + 1, length, sketched)
    sums = jnp.where(line == 2 * WIDTH + 2, along, sums)
    keep_ref[0:WIDTH, :] = inverse
    keep_ref[WIDTH : 2 * WIDTH, :] = jnp.broadcast_to(diagonal, (WIDTH, LANES))
    keep_ref[2 * WIDTH : 2 * WIDTH + 8, :] = jnp.broadcast_to(sketched_rhs, (8, LANES))
    keep_ref[2 * WIDTH + 8 :, :] = jnp.broadcast_to(sums, (8, LANES))


def image_body(
    places_ref,
    parts_ref,
    theta_ref,
    y_ref,
    direction_ref,
    keep_ref,
    blocks_ref,
    out_ref,
    sums_ref,
    scaled_ref,
    acc_ref,
):
    total = parts_ref[0]
    for i in range(1, ROW_PARTS):
        total += parts_ref[i]
    scaled = theta_ref[...] * total
    per_block = ORDER // LANES
    for j in range(LOCAL // ORDER):
        h, first = j // 2, j % 2 * per_block
        line = jnp.concatenate(
            [scaled[h, first + q : first + q + 1, :] for q in range(per_block)], axis=1
        )
        scaled_ref[j] = jnp.broadcast_to(line, (16, ORDER)).astype(BF16)
    acc_ref[...] = jnp.zeros(acc_ref.shape, F32)
    for n in range(BLOCKS):
        product = lax.dot_general(
            scaled_ref[place_of(places_ref, BLOCKS + n)], blocks_ref[n], NT, preferred_element_type=F32
        )
        acc_ref[place_of(places_ref, n)] += product[0:8]

    whole = jnp.concatenate([acc_ref[r, 0:1, :] for r in range(LOCAL // ORDER)], axis=1)
    sketched = to_row(jnp.sum(y_ref[...] * whole, axis=1, keepdims=True), WIDTH)
    curvature = jnp.sum(direction_ref[...] * whole, axis=1, keepdims=True)
    sums = jnp.where(iota((1, LANES), 1) == 2 * WIDTH, curvature, sketched)
    sums += keep_ref[2 * WIDTH + 8 : 2 * WIDTH + 9, :]
    sums_ref[...] = jnp.broadcast_to(sums, sums_ref.shape)
    row = iota((8, LANES), 0)
    for h in range(CORES):
        tile = jnp.zeros((8, LANES), F32)
        for t in range(HALF_TILES):
            r, at = (h * HALF_TILES + t) // per_block, LANES * (t % per_block)
            tile = jnp.where(row == t, acc_ref[r, :, at : at + LANES], tile)
        out_ref[h] = tile


def lines_body(
    me_ref, image_ref, parts_ref, y_ref, rhs_ref, direction_ref, out_ref, sums_ref, mine_ref
):
    shares = LANES // WIDTH
    column = lax.div(me_ref[0], CORES)
    start = pl.multiple_of(lax.div(column, shares) * LANES, LANES)
    turn = lax.rem(shares - lax.rem(column, shares), shares) * WIDTH
    mine_ref[0:WIDTH, :] = pltpu.roll(y_ref[:, pl.ds(start, LANES)], turn, 1)
    rhs = jnp.broadcast_to(rhs_ref[:, pl.ds(start, LANES)], (8, LANES))
    mine_ref[WIDTH : WIDTH + 8, :] = pltpu.roll(rhs, turn, 1)
    direction = jnp.broadcast_to(direction_ref[:, pl.ds(start, LANES)], (8, LANES))
    mine_ref[WIDTH + 8 :, :] = pltpu.roll(direction, turn, 1)
    sums = jnp.sum(parts_ref[...], axis=0, keepdims=True)
    sums_ref[...] = jnp.broadcast_to(sums, sums_ref.shape)
    lane = iota((8, LANES), 1)
    row = iota((8, LANES), 0)
    shares = LANES // WIDTH
    added = jnp.broadcast_to(
        jnp.where(iota((1, LANES), 1) <= 2 * WIDTH, sums, 0.0), (8, LANES)
    )
    for u in range(TILES // 2):
        pack = added
        for v in range(2):
            t = 2 * u + v
            line = image_ref[t // HALF_TILES, t % HALF_TILES : t % HALF_TILES + 1, :]
            for q in range(shares):
                turned = line if q == 0 else pltpu.roll(line, LANES - WIDTH * q, 1)
                pack = jnp.where((lane < WIDTH) & (row == shares * v + q), turned, pack)
        out_ref[8 * u : 8 * u + 8, :] = pack


def step_body(
    parts_ref, sums_ref, keep_ref, mine_ref, solution_ref, residual_ref, precond_ref
):
    total = parts_ref[0:8, :]
    for i in range(1, COL_PARTS // 8):
        total += parts_ref[8 * i : 8 * i + 8, :]
    total = jnp.sum(total, axis=0, keepdims=True)
    sums = sums_ref[0:1, :]
    lane = iota((1, LANES), 1)
    inverse = keep_ref[0:WIDTH, :]
    diagonal = keep_ref[WIDTH : 2 * WIDTH, 0:1]
    sketched_rhs = keep_ref[2 * WIDTH : 2 * WIDTH + 1, :]

    def pick(line, at):
        return jnp.sum(jnp.where(lane == at, line, 0.0), axis=1, keepdims=True)

    along = pick(sums, 2 * WIDTH + 2)
    curvature = pick(total, 2 * WIDTH) + regularize * pick(sums, 2 * WIDTH + 1)
    alpha = along / curvature

    ysketch = mine_ref[0:WIDTH, :]
    rhs = mine_ref[WIDTH : WIDTH + 1, :]
    direction = mine_ref[WIDTH + 8 : WIDTH + 9, :]
    image = total + regularize * direction
    residual = rhs - alpha * image
    sketched_image = pltpu.roll(total, LANES - WIDTH, 1) + regularize * pltpu.roll(sums, WIDTH, 1)
    sketched_image = jnp.where(lane < WIDTH, sketched_image, 0.0)
    res_coeffs = solve_gram(inverse, diagonal, sketched_rhs - alpha * sketched_image)
    precond_residual = (
        residual - jnp.sum(ysketch * to_column(res_coeffs, WIDTH), axis=0, keepdims=True)
    ) / precond_shift
    solution_ref[...] = (alpha * direction)[0, :WIDTH]
    residual_ref[...] = residual[0, :WIDTH]
    precond_ref[...] = precond_residual[0, :WIDTH]


def exchange(value, axis):
    return lax.all_to_all(value, axis, 0, 0, tiled=True)


def shards(blocks, block_rows, block_cols, sketch, theta, rhs):
    values = blocks[0, 0]
    omega = sketch.T
    rhs_line = rhs.reshape(1, LOCAL)
    theta_tiles = theta.reshape(CORES, HALF_TILES, LANES)
    places = jnp.concatenate([block_rows[0, 0], block_cols[0, 0]])
    places = jnp.sum(jnp.left_shift(places, 2 * jnp.arange(2 * BLOCKS, dtype=jnp.int32)))
    me = lax.axis_index("core") + CORES * lax.axis_index(("y", "far", "near"))
    me = me.astype(jnp.int32)
    places = (places + lax.shift_right_arithmetic(me, 30)).reshape(1)
    me = me.reshape(1)
    shape = jax.ShapeDtypeStruct
    work = 2 * BLOCKS * ORDER * ORDER

    with jax.named_scope("sketch_cols"):
        terms = call(
            sketch_body,
            [smem(), smem(), vmem(), vmem()],
            shape((CORES, WIDTH, HALF), F32),
            flops=work * WIDTH,
            name="sketch_cols",
        )(me, places, omega, values)
        parts = lax.all_gather(terms, "core")
        parts = call(
            pair_body, [smem(), vmem()], shape((X_PARTS, WIDTH, HALF + LANES), I16), name="pair"
        )(me, parts)
        parts = exchange(parts, "x")
    with jax.named_scope("scaled"):
        scaled = call(
            scale_body, [smem(), vmem(), vmem()], shape((WIDTH, HALF), BF16), name="scaled"
        )(me, parts, theta_tiles)
        scaled = lax.all_gather(scaled, "core")
    with jax.named_scope("ysketch"):
        terms = call(
            forward_body,
            [smem(), vmem(), vmem()],
            shape((SHARES, 8 * SHARE_TILES + 8, LANES), I16),
            scratch=[pltpu.VMEM((SHARES, SHARE_TILES, 8, LANES), F32)],
            flops=work * WIDTH,
            name="ysketch",
        )(places, scaled, values)
        parts = exchange(terms, ("y", "near"))
        parts = call(
            near_body,
            [vmem()],
            shape((FAR_PARTS, 8 * SHARE_TILES + 8, LANES), I16),
            name="ysketch_near",
        )(parts)
        parts = exchange(parts, "far")
        parts = call(
            far_body,
            [vmem()],
            shape((SHARES, SHARE_TILES, 8, LANES), F32),
            name="ysketch_far",
        )(parts)
        tiles = exchange(parts, ("y", "near"))
    with jax.named_scope("gram"):
        ysketch, terms = call(
            gram_body,
            [vmem(), vmem(), vmem()],
            (shape((WIDTH, LOCAL), F32), shape((ROW_PARTS, 2, 8, LANES), F32)),
            scratch=[pltpu.VMEM((LANES, LOCAL), F32)],
            name="gram",
        )(tiles, omega, rhs_line)
        parts = exchange(terms, ("x", "core"))
    with jax.named_scope("direction"):
        terms, keep, direction = call(
            factor_body,
            [smem(), vmem(), vmem(), vmem(), vmem()],
            (
                shape((ROW_PARTS, CORES, HALF_TILES, LANES), F32),
                shape((2 * WIDTH + 16, LANES), F32),
                shape((1, LOCAL), F32),
            ),
            scratch=[
                pltpu.VMEM((16, LOCAL), BF16),
                pltpu.VMEM((LOCAL // ORDER, 8, ORDER), F32),
            ],
            flops=work,
            name="direction",
        )(places, parts, ysketch, rhs_line, values)
        parts = exchange(terms, ("x", "core"))
    with jax.named_scope("image"):
        image, terms = call(
            image_body,
            [smem()] + [vmem()] * 6,
            (shape((CORES, HALF_TILES, LANES), F32), shape((ROW_PARTS, LANES), F32)),
            scratch=[
                pltpu.VMEM((LOCAL // ORDER, 16, ORDER), BF16),
                pltpu.VMEM((LOCAL // ORDER, 8, ORDER), F32),
            ],
            flops=work,
            name="image",
        )(places, parts, theta_tiles, ysketch, direction, keep, values)
        parts = exchange(terms, ("x", "core"))
        terms, sums, mine = call(
            lines_body,
            [smem()] + [vmem()] * 5,
            (
                shape((COL_PARTS, LANES), F32),
                shape((8, LANES), F32),
                shape((WIDTH + 16, LANES), F32),
            ),
            name="lines",
        )(me, image, parts, ysketch, rhs_line, direction)
        parts = exchange(terms, ("y", "far", "near"))
    with jax.named_scope("step"):
        share = shape((LOCAL // COL_PARTS,), F32)
        return call(
            step_body,
            [vmem()] * 4,
            (share, share, share),
            name="step",
        )(parts, sums, keep, mine)


def solution(mesh):
    row, col = ("x", "core"), ("y", "far", "near")
    fine = jax.sharding.Mesh(
        mesh.devices.reshape(X_PARTS, CORES, Y_PARTS, FAR_PARTS, NEAR_PARTS),
        ("x", "core", "y", "far", "near"),
    )
    in_specs = (
        P(row, col, None, None, None),
        P(row, col, None),
        P(row, col, None),
        P(row, None),
        P(col),
        P(row),
    )
    out_specs = (P(row + col), P(row + col), P(row + col))
    return jax.shard_map(shards, mesh=fine, in_specs=in_specs, out_specs=out_specs, check_vma=False)
```
